32 devices in a mesh: dp: 4 (over x, core), expert: 8 (over z, y).
Axes of the slice: x: 2, y: 2, z: 4, core: 2. Of those that a mesh axis runs over, the one named last changes fastest.
Arguments:
- tokens: bfloat16 [8192, 1024], P(('dp', 'expert')), may hold values from -6 to 6
- norm_gain: float32 [1024], replicated, may hold values from 0.5 to 1.5
- query_weight: bfloat16 [1024, 512], replicated, may hold values from -0.1875 to 0.1875
- key_weight: bfloat16 [1024, 512], replicated, may hold values from -0.1875 to 0.1875
- value_weight: bfloat16 [1024, 2560], replicated, may hold values from -0.1875 to 0.1875
- output_weight: bfloat16 [1024, 2560], replicated, may hold values from -3 to 3
- value_router: bfloat16 [1024, 20], replicated, may hold values from -0.125 to 0.125
- output_router: bfloat16 [1024, 20], replicated, may hold values from -0.125 to 0.125
- expert_router: bfloat16 [1024, 192], replicated, may hold values from -0.0625 to 0.0625
- expert_up: bfloat16 [192, 1024, 128], P('expert'), may hold values from -0.125 to 0.125
- expert_down: bfloat16 [192, 1024, 128], P('expert'), may hold values from -0.5 to 0.5
- lengths: int32 [32], P(('dp', 'expert')), may hold values from 64 to 256, as said below
- value_choice: int32 [8192, 4, 2], P(('dp', 'expert')), may hold values from 0 to 4, all different within a row
- output_choice: int32 [8192, 4, 2], P(('dp', 'expert')), may hold values from 0 to 4, all different within a row
- expert_choice: int32 [8192, 16], P(('dp', 'expert')), may hold values from 0 to 191, all different within a row; in each aligned block of 256 rows (0 to 255, 256 to 511, ...) at most 32 rows name the same one
- running_counts: int32 [192], P(('dp', 'expert')), may hold values from 0 to 63
- cotangent: bfloat16 [8192, 1024], P(('dp', 'expert')), may hold values from -6 to 6
Outputs:
- output: bfloat16 [8192, 1024], P(('dp', 'expert'))
- grad_tokens: bfloat16 [8192, 1024], P(('dp', 'expert'))
- grad_gain: float32 [1024], P(('dp', 'expert'))
- grad_query: float32 [1024, 512], P(('dp', 'expert'))
- grad_key: float32 [1024, 512], P(('dp', 'expert'))
- grad_value: float32 [1024, 2560], P(('dp', 'expert'))
- grad_output: float32 [1024, 2560], P(('dp', 'expert'))
- grad_value_router: float32 [1024, 20], P(('dp', 'expert'))
- grad_output_router: float32 [1024, 20], P(('dp', 'expert'))
- grad_expert_router: float32 [1024, 192], P(('dp', 'expert'))
- grad_expert_up: float32 [192, 1024, 128], P('expert', 'dp')
- grad_expert_down: float32 [192, 1024, 128], P('expert', 'dp')
- counts: int32 [192], P(('dp', 'expert'))
The draws below stay inside these ranges and needn't reach their ends.
Inputs may be any that keep to these rules, and one draw needn't show every extreme that they name: `lengths`: some sequence has length exactly 256. `value_choice`: A token names 2 different experts in each head. `output_choice`: A token names 2 different experts in each head. `expert_choice`: A token names 16 different experts; within the 256 rows of one device no expert is named more than 32 times, a bound that some block reaches there.
All inputs are finite; a program needn't handle non-finite values.
Results may differ from the reference program's by a relative error of at most 0.012.
The reference program's roundings to bfloat16 on the way count: a program that leaves them out, or rounds other values in their place, can miss the bound.
Values may be sent and summed in bfloat16 or wider, within the bound.
No kernel may reach another device: no remote copies, remote signals or barrier semaphores. Data moves between devices by JAX's collectives and lax.ppermute only.
A program may use at most 256 MiB of HBM per device.

```python
import math
import jax
import jax.numpy as jnp
import numpy as np
from jax import lax

D = 1024
HEADS = 4
HEAD = 128
AEXP = 5
ASEL = 2
FF_E = 128
TOPK = 16
TOK_DEV = 256
SEQS = 32
TOKENS = 8192
EXPERTS = 192
CAP = 32


def draw_lengths(key, part):
    key = jax.random.fold_in(key, 7)
    draw_key, pick_key = jax.random.split(key)
    drawn = jax.random.randint(draw_key, (SEQS,), TOK_DEV // 4, TOK_DEV + 1, dtype=jnp.int32)
    longest = jax.random.randint(pick_key, (), 0, SEQS, dtype=jnp.int32)
    return jnp.where(jnp.arange(SEQS, dtype=jnp.int32) == longest, TOK_DEV, drawn).astype(jnp.int32)


def with_ends(entries, rng, least, top_value):
    dims = entries.shape
    index_at = [jax.random.randint(jax.random.fold_in(rng, axis), (), 0, dims[axis]) for axis in range(len(dims))]
    entries = entries.at[tuple(index_at)].set(least)
    longest = dims.index(max(dims))
    index_at[longest] = (index_at[longest] + 1) % dims[longest]
    return entries.at[tuple(index_at)].set(top_value)


def block_scale(key, extent, cuts, low, largest):
    loudness = 1.0
    for dim, shards_of in cuts:
        heights = jax.random.uniform(jax.random.fold_in(jax.random.fold_in(key, 6), dim), (shards_of,), jnp.float32, low / len(cuts), largest / len(cuts))
        loudness = loudness * jnp.repeat(jnp.exp(heights), extent[dim] // shards_of).reshape((-1,) + (1,) * (len(extent) - 1 - dim))
    return loudness


def picks_of(key, rows, amount, top, lift):
    ranking = jax.random.permutation(jax.random.fold_in(key, 1), amount)
    favour = ranking
    for power in range(3):
        favour = favour * favour // amount
    favour = favour * lift // amount
    lots = jax.random.randint(jax.random.fold_in(key, 2), (rows, amount), 0, 4096) + favour
    sure = jax.random.permutation(jax.random.fold_in(key, 3), rows)[jnp.arange(amount) % rows]
    lots = jnp.where(jnp.arange(rows)[:, None] == sure[None, :], 1 << 14, lots)
    merit = lots * amount + jnp.arange(amount)
    return lax.top_k(merit.astype(jnp.int32), top)[1].astype(jnp.int32)


def shared_out(rng, own, number, rows, count, top, bound, skew):
    sequence = jax.random.permutation(rng, count)
    crowded, ordinary = load_shares(count, rows * top, bound, skew, True), load_shares(count, rows * top, bound, skew, False)
    places = jnp.arange(count)

    def named(sizes, turn):
        used = int((sizes > 0).sum())
        fixed = max(1, used // 4)
        passed = fixed + (places - fixed + turn * (used - fixed)) % max(1, count - fixed)
        return jnp.zeros((count,), jnp.int32).at[sequence[jnp.where(places < fixed, places, passed)]].set(jnp.asarray(sizes, jnp.int32))

    sizes = jnp.where(number % 4 == 0, named(crowded, number // 4), named(ordinary, number - number // 4 - 1))
    mixed = jax.random.permutation(jax.random.fold_in(own, 3), count)
    source_of, sink = mixed[0:count // 2 * 2:2], mixed[1:count // 2 * 2:2]
    slack = jnp.minimum(sizes[source_of] - 1, bound - sizes[sink]) // 2
    slack = jnp.where((source_of == sequence[0]) | (sink == sequence[0]) | (sizes[sink] == 0), 0, jnp.maximum(slack, 0))
    passed = jax.random.randint(jax.random.fold_in(own, 4), (count // 2,), 0, 1 << 20) % (slack + 1)
    sizes = sizes.at[source_of].add(-passed).at[sink].add(passed)
    items = jnp.searchsorted(jnp.cumsum(sizes), jnp.arange(rows * top), side="right").astype(jnp.int32)
    table = items.reshape(top, rows).T
    table = table[jax.random.permutation(jax.random.fold_in(own, 1), rows)]
    turn = jax.random.randint(jax.random.fold_in(own, 2), (rows, 1), 0, top)
    return jnp.take_along_axis(table, (jnp.arange(top)[None, :] + turn) % top, axis=1)


def load_shares(count, total, reach, lean, full):
    loads = [(1 << 20) // math.isqrt(grade ** lean) + 1 for grade in range(1, count + 1)]
    largest = reach if full else min(reach, max(-(-total // count), total * loads[0] // sum(loads)))
    least = 1 if total - largest >= count - 1 else 0
    holding, surplus = [largest] + [least] * (count - 1), total - largest - least * (count - 1)
    while surplus > 0:
        movable = [i for i in range(1, count) if holding[i] < largest] or [i for i in range(1, count) if holding[i] < reach]
        pool, budget = sum([loads[i] for i in movable]), surplus
        for i in movable:
            extra = min(reach - holding[i], max(1, budget * loads[i] // pool), surplus)
            holding[i] = holding[i] + extra
            surplus = surplus - extra
    return np.array(holding)


def gaussian(stream_key, dims, width, limit, cuts=(), kind=jnp.bfloat16):
    level = block_scale(stream_key, dims, cuts, -0.22, 0.18) if cuts else 1.0
    values = jax.random.normal(stream_key, dims, jnp.float32) * width * level
    return jnp.minimum(jnp.maximum(values, -limit), limit).astype(kind)


def setup_inputs(seed: int = 0) -> dict:
    key_of = jax.random.split(jax.random.key(seed), 18)
    tokens = gaussian(key_of[0], (TOKENS, D), 1.0, 6.0, ((0, 32),))
    norm_gain = jnp.clip(1.0 + 0.1 * jax.random.normal(key_of[1], (D,), jnp.float32), 0.5, 1.5)
    query_weight = gaussian(key_of[2], (D, HEADS * HEAD), D ** -0.5, 0.1875)
    key_weight = gaussian(key_of[3], (D, HEADS * HEAD), D ** -0.5, 0.1875)
    value_weight = gaussian(key_of[4], (D, HEADS * AEXP * HEAD), D ** -0.5, 0.1875)
    output_weight = gaussian(key_of[5], (D, HEADS * AEXP * HEAD), 4 ** -0.5, 3.0)
    value_router = gaussian(key_of[6], (D, HEADS * AEXP), (2 * D) ** -0.5, 0.125)
    output_router = gaussian(key_of[7], (D, HEADS * AEXP), (2 * D) ** -0.5, 0.125)
    expert_router = gaussian(key_of[8], (D, EXPERTS), (8 * D) ** -0.5, 0.0625)
    expert_up = gaussian(key_of[9], (EXPERTS, D, FF_E), (2 * D) ** -0.5, 0.125, ((0, 8),))
    expert_down = gaussian(key_of[10], (EXPERTS, D, FF_E), FF_E ** -0.5, 0.5, ((0, 8),))
    lengths = draw_lengths(jax.random.fold_in(key_of[17], 71), 0)
    value_choice = picks_of(key_of[12], TOKENS * HEADS, AEXP, ASEL, 0).reshape((TOKENS, HEADS, ASEL))
    output_choice = picks_of(key_of[13], TOKENS * HEADS, AEXP, ASEL, 0).reshape((TOKENS, HEADS, ASEL))
    expert_choice_keys = jax.random.split(jax.random.fold_in(key_of[14], 1), TOKENS // TOK_DEV)
    expert_choice_turns = jax.random.permutation(jax.random.fold_in(key_of[14], 3), TOKENS // TOK_DEV)
    expert_choice = jax.vmap(lambda own, number: shared_out(jax.random.fold_in(key_of[14], 2), own, number, TOK_DEV, EXPERTS, TOPK, CAP, 1))(expert_choice_keys, expert_choice_turns).reshape((TOKENS, TOPK))
    running_counts = with_ends(jax.random.randint(key_of[15], (EXPERTS,), 0, TOK_DEV // 4), jax.random.fold_in(key_of[15], 1), 0, (TOK_DEV // 4) - 1).astype(jnp.int32)
    cotangent = gaussian(key_of[16], (TOKENS, D), 1.0, 6.0, ((0, 32),))
    return dict(tokens=tokens, norm_gain=norm_gain, query_weight=query_weight, key_weight=key_weight, value_weight=value_weight, output_weight=output_weight, value_router=value_router, output_router=output_router, expert_router=expert_router, expert_up=expert_up, expert_down=expert_down, lengths=lengths, value_choice=value_choice, output_choice=output_choice, expert_choice=expert_choice, running_counts=running_counts, cotangent=cotangent)


@jax.custom_vjp
def low(v):
    return lax.optimization_barrier(v.astype(jnp.bfloat16)).astype(jnp.float32)

@jax.custom_vjp
def low_back(v):
    return v

def low_keep(v):
    return (low(v), None)

def low_pass(kept, grad):
    return (grad,)

def back_keep(v):
    return (v, None)

def back_low(kept, grad):
    return (low(grad),)
low.defvjp(low_keep, low_pass)
low_back.defvjp(back_keep, back_low)
HIGHEST = lax.Precision.HIGHEST

def rope_tables(seq_rows, head_width):
    half_width = head_width // 2
    ladder = jnp.arange(half_width, dtype=jnp.float32) * (2.0 / head_width)
    freqs = jnp.exp(-math.log(10000.0) * ladder)
    angles = jnp.arange(seq_rows, dtype=jnp.float32)[:, None] * freqs[None, :]
    return (jnp.cos(angles), jnp.sin(angles))

def rotate(vectors, cosine, sine):
    half_width = vectors.shape[-1] // 2
    former = vectors[..., :half_width]
    latter = vectors[..., half_width:]
    cos_rows = cosine[:, None, :]
    sin_rows = sine[:, None, :]
    return jnp.concatenate([former * cos_rows - latter * sin_rows, former * sin_rows + latter * cos_rows], axis=-1)

def slots(picks, experts_all, capacity):
    seq_rows, picks_per = picks.shape
    labels = jnp.arange(experts_all, dtype=jnp.int32)
    member = lax.optimization_barrier(jnp.sum((picks[:, :, None] == labels[None, None, :]).astype(jnp.int32), axis=1, dtype=jnp.int32))
    earlier = (jnp.cumsum(member, axis=0, dtype=jnp.int32) - member).astype(jnp.int32)
    places = jnp.take_along_axis(earlier, picks, axis=1)
    flat = (picks * capacity + places).astype(jnp.int32)
    filler = jnp.full((experts_all * capacity,), seq_rows * picks_per, jnp.int32)
    owner = filler.at[flat.reshape(-1)].set(jnp.arange(seq_rows * picks_per, dtype=jnp.int32))
    return (member, flat, owner)

def layer(inputs, weights, seq_length, value_pick, output_pick, expert_pick, flat, owner):
    norm_gain, query_weight, key_weight, value_weight, output_weight, value_router, output_router, expert_router, expert_up, expert_down = weights
    seq_rows = inputs.shape[0]
    row_mean = lax.optimization_barrier(jnp.mean(inputs, axis=1, keepdims=True))
    centered = inputs - row_mean
    variance = lax.optimization_barrier(jnp.mean(centered * centered, axis=1, keepdims=True))
    normed = low(centered * lax.rsqrt(variance + 1e-05) * norm_gain)
    query_pre = low_back(jnp.dot(normed, query_weight, precision=HIGHEST)).reshape(seq_rows, HEADS, HEAD)
    key_pre = low_back(jnp.dot(normed, key_weight, precision=HIGHEST)).reshape(seq_rows, HEADS, HEAD)
    cosine, sine = rope_tables(seq_rows, HEAD)
    query = low(rotate(query_pre, cosine, sine))
    keys = low(rotate(key_pre, cosine, sine))
    values_all = low_back(jnp.dot(inputs, value_weight, precision=HIGHEST)).reshape(seq_rows, HEADS, AEXP, HEAD)
    value_logit = low_back(jnp.dot(inputs, value_router, precision=HIGHEST)).reshape(seq_rows, HEADS, AEXP)
    output_logit = low_back(jnp.dot(inputs, output_router, precision=HIGHEST)).reshape(seq_rows, HEADS, AEXP)
    labels = jnp.arange(AEXP, dtype=jnp.int32)
    value_mask = lax.optimization_barrier(jnp.sum((value_pick[..., None] == labels).astype(jnp.float32), axis=2))
    output_mask = lax.optimization_barrier(jnp.sum((output_pick[..., None] == labels).astype(jnp.float32), axis=2))
    value_gate = jax.nn.sigmoid(value_logit) * value_mask
    output_gate = jax.nn.sigmoid(output_logit) * output_mask
    mixed = low(jnp.einsum('the,thew->thw', value_gate, values_all, precision=HIGHEST))
    position = jnp.arange(seq_rows, dtype=jnp.int32)
    allowed = (position[None, :] <= position[:, None]) & (position[None, :] < seq_length)
    scores = low_back(jnp.einsum('qhw,khw->hqk', query, keys, precision=HIGHEST) * (1.0 / math.sqrt(HEAD)))
    scores = jnp.where(allowed[None], scores, -1e+30)
    probs = low(jax.nn.softmax(scores, axis=-1))
    attended = low_back(jnp.einsum('hqk,khw->qhw', probs, mixed, precision=HIGHEST))
    expanded = low(output_gate[..., None] * attended[:, :, None, :]).reshape(seq_rows, HEADS * AEXP * HEAD)
    branch = low_back(jnp.dot(expanded, output_weight.T, precision=HIGHEST))
    hidden = inputs + branch
    hidden_low = low(hidden)
    router_logit = low_back(jnp.dot(hidden_low, expert_router, precision=HIGHEST))
    valid_rows = (position < seq_length).astype(jnp.float32)
    chosen = jnp.take_along_axis(jax.nn.sigmoid(router_logit), expert_pick, axis=1) * valid_rows[:, None]
    padded = jnp.concatenate([hidden_low, jnp.zeros((1, D), jnp.float32)], axis=0)
    rows = low_back(padded[owner // TOPK]).reshape(EXPERTS, CAP, D)
    pre = low_back(jnp.einsum('ecd,edf->ecf', rows, expert_up, precision=HIGHEST))
    act = low(jax.nn.gelu(pre))
    expert_rows = low(low_back(jnp.einsum('ecf,edf->ecd', act, expert_down, precision=HIGHEST)))
    back = expert_rows.reshape(EXPERTS * CAP, D)[flat]
    moe = jnp.einsum('tk,tkd->td', chosen, back, precision=HIGHEST)
    return hidden + moe

def reference(tokens, norm_gain, query_weight, key_weight, value_weight, output_weight, value_router, output_router, expert_router, expert_up, expert_down, lengths, value_choice, output_choice, expert_choice, running_counts, cotangent):
    params = tuple((p.astype(jnp.float32) for p in (norm_gain, query_weight, key_weight, value_weight, output_weight, value_router, output_router, expert_router, expert_up, expert_down)))
    seq_tokens = tokens.astype(jnp.float32).reshape(SEQS, TOK_DEV, D)
    seq_cot = cotangent.astype(jnp.float32).reshape(SEQS, TOK_DEV, D)
    seq_value = value_choice.astype(jnp.int32).reshape(SEQS, TOK_DEV, HEADS, ASEL)
    seq_output = output_choice.astype(jnp.int32).reshape(SEQS, TOK_DEV, HEADS, ASEL)
    seq_expert = expert_choice.astype(jnp.int32).reshape(SEQS, TOK_DEV, TOPK)

    def visit(carry, item):
        grads_total, counts_total = carry
        seq_input, seq_grad, seq_length, value_pick, output_pick, expert_pick = item
        member, flat, owner = slots(expert_pick, EXPERTS, CAP)

        def forward(seq_in, *weights):
            return layer(seq_in, weights, seq_length, value_pick, output_pick, expert_pick, flat, owner)
        result, pull = jax.vjp(forward, seq_input, *params)
        grads = pull(seq_grad)
        valid_int = (jnp.arange(TOK_DEV, dtype=jnp.int32) < seq_length).astype(jnp.int32)
        counts_total = (counts_total + lax.optimization_barrier(jnp.sum(member * valid_int[:, None], axis=0, dtype=jnp.int32))).astype(jnp.int32)
        grads_total = jax.tree.map(lambda a, b: (a + b).astype(a.dtype), grads_total, tuple(grads[1:]))
        return ((grads_total, counts_total), (result.astype(jnp.bfloat16), grads[0].astype(jnp.bfloat16)))
    start = (tuple((jnp.zeros(p.shape, p.dtype) for p in params)), jnp.zeros((EXPERTS,), jnp.int32))
    (grads_total, counts_total), (outputs, grad_inputs) = lax.scan(visit, start, (seq_tokens, seq_cot, lengths.astype(jnp.int32), seq_value, seq_output, seq_expert))
    return (outputs.reshape(TOKENS, D), grad_inputs.reshape(TOKENS, D), grads_total[0], grads_total[1], grads_total[2], grads_total[3], grads_total[4], grads_total[5], grads_total[6], grads_total[7], grads_total[8], grads_total[9], (running_counts.astype(jnp.int32) + counts_total).astype(jnp.int32))
```

```python
import functools
import math

import jax
import jax.numpy as jnp
from jax import lax
from jax.experimental import pallas as pl
from jax.experimental.pallas import tpu as pltpu
from jax.sharding import PartitionSpec as P

HEADS = 4
HEAD = 128
AEXP = 5
BF = jnp.bfloat16
F32 = jnp.float32
VMEM_LIMIT = 60 * 1024 * 1024
GELU_C = math.sqrt(2.0 / math.pi)
GELU_K = 0.044715


def rope_tables(seq_rows, head_width):
    half_width = head_width // 2
    ladder = jnp.arange(half_width, dtype=jnp.float32) * (2.0 / head_width)
    freqs = jnp.exp(-math.log(10000.0) * ladder)
    angles = jnp.arange(seq_rows, dtype=jnp.float32)[:, None] * freqs[None, :]
    return (jnp.cos(angles), jnp.sin(angles))


def rotate(vectors, cosine, sine):
    half_width = vectors.shape[-1] // 2
    former = vectors[..., :half_width]
    latter = vectors[..., half_width:]
    cos_rows = cosine[:, None, :]
    sin_rows = sine[:, None, :]
    return jnp.concatenate(
        [former * cos_rows - latter * sin_rows, former * sin_rows + latter * cos_rows], axis=-1
    )


def unrotate(grads, cosine, sine):
    half_width = grads.shape[-1] // 2
    former = grads[..., :half_width]
    latter = grads[..., half_width:]
    cos_rows = cosine[:, None, :]
    sin_rows = sine[:, None, :]
    return jnp.concatenate(
        [former * cos_rows + latter * sin_rows, latter * cos_rows - former * sin_rows], axis=-1
    )


def contract_rows(left, right):
    return lax.dot_general(
        left, right, (((0,), (0,)), ((), ())), preferred_element_type=jnp.float32
    )


def contract_cols(left, right):
    return lax.dot_general(
        left, right, (((1,), (1,)), ((), ())), preferred_element_type=jnp.float32
    )


class Grid:
    def __init__(self, size):
        self.hi = 4
        self.lo = size // 4
        self.size = size

    def hi_shift(self, x):
        pairs = [
            (i, ((i // self.lo + 1) % self.hi) * self.lo + i % self.lo) for i in range(self.size)
        ]
        return lax.ppermute(x, "expert", pairs)

    def lo_shift(self, x):
        pairs = [
            (i, (i // self.lo) * self.lo + (i % self.lo + 1) % self.lo) for i in range(self.size)
        ]
        return lax.ppermute(x, "expert", pairs)

    def sources(self):
        me = lax.axis_index("expert")
        h, l = me // self.lo, me % self.lo
        return [
            ((h + self.hi - dh) % self.hi) * self.lo + (l + self.lo - dl) % self.lo
            for dh in range(self.hi)
            for dl in range(self.lo)
        ]

    def all_rows(self, block):
        rows = {(0, 0): block}
        for step in range(self.hi + self.lo - 2):
            fresh = {}
            for dh in range(self.hi):
                for dl in range(self.lo):
                    if dh + dl == step + 1:
                        if dl > 0:
                            fresh[(dh, dl)] = self.lo_shift(rows[(dh, dl - 1)])
                        else:
                            fresh[(dh, dl)] = self.hi_shift(rows[(dh - 1, dl)])
            keys = list(fresh)
            rows.update(zip(keys, lax.optimization_barrier(tuple(fresh[k] for k in keys))))
        return [rows[(dh, dl)] for dh in range(self.hi) for dl in range(self.lo)]

    def sum_rows(self, parts):
        def part(a, b):
            return parts[((self.hi - a) % self.hi) * self.lo + (self.lo - b) % self.lo]

        sums = []
        for a in range(self.hi - 1, -1, -1):
            acc = part(a, self.lo - 1)
            for b in range(self.lo - 2, -1, -1):
                acc = add(part(a, b), self.lo_shift(acc))
            sums.append(acc)
        acc = sums[0]
        for s in range(1, self.hi):
            acc = add(sums[s], self.hi_shift(acc))
        return acc


def add(a, b):
    return (a.astype(F32) + b.astype(F32)).astype(BF)


class Tree:
    def __init__(self, dp, grid):
        self.grid = grid
        self.dp = dp
        self.xs = dp // 2

    def coords(self):
        dp, ex = lax.axis_index("dp"), lax.axis_index("expert")
        return jnp.stack([dp % 2, dp // 2, ex % self.grid.lo, ex // self.grid.lo])

    def core_shift(self, x):
        return lax.ppermute(x, "dp", [(i, i ^ 1) for i in range(self.dp)])

    def x_shift(self, x):
        pairs = [(i, (i // 2 + 1) % self.xs * 2 + i % 2) for i in range(self.dp)]
        return lax.ppermute(x, "dp", pairs)

    def ring(self, parts, shift):
        acc = parts[-1]
        for b in range(len(parts) - 2, -1, -1):
            acc = add(parts[b], shift(acc))
        return acc

    def sum_rows(self, near, far):
        got = self.core_shift(far)
        lo, hi = self.grid.lo, self.grid.hi
        acc = self.ring([add(near[i], got[i]) for i in range(self.xs)], self.x_shift)
        acc = self.ring([acc[i] for i in range(lo)], self.grid.lo_shift)
        acc, last = self.ring_but_last([acc[i] for i in range(hi)], self.grid.hi_shift)
        return acc.astype(F32) + last.astype(F32)

    def ring_but_last(self, parts, shift):
        acc = parts[-1]
        for b in range(len(parts) - 2, 0, -1):
            acc = add(parts[b], shift(acc))
        return shift(acc), parts[0]


def gather_kernel(count, cap, *refs):
    rows, slots, out = refs[:count], refs[count : 2 * count], refs[2 * count]
    experts = out.shape[0]
    seq_rows = slots[0].shape[1]
    step = 8
    for i in range(count):
        for e0 in range(0, experts, step):
            idx = slots[i][e0 : e0 + step, :]
            place = lax.broadcasted_iota(jnp.int32, (step, cap, seq_rows), 1).astype(F32)
            pick = (idx[:, None, :] == place).astype(F32).astype(BF).reshape(step * cap, seq_rows)
            got = jnp.dot(pick, rows[i][:seq_rows, :], preferred_element_type=F32)
            out[e0 : e0 + step, i * cap : (i + 1) * cap, :] = got.astype(BF).reshape(
                step, cap, got.shape[1]
            )


def gather_call(rows, slots, cap):
    count = len(rows)
    experts = slots[0].shape[0]
    width = rows[0].shape[1]
    flops = 2 * count * experts * cap * slots[0].shape[1] * width
    return pl.pallas_call(
        functools.partial(gather_kernel, count, cap),
        out_shape=jax.ShapeDtypeStruct((experts, count * cap, width), BF),
        compiler_params=pltpu.CompilerParams(vmem_limit_bytes=40 * 1024 * 1024),
        cost_estimate=pl.CostEstimate(
            flops=flops, bytes_accessed=2 * experts * count * cap * width, transcendentals=0
        ),
        name="gather_rows",
    )(*rows, *slots)


def expert_kernel(groups, per, cap, at_ref, *refs):
    n = groups // per
    xs_in, gs_in = refs[:n], refs[n : 2 * n]
    up, down, router, slot = refs[2 * n : 2 * n + 4]
    outs = refs[2 * n + 4 :]
    moe = outs[:groups]
    dhid = outs[groups : 2 * groups]
    near, far, grt = outs[2 * groups : 2 * groups + 3]
    xs, gs, w, d2, rw, dr, gacc = outs[2 * groups + 3 :]
    e = pl.program_id(0)
    ff = up.shape[2]

    @pl.when(e == 0)
    def _():
        w[:, ff:] = router[...]
        grt[...] = jnp.zeros_like(grt)

    for i in range(n):
        xs[i * per * cap : (i + 1) * per * cap, :] = xs_in[i][0]
        gs[i * per * cap : (i + 1) * per * cap, :] = gs_in[i][0]
    w[:, :ff] = up[0]
    both = jnp.dot(xs[...], w[...], preferred_element_type=F32)
    pre = both[:, :ff]
    sel = lax.broadcasted_iota(jnp.int32, pre.shape, 1) == e
    chosen = jnp.sum(jnp.where(sel, jax.nn.sigmoid(both[:, ff:]), 0.0), axis=1, keepdims=True)
    square = pre * pre
    t = jnp.tanh(GELU_C * (pre + GELU_K * (square * pre)))
    half = 0.5 * (1.0 + t)
    act = (half * pre).astype(BF)
    slope = half + 0.5 * pre * (1.0 - t * t) * (GELU_C * (1.0 + 3.0 * GELU_K * square))
    u = jnp.dot(gs[...], down[0], preferred_element_type=F32)
    act32 = act.astype(F32)
    dchosen = jnp.sum(u * act32, axis=1, keepdims=True)
    drl = dchosen * chosen * (1.0 - chosen)
    a2 = (chosen * act32).astype(BF)
    d2[:, :ff] = (chosen * u * slope).astype(BF)
    d2[:, ff:] = jnp.where(sel, drl, 0.0).astype(BF)
    got = lax.dot_general(
        a2, down[0], (((1,), (1,)), ((), ())), preferred_element_type=F32
    ).astype(BF)
    dgot = lax.dot_general(
        d2[...], w[...], (((1,), (1,)), ((), ())), preferred_element_type=F32
    ).astype(BF)
    at = pl.multiple_of(e * cap, cap)
    for s in range(groups):
        rw[s, pl.ds(at, cap), :] = got[s * cap : (s + 1) * cap]
        dr[s, pl.ds(at, cap), :] = dgot[s * cap : (s + 1) * cap]
    gu = lax.dot_general(d2[...], xs[...], (((0,), (0,)), ((), ())), preferred_element_type=F32)
    gacc[0] = gu[:ff]
    grt[...] += gu[ff : ff + grt.shape[0]]
    gacc[1] = lax.dot_general(a2, gs[...], (((0,), (0,)), ((), ())), preferred_element_type=F32)
    x_size, _, _, _, lanes = near.shape
    for xr in range(x_size):
        base = lax.rem(at_ref[1] + xr, x_size) * 2
        for cr, out in enumerate((near, far)):
            cut = pl.multiple_of((base + lax.rem(at_ref[0] + cr, 2)) * lanes, lanes)
            for i in range(2):
                out[xr, 0, i] = gacc[i, :, pl.ds(cut, lanes)].astype(BF)

    @pl.when(e == pl.num_programs(0) - 1)
    def _():
        experts = slot.shape[2]
        total = experts * cap
        rowi = lax.broadcasted_iota(jnp.int32, (experts, total), 0)
        coli = lax.broadcasted_iota(jnp.int32, (experts, total), 1)
        spread = (coli // cap == rowi).astype(F32).astype(BF)
        for s in range(groups):
            wide = jnp.dot(slot[s], spread, preferred_element_type=F32)
            lane = lax.broadcasted_iota(jnp.int32, wide.shape, 1) % cap
            put = (wide == lane.astype(F32)).astype(F32).astype(BF)
            dhid[s][...] = jnp.dot(put, dr[s], preferred_element_type=F32).astype(BF)
            moe[s][...] = jnp.dot(put, rw[s], preferred_element_type=F32).astype(BF)


def expert_call(coords, x_size, xs, gs, up, down, router, slot, cap):
    n = len(xs)
    experts, width, ff = up.shape
    groups, seq_rows, _ = slot.shape
    per = groups // n
    rows = groups * cap
    pad = -(-experts // 8) * 8
    lanes = width // (2 * x_size)
    row_spec = pl.BlockSpec((1, per * cap, width), lambda e, _: (e, 0, 0))
    w_spec = pl.BlockSpec((1, width, ff), lambda e, _: (e, 0, 0))
    whole = lambda *shape: pl.BlockSpec(shape, lambda e, _: (0,) * len(shape))
    g_spec = pl.BlockSpec((x_size, 1, 2, ff, lanes), lambda e, _: (0, e, 0, 0, 0))
    one = jax.ShapeDtypeStruct((seq_rows, width), BF)
    flops = experts * rows * width * ff * 2 * 8 + 4 * groups * seq_rows * experts * cap * width
    outs = pl.pallas_call(
        functools.partial(expert_kernel, groups, per, cap),
        grid_spec=pltpu.PrefetchScalarGridSpec(
            num_scalar_prefetch=1,
            grid=(experts,),
            in_specs=[row_spec] * (2 * n)
            + [w_spec, w_spec, whole(width, ff), whole(groups, seq_rows, experts)],
            out_specs=[whole(seq_rows, width)] * (2 * groups) + [g_spec, g_spec, whole(pad, width)],
            scratch_shapes=[
                pltpu.VMEM((rows, width), BF),
                pltpu.VMEM((rows, width), BF),
                pltpu.VMEM((width, 2 * ff), BF),
                pltpu.VMEM((rows, 2 * ff), BF),
                pltpu.VMEM((groups, experts * cap, width), BF),
                pltpu.VMEM((groups, experts * cap, width), BF),
                pltpu.VMEM((2, ff, width), F32),
            ],
        ),
        out_shape=[one] * (2 * groups)
        + [jax.ShapeDtypeStruct((x_size, experts, 2, ff, lanes), BF)] * 2
        + [jax.ShapeDtypeStruct((pad, width), F32)],
        compiler_params=pltpu.CompilerParams(vmem_limit_bytes=VMEM_LIMIT),
        cost_estimate=pl.CostEstimate(
            flops=flops, bytes_accessed=experts * rows * width * 8, transcendentals=0
        ),
        name="experts",
    )(coords, *xs, *gs, up, down, router, slot)
    return outs[:groups], outs[groups : 2 * groups], outs[-3], outs[-2], outs[-1]


def spread_kernel(sizes, rows, at_ref, *refs):
    left, right = refs[0], refs[1]
    extra = refs[2] if len(refs) == 7 else None
    near, far, turned, res = refs[-4:]
    x_size, lo, hi = sizes

    @pl.when(pl.program_id(0) == 0)
    def _():
        turned[...] = jnp.transpose(left[...])

    got = jnp.dot(turned[...], right[...], preferred_element_type=F32)
    res[...] = got if extra is None else got + extra[...].astype(F32)
    for cr, out in enumerate((near, far)):
        core = lax.rem(at_ref[0] + cr, 2)
        for xr in range(x_size):
            x = lax.rem(at_ref[1] + xr, x_size)
            for lr in range(lo):
                l = lax.rem(at_ref[2] + lr, lo)
                for hr in range(hi):
                    h = lax.rem(at_ref[3] + hr, hi)
                    start = (((x * 2 + core) * hi + h) * lo + l) * rows
                    out[xr, lr, hr] = res[pl.ds(pl.multiple_of(start, rows), rows), :].astype(BF)


def spread_call(coords, tree, left, right, tile, extra=None):
    seq_rows, width = left.shape
    cols = right.shape[1]
    sizes = (tree.xs, tree.grid.lo, tree.grid.hi)
    rows = width // (tree.dp * tree.grid.size)
    o_spec = pl.BlockSpec((*sizes, rows, tile), lambda j, _: (0, 0, 0, 0, j))
    in_specs = [
        pl.BlockSpec((seq_rows, width), lambda j, _: (0, 0)),
        pl.BlockSpec((seq_rows, tile), lambda j, _: (0, j)),
    ]
    args = [left, right]
    if extra is not None:
        in_specs.append(pl.BlockSpec((width, tile), lambda j, _: (0, j)))
        args.append(extra)
    return pl.pallas_call(
        functools.partial(spread_kernel, sizes, rows),
        grid_spec=pltpu.PrefetchScalarGridSpec(
            num_scalar_prefetch=1,
            grid=(cols // tile,),
            in_specs=in_specs,
            out_specs=[o_spec, o_spec],
            scratch_shapes=[pltpu.VMEM((width, seq_rows), BF), pltpu.VMEM((width, tile), F32)],
        ),
        out_shape=[jax.ShapeDtypeStruct((*sizes, rows, cols), BF)] * 2,
        compiler_params=pltpu.CompilerParams(vmem_limit_bytes=40 * 1024 * 1024),
        cost_estimate=pl.CostEstimate(
            flops=2 * seq_rows * width * cols, bytes_accessed=2 * width * cols, transcendentals=0
        ),
        name="weight_grad",
    )(coords, *args)


def shards(
    tokens,
    norm_gain,
    query_weight,
    key_weight,
    value_weight,
    output_weight,
    value_router,
    output_router,
    expert_router,
    expert_up,
    expert_down,
    lengths,
    value_choice,
    output_choice,
    expert_choice,
    running_counts,
    cotangent,
):
    seq_rows, model_width = tokens.shape
    groups = lax.axis_size("expert")
    grid = Grid(groups)
    me = lax.axis_index("expert")
    local_experts, _, ff = expert_up.shape
    experts_all = local_experts * groups
    picks_per = expert_choice.shape[1]
    cap = 3 * seq_rows * picks_per // (2 * experts_all)
    score_scale = 1.0 / math.sqrt(HEAD)
    position = jnp.arange(seq_rows, dtype=jnp.int32)
    seq_length = lengths[0]

    tree = Tree(lax.axis_size("dp"), grid)
    coords = tree.coords()
    code = jnp.where((position < seq_length)[:, None], expert_choice + 1, 0)
    digits = jnp.concatenate([code // 16, code % 16], axis=1).astype(BF)
    digits = digits.reshape(-1, model_width)
    meta_rows = digits.shape[0]
    meta = jnp.pad(digits, ((0, -meta_rows % 16), (0, 0)))
    grads_all = grid.all_rows(jnp.concatenate([cotangent, meta], axis=0))
    codes = jnp.stack([g[seq_rows : seq_rows + meta_rows] for g in grads_all])
    codes = codes.reshape(groups, seq_rows, 2, picks_per).astype(F32)
    picks = (codes[:, :, 0] * 16.0 + codes[:, :, 1]).astype(jnp.int32) - 1
    mine = me * local_experts + jnp.arange(local_experts, dtype=jnp.int32)
    member = jnp.any(picks[:, :, None, :] == mine[None, None, :, None], axis=3)
    below = (position[:, None] > position[None, :]).astype(BF)
    earlier = jnp.einsum("tu,sue->ste", below, member.astype(BF), preferred_element_type=F32)
    slot = jnp.where(member, earlier, -1.0)
    slot_low = slot.astype(BF)
    slot_t = jnp.swapaxes(slot, 1, 2)
    slots = [slot_t[s] for s in range(groups)]
    gs = [
        gather_call(grads_all[s : s + 2], slots[s : s + 2], cap) for s in range(0, groups, 2)
    ]

    inputs = tokens.astype(jnp.float32)
    row_mean = jnp.mean(inputs, axis=1, keepdims=True)
    centered = inputs - row_mean
    inverse_std = lax.rsqrt(jnp.mean(centered * centered, axis=1, keepdims=True) + 1e-05)
    scaled = centered * inverse_std
    normed_low = (scaled * norm_gain).astype(jnp.bfloat16)
    cosine, sine = rope_tables(seq_rows, HEAD)
    query_pre = jnp.dot(normed_low, query_weight, preferred_element_type=jnp.float32).reshape(
        seq_rows, HEADS, HEAD
    )
    key_pre = jnp.dot(normed_low, key_weight, preferred_element_type=jnp.float32).reshape(
        seq_rows, HEADS, HEAD
    )
    query_rot = rotate(query_pre, cosine, sine).astype(jnp.bfloat16)
    key_rot = rotate(key_pre, cosine, sine).astype(jnp.bfloat16)
    values_all = jnp.dot(tokens, value_weight, preferred_element_type=jnp.float32).reshape(
        seq_rows, HEADS, AEXP, HEAD
    )
    labels = jnp.arange(AEXP, dtype=jnp.int32)
    value_mask = jnp.sum((value_choice[..., None] == labels).astype(jnp.float32), axis=2)
    output_mask = jnp.sum((output_choice[..., None] == labels).astype(jnp.float32), axis=2)
    value_sig = jax.nn.sigmoid(
        jnp.dot(tokens, value_router, preferred_element_type=jnp.float32).reshape(
            seq_rows, HEADS, AEXP
        )
    )
    output_sig = jax.nn.sigmoid(
        jnp.dot(tokens, output_router, preferred_element_type=jnp.float32).reshape(
            seq_rows, HEADS, AEXP
        )
    )
    value_gate = value_sig * value_mask
    output_gate = output_sig * output_mask
    mixed = jnp.sum(value_gate[..., None] * values_all, axis=2).astype(jnp.bfloat16)

    allowed = (position[None, :] <= position[:, None]) & (position[None, :] < seq_length)
    scores = (
        jnp.einsum("qhw,khw->hqk", query_rot, key_rot, preferred_element_type=jnp.float32)
        * score_scale
    )
    scores = jnp.where(allowed[None], scores, -1e30)
    top = jnp.max(scores, axis=2, keepdims=True)
    expo = jnp.exp(scores - top)
    probs = expo / jnp.sum(expo, axis=2, keepdims=True)
    probs_low = probs.astype(jnp.bfloat16)
    attended = jnp.einsum("hqk,khw->qhw", probs_low, mixed, preferred_element_type=jnp.float32)
    expanded = (
        (output_gate[..., None] * attended[:, :, None, :])
        .astype(jnp.bfloat16)
        .reshape(seq_rows, HEADS * AEXP * HEAD)
    )
    hidden = inputs + contract_cols(expanded, output_weight)
    hidden_low = hidden.astype(jnp.bfloat16)

    hidden_all = grid.all_rows(hidden_low)
    xs = [
        gather_call(hidden_all[s : s + 2], slots[s : s + 2], cap) for s in range(0, groups, 2)
    ]
    router_mine = lax.dynamic_slice_in_dim(expert_router, me * local_experts, local_experts, 1)
    router_pad = jnp.pad(router_mine, ((0, 0), (0, ff - local_experts)))
    moe_parts, dhid_parts, near, far, grad_router_t = expert_call(
        coords, tree.xs, xs, gs, expert_up, expert_down, router_pad, slot_low, cap
    )
    dhidden = cotangent.astype(F32) + grid.sum_rows(dhid_parts).astype(F32)
    output = (hidden + grid.sum_rows(moe_parts).astype(F32)).astype(BF)
    got = tree.core_shift(far)
    acc, last = tree.ring_but_last(
        [add(near[i], got[i]) for i in range(tree.xs)], tree.x_shift
    )
    expert_grads = jnp.swapaxes(acc.astype(F32) + last.astype(F32), 2, 3)

    devices = tree.dp * groups
    rows_each = model_width // devices
    labels_all = jnp.arange(experts_all, dtype=jnp.int32)
    local_counts = jnp.sum(
        (code[:, :, None] == labels_all + 1).astype(jnp.int32), axis=(0, 1), dtype=jnp.int32
    )
    bits = (local_counts[:, None] >> jnp.arange(6, dtype=jnp.int32)) & 1
    bits = bits.reshape(devices, experts_all // devices, 6)
    bits = jnp.pad(bits, ((0, 0), (0, rows_each - experts_all // devices), (0, 0)))
    bits = bits.reshape(model_width, 6).astype(BF)
    routers = 2 * HEADS * AEXP
    small = -(-(routers + experts_all + 6) // 256) * 256
    extra = jnp.pad(bits, ((0, 0), (routers + experts_all, small - routers - experts_all - 6)))
    extra = lax.dynamic_update_slice_in_dim(
        extra,
        jnp.transpose(grad_router_t)[:, :local_experts].astype(BF),
        routers + me * local_experts,
        1,
    )

    dbranch_low = dhidden.astype(jnp.bfloat16)
    sum_output = tree.sum_rows(*spread_call(coords, tree, dbranch_low, expanded, 512))
    dexpanded = jnp.dot(dbranch_low, output_weight, preferred_element_type=jnp.float32).reshape(
        seq_rows, HEADS, AEXP, HEAD
    )
    dattended_low = jnp.sum(output_gate[..., None] * dexpanded, axis=2).astype(jnp.bfloat16)
    doutput_gate = jnp.sum(dexpanded * attended[:, :, None, :], axis=3)
    doutput_logit = (
        (doutput_gate * output_mask * output_sig * (1.0 - output_sig))
        .astype(jnp.bfloat16)
        .reshape(seq_rows, HEADS * AEXP)
    )
    dprobs = jnp.einsum("qhw,khw->hqk", dattended_low, mixed, preferred_element_type=jnp.float32)
    inner = jnp.sum(probs * dprobs, axis=2, keepdims=True)
    dscore_low = (probs * (dprobs - inner)).astype(jnp.bfloat16)
    dquery_rot = (
        jnp.einsum("hqk,khw->qhw", dscore_low, key_rot, preferred_element_type=jnp.float32)
        * score_scale
    )
    dkey_rot = (
        jnp.einsum("hqk,qhw->khw", dscore_low, query_rot, preferred_element_type=jnp.float32)
        * score_scale
    )
    dmixed = jnp.einsum(
        "hqk,qhw->khw", probs_low, dattended_low, preferred_element_type=jnp.float32
    )
    dquery_low = (
        unrotate(dquery_rot, cosine, sine).astype(jnp.bfloat16).reshape(seq_rows, HEADS * HEAD)
    )
    dkey_low = unrotate(dkey_rot, cosine, sine).astype(jnp.bfloat16).reshape(seq_rows, HEADS * HEAD)
    dvalues_low = (
        (value_gate[..., None] * dmixed[:, :, None, :])
        .astype(jnp.bfloat16)
        .reshape(seq_rows, HEADS * AEXP * HEAD)
    )
    dvalue_gate = jnp.sum(dmixed[:, :, None, :] * values_all, axis=3)
    dvalue_logit = (
        (dvalue_gate * value_mask * value_sig * (1.0 - value_sig))
        .astype(jnp.bfloat16)
        .reshape(seq_rows, HEADS * AEXP)
    )
    sum_value = tree.sum_rows(*spread_call(coords, tree, tokens, dvalues_low, 512))
    dqk_low = jnp.concatenate([dquery_low, dkey_low], axis=1)
    sum_qk = tree.sum_rows(*spread_call(coords, tree, normed_low, dqk_low, 512))
    dlogits = jnp.concatenate([dvalue_logit, doutput_logit], axis=1)
    dlogits = jnp.pad(dlogits, ((0, 0), (0, small - routers)))
    sum_small = tree.sum_rows(*spread_call(coords, tree, tokens, dlogits, small, extra))
    dnormed = contract_cols(dquery_low, query_weight) + contract_cols(dkey_low, key_weight)
    dscaled = dnormed * norm_gain
    dnorm_in = inverse_std * (
        dscaled
        - jnp.mean(dscaled, axis=1, keepdims=True)
        - scaled * jnp.mean(dscaled * scaled, axis=1, keepdims=True)
    )
    dinput_rest = (
        contract_cols(dvalues_low, value_weight)
        + contract_cols(dvalue_logit, value_router)
        + contract_cols(doutput_logit, output_router)
    )
    grad_tokens = (dhidden + dnorm_in + dinput_rest).astype(jnp.bfloat16)

    qk = HEADS * HEAD
    grad_query, grad_key = sum_qk[:, :qk], sum_qk[:, qk:]
    first = (lax.axis_index("dp") * groups + me) * rows_each
    rows_of = lambda w: lax.dynamic_slice_in_dim(w, first, rows_each, 0)
    grad_gain = jnp.sum(
        grad_query * rows_of(query_weight).astype(F32) + grad_key * rows_of(key_weight).astype(F32),
        axis=1,
    ) / rows_of(norm_gain)
    half = HEADS * AEXP
    got_bits = sum_small[: experts_all // devices, routers + experts_all :][:, :6]
    got_counts = jnp.sum(got_bits * (2.0 ** jnp.arange(6, dtype=F32)), axis=1)
    counts = running_counts + got_counts.astype(jnp.int32)
    return (
        output,
        grad_tokens,
        grad_gain,
        grad_query,
        grad_key,
        sum_value,
        sum_output,
        sum_small[:, :half],
        sum_small[:, half:routers],
        sum_small[:, routers : routers + experts_all],
        expert_grads[:, 0],
        expert_grads[:, 1],
        counts,
    )


def solution(mesh):
    both = ("dp", "expert")
    in_specs = (
        P(both, None),
        P(),
        P(),
        P(),
        P(),
        P(),
        P(),
        P(),
        P(),
        P("expert", None, None),
        P("expert", None, None),
        P(both),
        P(both, None, None),
        P(both, None, None),
        P(both, None),
        P(both),
        P(both, None),
    )
    out_specs = (
        P(both, None),
        P(both, None),
        P(both),
        P(both, None),
        P(both, None),
        P(both, None),
        P(both, None),
        P(both, None),
        P(both, None),
        P(both, None),
        P("expert", "dp", None),
        P("expert", "dp", None),
        P(both),
    )
    return jax.shard_map(shards, mesh=mesh, in_specs=in_specs, out_specs=out_specs, check_vma=False)
```

```python
import functools
import math

import jax
import jax.numpy as jnp
from jax import lax
from jax.experimental import pallas as pl
from jax.experimental.pallas import tpu as pltpu
from jax.sharding import PartitionSpec as P

HEADS = 4
HEAD = 128
AEXP = 5
BF = jnp.bfloat16
F32 = jnp.float32
VMEM_LIMIT = 60 * 1024 * 1024
GELU_C = math.sqrt(2.0 / math.pi)
GELU_K = 0.044715


def rope_tables(seq_rows, head_width):
    half_width = head_width // 2
    ladder = jnp.arange(half_width, dtype=jnp.float32) * (2.0 / head_width)
    freqs = jnp.exp(-math.log(10000.0) * ladder)
    angles = jnp.arange(seq_rows, dtype=jnp.float32)[:, None] * freqs[None, :]
    cosine, sine = jnp.cos(angles), jnp.sin(angles)
    return (
        jnp.concatenate([cosine, cosine], axis=1),
        jnp.concatenate([-sine, sine], axis=1),
    )


class Task:
    def __init__(self, gen):
        self.gen = gen
        self.done = False
        self.result = None
        self.advance(None)

    def advance(self, value):
        try:
            self.out = self.gen.send(value)
        except StopIteration as stop:
            self.done, self.out, self.result = True, None, stop.value


def end_round(tasks, extra=()):
    tasks = [t for t in tasks if not t.done]
    got, extra = lax.optimization_barrier((tuple(t.out for t in tasks), extra))
    for task, value in zip(tasks, got):
        task.advance(value)
    return extra


def finish(tasks, extra=()):
    while any(not t.done for t in tasks):
        extra = end_round(tasks, extra)
    return extra


def total(*parts):
    return functools.reduce(lambda a, b: a + b, [p.astype(F32) for p in parts])


def add(*parts):
    return total(*parts).astype(BF)


class Grid:
    def __init__(self, dp, size):
        self.dp = dp
        self.xs = dp // 2
        self.hi = 4
        self.lo = size // 4
        self.size = size

    def coords(self):
        dp, ex = lax.axis_index("dp"), lax.axis_index("expert")
        return jnp.stack([dp % 2, dp // 2, ex % self.lo, ex // self.lo])

    def half(self, x, axis, core):
        shape = x.shape
        each = shape[axis] // self.dp
        x = x.reshape(shape[:axis] + (self.xs, 2, each) + shape[axis + 1 :])
        x = lax.dynamic_index_in_dim(x, core, axis + 1, False)
        return x.reshape(shape[:axis] + (self.xs * each,) + shape[axis + 1 :])

    def core_shift(self, x):
        return lax.ppermute(x, "dp", [(i, i ^ 1) for i in range(self.dp)])

    def x_shift(self, x):
        pairs = [(i, (i // 2 + 1) % self.xs * 2 + i % 2) for i in range(self.dp)]
        return lax.ppermute(x, "dp", pairs)

    def hi_shift(self, x, by=1):
        pairs = [
            (i, ((i // self.lo + by) % self.hi) * self.lo + i % self.lo) for i in range(self.size)
        ]
        return lax.ppermute(x, "expert", pairs)

    def lo_shift(self, x):
        pairs = [
            (i, (i // self.lo) * self.lo + (i % self.lo + 1) % self.lo) for i in range(self.size)
        ]
        return lax.ppermute(x, "expert", pairs)

    def sources(self):
        me = lax.axis_index("expert")
        h, l = me // self.lo, me % self.lo
        return [
            ((h + self.hi - dh) % self.hi) * self.lo + (l + self.lo - dl) % self.lo
            for dh in range(self.hi)
            for dl in range(self.lo)
        ]

    def gather_rows(self, block, known, last_over_hi=False):
        rows = {(0, 0): block}
        known[0] = block
        steps = self.hi + self.lo - 2
        last = (self.hi - 1, self.lo - 1)
        for step in range(steps):
            fresh = {}
            for dh in range(self.hi):
                for dl in range(self.lo):
                    if dh + dl == step + 1:
                        if dl == 0 or (last_over_hi and (dh, dl) == last):
                            fresh[(dh, dl)] = self.hi_shift(rows[(dh - 1, dl)])
                        else:
                            fresh[(dh, dl)] = self.lo_shift(rows[(dh, dl - 1)])
            got = yield fresh
            for (dh, dl), value in got.items():
                known[dh * self.lo + dl] = value
            if last_over_hi and step == steps - 2:
                got = yield got
            rows.update(got)

    def at(self, a, b):
        return ((self.hi - a) % self.hi) * self.lo + (self.lo - b) % self.lo

    def sum_rows(self, part):
        p = lambda a, b: part(self.at(a, b))
        sums = {}
        for step in range(self.hi + self.lo - 2):
            sent = {}
            for a in range(self.hi):
                for b in range(self.lo):
                    if (self.hi - 1 - a) + (self.lo - 1 - b) == step:
                        mine = add(p(a, b), *sums.pop((a, b), ()))
                        if b > 0:
                            sent[(a, b - 1, 0)] = self.lo_shift(mine)
                        else:
                            sent[(a - 1, b, 1)] = self.hi_shift(mine)
            got = yield sent
            for (a, b, _), value in got.items():
                sums.setdefault((a, b), []).append(value)
        return [p(0, 0), *sums.pop((0, 0))]

    def sum_rows_hi(self, part):
        p = lambda a, b: part(self.at(a, b))
        if self.lo != 2:
            return (yield from self.sum_rows(part))
        one, own = yield self.hi_shift(p(3, 1)), self.lo_shift(p(0, 1))
        one, two = yield self.lo_shift(add(p(2, 1), one)), self.hi_shift(p(3, 0))
        one, two = yield self.hi_shift(add(p(2, 0), one, two)), self.lo_shift(p(1, 1))
        one = yield self.hi_shift(add(p(1, 0), one, two))
        return [p(0, 0), own, one]

    def ring(self, parts, shift):
        acc = parts[-1]
        for b in range(len(parts) - 2, -1, -1):
            acc = yield shift(acc)
            if b:
                acc = add(parts[b], acc)
        return [parts[0], acc]

    def tree(self, parts, order):
        shifts = {"x": self.x_shift, "lo": self.lo_shift, "hi": self.hi_shift}
        left = ["x", "lo", "hi"]
        for name in order:
            if name != order[0]:
                axis = left.index(name)
                parts = [
                    add(*[lax.index_in_dim(v, i, axis, False) for v in acc])
                    for i in range(acc[0].shape[axis])
                ]
            left.remove(name)
            if name == order[-1] == "hi":
                acc = yield [self.hi_shift(parts[b], b) for b in range(1, self.hi)]
                return total(parts[0], *acc)
            acc = yield from self.ring(parts, shifts[name])
        return total(*acc)

    def expert_tree(self, near, far, cuts):
        got = yield self.core_shift(far)
        each = near.shape[1] // cuts
        out = []
        for c in range(cuts):
            cut = slice(c * each, (c + 1) * each)
            acc = add(near[self.xs - 1, cut], got[self.xs - 1, cut])
            for b in range(self.xs - 2, -1, -1):
                acc, near, got = yield self.x_shift(acc), near, got
                if b:
                    acc = add(near[b, cut], got[b, cut], acc)
            out.append((near[0, cut], got[0, cut], acc))
        return out


def gather_kernel(js, cap, *refs):
    count = len(js)
    rows, slots, out = refs[:count], [refs[count].at[j] for j in js], refs[count + 1]
    step, seq_rows = slots[0].shape
    for i in range(count):
        place = lax.broadcasted_iota(jnp.int32, (step, cap, seq_rows), 1).astype(F32)
        pick = (slots[i][...][:, None, :] == place).astype(F32).astype(BF)
        got = jnp.dot(
            pick.reshape(step * cap, seq_rows), rows[i][...], preferred_element_type=F32
        )
        out[:, i * cap : (i + 1) * cap, :] = got.astype(BF).reshape(step, cap, got.shape[1])


def slot_kernel(count, base_ref, *refs):
    codes, out, turned = refs[:count], refs[count], refs[count + 1]
    _, experts, seq_rows = out.shape
    ids = base_ref[0] + 1 + lax.broadcasted_iota(jnp.int32, (experts, seq_rows), 0)
    before = lax.broadcasted_iota(jnp.int32, (seq_rows, seq_rows), 0)
    after = lax.broadcasted_iota(jnp.int32, (seq_rows, seq_rows), 1)
    earlier = (before < after).astype(F32).astype(BF)
    for s in range(count):
        member = codes[s][0:1, :] == ids
        for k in range(1, codes[s].shape[0]):
            member = member | (codes[s][k : k + 1, :] == ids)
        ones = member.astype(F32)
        place = jnp.dot(ones.astype(BF), earlier, preferred_element_type=F32)
        slot = jnp.where(member, place, -1.0)
        out[s] = slot
        turned[s] = jnp.transpose(slot).astype(BF)


def slot_call(codes, base, experts):
    count = len(codes)
    seq_rows = codes[0].shape[1]
    vmem = pl.BlockSpec(memory_space=pltpu.VMEM)
    return pl.pallas_call(
        functools.partial(slot_kernel, count),
        in_specs=[pl.BlockSpec(memory_space=pltpu.SMEM)] + [vmem] * count,
        out_specs=[vmem, vmem],
        out_shape=[
            jax.ShapeDtypeStruct((count, experts, seq_rows), F32),
            jax.ShapeDtypeStruct((count, seq_rows, experts), BF),
        ],
        compiler_params=pltpu.CompilerParams(vmem_limit_bytes=20 * 1024 * 1024),
        name="slots",
    )(base, *codes)


def gather_call(rows, slots, js, cap):
    count = len(rows)
    experts = slots.shape[1]
    width = rows[0].shape[1]
    groups, _, seq_rows = slots.shape
    flops = 2 * count * experts * cap * seq_rows * width
    return pl.pallas_call(
        functools.partial(gather_kernel, js, cap),
        grid=(experts // 8,),
        in_specs=[pl.BlockSpec((seq_rows, width), lambda i: (0, 0))] * count
        + [pl.BlockSpec((groups, 8, seq_rows), lambda i: (0, i, 0))],
        out_specs=pl.BlockSpec((8, count * cap, width), lambda i: (i, 0, 0)),
        out_shape=jax.ShapeDtypeStruct((experts, count * cap, width), BF),
        compiler_params=pltpu.CompilerParams(vmem_limit_bytes=VMEM_LIMIT),
        cost_estimate=pl.CostEstimate(
            flops=flops, bytes_accessed=2 * experts * count * cap * width, transcendentals=0
        ),
        name="gather_rows",
    )(*rows, slots)


def expert_kernel(groups, per, cap, many, at_ref, *refs):
    n = groups // per
    xs_in, gs_in = refs[:n], refs[n : 2 * n]
    up, down, router = refs[2 * n : 2 * n + 3]
    outs = refs[2 * n + 3 :]
    moe = outs[:groups]
    dhid = outs[groups : 2 * groups]
    near, far, grt = outs[2 * groups : 2 * groups + 3]
    xs, gs, w, d2, gacc = outs[2 * groups + 3 :]
    step = pl.program_id(0)
    ff = up.shape[2]

    @pl.when(step == 0)
    def _():
        for k in range(many):
            w[k, :, ff:] = router[...]
        grt[...] = jnp.zeros_like(grt)

    for k in range(many):
        for i in range(n):
            xs[k, i * per * cap : (i + 1) * per * cap, :] = xs_in[i][k]
            gs[k, i * per * cap : (i + 1) * per * cap, :] = gs_in[i][k]
        w[k, :, :ff] = up[k]
    both = [jnp.dot(xs[k], w[k], preferred_element_type=F32) for k in range(many)]
    us = [jnp.dot(gs[k], down[k], preferred_element_type=F32) for k in range(many)]
    scaled = []
    for k in range(many):
        pre, u = both[k][:, :ff], us[k]
        sel = lax.broadcasted_iota(jnp.int32, pre.shape, 1) == step * many + k
        logit = jnp.sum(jnp.where(sel, both[k][:, ff:], 0.0), axis=1, keepdims=True)
        chosen = jax.nn.sigmoid(logit)
        square = pre * pre
        t = jnp.tanh(GELU_C * (pre + GELU_K * (square * pre)))
        half = 0.5 * (1.0 + t)
        act = (half * pre).astype(BF)
        slope = half + 0.5 * pre * (1.0 - t * t) * (GELU_C * (1.0 + 3.0 * GELU_K * square))
        act32 = act.astype(F32)
        dchosen = jnp.sum(u * act32, axis=1, keepdims=True)
        drl = dchosen * chosen * (1.0 - chosen)
        scaled.append((chosen * act32).astype(BF))
        d2[k, :, :ff] = (chosen * u * slope).astype(BF)
        d2[k, :, ff:] = jnp.where(sel, drl, 0.0).astype(BF)
    for k in range(many):
        dgot = lax.dot_general(
            d2[k], w[k], (((1,), (1,)), ((), ())), preferred_element_type=F32
        ).astype(BF)
        got = lax.dot_general(
            scaled[k], down[k], (((1,), (1,)), ((), ())), preferred_element_type=F32
        ).astype(BF)
        for s in range(groups):
            moe[s][k] = got[s * cap : (s + 1) * cap]
            dhid[s][k] = dgot[s * cap : (s + 1) * cap]
    x_size, _, _, _, lanes = near.shape
    for k in range(many):
        gu = lax.dot_general(d2[k], xs[k], (((0,), (0,)), ((), ())), preferred_element_type=F32)
        gacc[k, 0] = gu[:ff]
        grt[...] += gu[ff : ff + grt.shape[0]]
        gacc[k, 1] = lax.dot_general(
            scaled[k], gs[k], (((0,), (0,)), ((), ())), preferred_element_type=F32
        )
        for xr in range(x_size):
            base = lax.rem(at_ref[1] + xr, x_size) * 2
            for cr, out in enumerate((near, far)):
                cut = pl.multiple_of((base + lax.rem(at_ref[0] + cr, 2)) * lanes, lanes)
                for i in range(2):
                    out[xr, k, i] = gacc[k, i, :, pl.ds(cut, lanes)].astype(BF)


def expert_call(coords, x_size, groups, xs, gs, up, down, router, cap, many=2):
    n = len(xs)
    experts, width, ff = up.shape
    per = groups // n
    rows = groups * cap
    pad = -(-experts // 8) * 8
    lanes = width // (2 * x_size)
    row_spec = pl.BlockSpec((many, per * cap, width), lambda e, _: (e, 0, 0))
    w_spec = pl.BlockSpec((many, width, ff), lambda e, _: (e, 0, 0))
    whole = lambda *shape: pl.BlockSpec(shape, lambda e, _: (0,) * len(shape))
    g_spec = pl.BlockSpec((x_size, many, 2, ff, lanes), lambda e, _: (0, e, 0, 0, 0))
    s_spec = pl.BlockSpec((many, cap, width), lambda e, _: (e, 0, 0))
    one = jax.ShapeDtypeStruct((experts, cap, width), BF)
    outs = pl.pallas_call(
        functools.partial(expert_kernel, groups, per, cap, many),
        grid_spec=pltpu.PrefetchScalarGridSpec(
            num_scalar_prefetch=1,
            grid=(experts // many,),
            in_specs=[row_spec] * (2 * n) + [w_spec, w_spec, whole(width, ff)],
            out_specs=[s_spec] * (2 * groups) + [g_spec, g_spec, whole(pad, width)],
            scratch_shapes=[
                pltpu.VMEM((many, rows, width), BF),
                pltpu.VMEM((many, rows, width), BF),
                pltpu.VMEM((many, width, 2 * ff), BF),
                pltpu.VMEM((many, rows, 2 * ff), BF),
                pltpu.VMEM((many, 2, ff, width), F32),
            ],
        ),
        out_shape=[one] * (2 * groups)
        + [jax.ShapeDtypeStruct((x_size, experts, 2, ff, lanes), BF)] * 2
        + [jax.ShapeDtypeStruct((pad, width), F32)],
        compiler_params=pltpu.CompilerParams(vmem_limit_bytes=VMEM_LIMIT),
        cost_estimate=pl.CostEstimate(
            flops=experts * rows * width * ff * 2 * 8,
            bytes_accessed=experts * rows * width * 8,
            transcendentals=0,
        ),
        name="experts",
    )(coords, *xs, *gs, up, down, router)
    return outs[:groups], outs[groups : 2 * groups], outs[-3], outs[-2], outs[-1]


def scatter_kernel(js, *refs):
    count = len(js)
    rows, slots, outs = refs[:count], [refs[count].at[j] for j in js], refs[count + 1 :]
    experts, cap, width = rows[0].shape
    all_slots = experts * cap
    rowi = lax.broadcasted_iota(jnp.int32, (experts, all_slots), 0)
    coli = lax.broadcasted_iota(jnp.int32, (experts, all_slots), 1)
    spread = (coli // cap == rowi).astype(F32).astype(BF)
    for s in range(count):
        wide = jnp.dot(slots[s][...], spread, preferred_element_type=F32)
        lane = lax.broadcasted_iota(jnp.int32, wide.shape, 1) % cap
        put = (wide == lane.astype(F32)).astype(F32).astype(BF)
        outs[s][...] = jnp.dot(
            put, rows[s][...].reshape(all_slots, width), preferred_element_type=F32
        ).astype(BF)


def scatter_call(rows, slots, js):
    count = len(rows)
    experts, cap, width = rows[0].shape
    seq_rows = slots.shape[1]
    return pl.pallas_call(
        functools.partial(scatter_kernel, js),
        out_shape=[jax.ShapeDtypeStruct((seq_rows, width), BF)] * count,
        compiler_params=pltpu.CompilerParams(vmem_limit_bytes=40 * 1024 * 1024),
        cost_estimate=pl.CostEstimate(
            flops=2 * count * seq_rows * experts * cap * width,
            bytes_accessed=2 * count * experts * cap * width,
            transcendentals=0,
        ),
        name="scatter_rows",
    )(*rows, slots)


AXES = ("x", "lo", "hi")


def spread_kernel(sizes, first, rows, at_ref, *refs):
    left, left_far, right, right_far = refs[:4]
    turned, res = refs[-2:]
    outs = refs[-2 - sizes[first] : -2]
    extra = refs[4] if len(refs) == 4 + len(outs) + 3 else None
    seq_rows = left.shape[0]
    x_size, lo, hi = sizes

    @pl.when(pl.program_id(0) == 0)
    def _():
        turned[:, :seq_rows] = jnp.transpose(left[...])
        turned[:, seq_rows:] = jnp.transpose(left_far[...])

    got = jnp.dot(turned[:, :seq_rows], right[...], preferred_element_type=F32)
    got += jnp.dot(turned[:, seq_rows:], right_far[...], preferred_element_type=F32)
    res[...] = got if extra is None else got + extra[...].astype(F32)
    for xr in range(x_size):
        x = lax.rem(at_ref[1] + xr, x_size)
        for lr in range(lo):
            l = lax.rem(at_ref[2] + lr, lo)
            for hr in range(hi):
                h = lax.rem(at_ref[3] + hr, hi)
                start = pl.multiple_of(((x * hi + h) * lo + l) * rows, rows)
                place = [xr, lr, hr]
                out = outs[place.pop(first)]
                out[place[0], place[1]] = res[pl.ds(start, rows), :].astype(BF)


def spread_call(coords, grid, left, right, tile, first, extra=None):
    seq_rows, width = left[0].shape
    cols = right[0].shape[1]
    sizes = (grid.xs, grid.lo, grid.hi)
    at = AXES.index(first)
    others = sizes[:at] + sizes[at + 1 :]
    rows = width // math.prod(sizes)
    o_spec = pl.BlockSpec((*others, rows, tile), lambda j, _: (0, 0, 0, j))
    in_specs = [pl.BlockSpec((seq_rows, width), lambda j, _: (0, 0))] * 2
    in_specs += [pl.BlockSpec((seq_rows, tile), lambda j, _: (0, j))] * 2
    args = [*left, *right]
    if extra is not None:
        in_specs.append(pl.BlockSpec((width, tile), lambda j, _: (0, j)))
        args.append(extra)
    return pl.pallas_call(
        functools.partial(spread_kernel, sizes, at, rows),
        grid_spec=pltpu.PrefetchScalarGridSpec(
            num_scalar_prefetch=1,
            grid=(cols // tile,),
            in_specs=in_specs,
            out_specs=[o_spec] * sizes[at],
            scratch_shapes=[pltpu.VMEM((width, 2 * seq_rows), BF), pltpu.VMEM((width, tile), F32)],
        ),
        out_shape=[jax.ShapeDtypeStruct((*others, rows, cols), BF)] * sizes[at],
        compiler_params=pltpu.CompilerParams(vmem_limit_bytes=40 * 1024 * 1024),
        cost_estimate=pl.CostEstimate(
            flops=4 * seq_rows * width * cols, bytes_accessed=2 * width * cols, transcendentals=0
        ),
        name="weight_grad",
    )(coords, *args)


NT = (((1,), (1,)), ((), ()))
TN = (((0,), (0,)), ((), ()))


def dot_nt(a, b):
    return lax.dot_general(a, b, NT, preferred_element_type=F32)


def dot_tn(a, b):
    return lax.dot_general(a, b, TN, preferred_element_type=F32)


def dot(a, b):
    return jnp.dot(a, b, preferred_element_type=F32)


def column(x, at):
    lane = lax.broadcasted_iota(jnp.int32, x.shape, 1)
    return jnp.sum(jnp.where(lane == at, x, 0.0), axis=1, keepdims=True)


def pick_mask(choice):
    picks = choice.shape[1]
    row = lax.broadcasted_iota(jnp.int32, (picks, HEADS * AEXP), 0)
    head = lax.broadcasted_iota(jnp.int32, (picks, HEADS * AEXP), 1) // AEXP
    low = choice.astype(F32).astype(BF)
    first = dot(low, (row == 2 * head).astype(F32).astype(BF))
    second = dot(low, (row == 2 * head + 1).astype(F32).astype(BF))
    expert = (lax.broadcasted_iota(jnp.int32, first.shape, 1) % AEXP).astype(F32)
    return ((first == expert) | (second == expert)).astype(F32)


def normalize(x):
    mean = jnp.mean(x, axis=1, keepdims=True)
    centered = x - mean
    inverse = lax.rsqrt(jnp.mean(centered * centered, axis=1, keepdims=True) + 1e-05)
    return centered * inverse, inverse


def probabilities(q, k, length):
    scores = dot_nt(q, k) * (1.0 / math.sqrt(HEAD))
    row = lax.broadcasted_iota(jnp.int32, scores.shape, 0)
    col = lax.broadcasted_iota(jnp.int32, scores.shape, 1)
    scores = jnp.where((col <= row) & (col < length), scores, -1e30)
    expo = jnp.exp(scores - jnp.max(scores, axis=1, keepdims=True))
    return expo / jnp.sum(expo, axis=1, keepdims=True)


def forward_kernel(
    length_ref, tokens, gain, cos, sin, wq, wk, wv, wo, vr, orr, vc, oc,
    hidden, hidden_low, normed, q_out, k_out, mixed_out, vals_out, att_out, exp_out,
    vsig, vmask, osig, omask, acc,
):
    h = pl.program_id(0)

    @pl.when(h == 0)
    def _():
        scaled, _ = normalize(tokens[...].astype(F32))
        normed[...] = (scaled * gain[...]).astype(BF)
        vsig[...] = jax.nn.sigmoid(dot(tokens[...], vr[...]))
        osig[...] = jax.nn.sigmoid(dot(tokens[...], orr[...]))
        vmask[...] = pick_mask(vc[...])
        omask[...] = pick_mask(oc[...])
        acc[...] = tokens[...].astype(F32)

    q = dot(normed[...], wq[...])
    k = dot(normed[...], wk[...])
    q = (q * cos[...] + pltpu.roll(q, HEAD // 2, 1) * sin[...]).astype(BF)
    k = (k * cos[...] + pltpu.roll(k, HEAD // 2, 1) * sin[...]).astype(BF)
    q_out[...] = q
    k_out[...] = k
    vals = dot(tokens[...], wv[...])
    vals_out[...] = vals
    gate = vsig[...] * vmask[...]
    mixed = jnp.zeros_like(q, F32)
    for e in range(AEXP):
        mixed += column(gate, h * AEXP + e) * vals[:, e * HEAD : (e + 1) * HEAD]
    mixed = mixed.astype(BF)
    mixed_out[...] = mixed
    probs = probabilities(q, k, length_ref[0]).astype(BF)
    att = dot(probs, mixed)
    att_out[...] = att
    gate = osig[...] * omask[...]
    for e in range(AEXP):
        exp_out[:, e * HEAD : (e + 1) * HEAD] = (column(gate, h * AEXP + e) * att).astype(BF)
    acc[...] += dot_nt(exp_out[...], wo[...])

    @pl.when(h == pl.num_programs(0) - 1)
    def _():
        hidden[...] = acc[...]
        hidden_low[...] = acc[...].astype(BF)


def whole_spec(*shape):
    return pl.BlockSpec(shape, lambda h, _: (0,) * len(shape))


def head_spec(rows, cols):
    return pl.BlockSpec((rows, cols), lambda h, _: (0, h))


def forward_call(lengths, tokens, gain, cos, sin, wq, wk, wv, wo, vr, orr, vc, oc):
    rows, width = tokens.shape
    many = AEXP * HEAD
    gates = HEADS * AEXP
    shape = lambda cols, kind: jax.ShapeDtypeStruct((rows, cols), kind)
    return pl.pallas_call(
        forward_kernel,
        grid_spec=pltpu.PrefetchScalarGridSpec(
            num_scalar_prefetch=1,
            grid=(HEADS,),
            in_specs=[
                whole_spec(rows, width),
                whole_spec(1, width),
                whole_spec(rows, HEAD),
                whole_spec(rows, HEAD),
                head_spec(width, HEAD),
                head_spec(width, HEAD),
                head_spec(width, many),
                head_spec(width, many),
                whole_spec(width, gates),
                whole_spec(width, gates),
                whole_spec(rows, 2 * HEADS),
                whole_spec(rows, 2 * HEADS),
            ],
            out_specs=[
                whole_spec(rows, width),
                whole_spec(rows, width),
                whole_spec(rows, width),
                head_spec(rows, HEAD),
                head_spec(rows, HEAD),
                head_spec(rows, HEAD),
                head_spec(rows, many),
                head_spec(rows, HEAD),
                head_spec(rows, many),
            ]
            + [whole_spec(rows, gates)] * 4,
            scratch_shapes=[pltpu.VMEM((rows, width), F32)],
        ),
        out_shape=[
            shape(width, F32),
            shape(width, BF),
            shape(width, BF),
            shape(HEADS * HEAD, BF),
            shape(HEADS * HEAD, BF),
            shape(HEADS * HEAD, BF),
            shape(HEADS * many, F32),
            shape(HEADS * HEAD, F32),
            shape(HEADS * many, BF),
        ]
        + [shape(gates, F32)] * 4,
        compiler_params=pltpu.CompilerParams(vmem_limit_bytes=40 * 1024 * 1024),
        cost_estimate=pl.CostEstimate(
            flops=2 * rows * width * HEADS * (2 * HEAD + 2 * many),
            bytes_accessed=2 * width * HEADS * (2 * HEAD + 2 * many),
            transcendentals=0,
        ),
        name="attention_forward",
    )(lengths, tokens, gain, cos, sin, wq, wk, wv, wo, vr, orr, vc, oc)


def backward_kernel(
    length_ref, dbranch, cos, sin, wo, q_in, k_in, mixed_in, vals, att, vsig, vmask, osig, omask,
    dqk, dvals, dlogits, dl,
):
    h = pl.program_id(0)

    @pl.when(h == 0)
    def _():
        dl[...] = jnp.zeros_like(dl)

    lane = lax.broadcasted_iota(jnp.int32, dl.shape, 1)
    scale = 1.0 / math.sqrt(HEAD)
    dexp = dot(dbranch[...], wo[...])
    datt = jnp.zeros_like(att)
    for e in range(AEXP):
        at = h * AEXP + e
        part = dexp[:, e * HEAD : (e + 1) * HEAD]
        sig, mask = column(osig[...], at), column(omask[...], at)
        datt += (sig * mask) * part
        logit = jnp.sum(part * att[...], axis=1, keepdims=True) * mask * sig * (1.0 - sig)
        dl[...] += jnp.where(lane == HEADS * AEXP + at, logit, 0.0)
    datt = datt.astype(BF)
    q, k, mixed = q_in[...], k_in[...], mixed_in[...]
    probs = probabilities(q, k, length_ref[0])
    dp = dot_nt(datt, mixed)
    inner = jnp.sum(probs * dp, axis=1, keepdims=True)
    dscore = (probs * (dp - inner)).astype(BF)
    dq = dot(dscore, k) * scale
    dk = dot_tn(dscore, q) * scale
    dmixed = dot_tn(probs.astype(BF), datt)
    dqk[:, :HEAD] = (dq * cos[...] - pltpu.roll(dq, HEAD // 2, 1) * sin[...]).astype(BF)
    dqk[:, HEAD:] = (dk * cos[...] - pltpu.roll(dk, HEAD // 2, 1) * sin[...]).astype(BF)
    for e in range(AEXP):
        at = h * AEXP + e
        part = vals[:, e * HEAD : (e + 1) * HEAD]
        sig, mask = column(vsig[...], at), column(vmask[...], at)
        dvals[:, e * HEAD : (e + 1) * HEAD] = ((sig * mask) * dmixed).astype(BF)
        logit = jnp.sum(part * dmixed, axis=1, keepdims=True) * mask * sig * (1.0 - sig)
        dl[...] += jnp.where(lane == at, logit, 0.0)

    @pl.when(h == pl.num_programs(0) - 1)
    def _():
        dlogits[...] = dl[...].astype(BF)


def backward_call(lengths, dbranch, cos, sin, wo, q, k, mixed, vals, att, gates):
    rows, width = dbranch.shape
    many = AEXP * HEAD
    return pl.pallas_call(
        backward_kernel,
        grid_spec=pltpu.PrefetchScalarGridSpec(
            num_scalar_prefetch=1,
            grid=(HEADS,),
            in_specs=[
                whole_spec(rows, width),
                whole_spec(rows, HEAD),
                whole_spec(rows, HEAD),
                head_spec(width, many),
                head_spec(rows, HEAD),
                head_spec(rows, HEAD),
                head_spec(rows, HEAD),
                head_spec(rows, many),
                head_spec(rows, HEAD),
            ]
            + [whole_spec(rows, HEADS * AEXP)] * 4,
            out_specs=[head_spec(rows, 2 * HEAD), head_spec(rows, many), whole_spec(rows, 128)],
            scratch_shapes=[pltpu.VMEM((rows, 128), F32)],
        ),
        out_shape=[
            jax.ShapeDtypeStruct((rows, HEADS * 2 * HEAD), BF),
            jax.ShapeDtypeStruct((rows, HEADS * many), BF),
            jax.ShapeDtypeStruct((rows, 128), BF),
        ],
        compiler_params=pltpu.CompilerParams(vmem_limit_bytes=40 * 1024 * 1024),
        cost_estimate=pl.CostEstimate(
            flops=2 * rows * width * HEADS * many * 2,
            bytes_accessed=2 * width * HEADS * many,
            transcendentals=0,
        ),
        name="attention_backward",
    )(lengths, dbranch, cos, sin, wo, q, k, mixed, vals, att, *gates)


def input_kernel(tokens, gain, dhidden, dqk, dvals, dlogits, wq, wk, wv, vr, orr, out, dn, rest):
    h = pl.program_id(0)

    @pl.when(h == 0)
    def _():
        gates = HEADS * AEXP
        dn[...] = jnp.zeros_like(dn)
        rest[...] = (
            dhidden[...]
            + dot_nt(dlogits[:, :gates], vr[...])
            + dot_nt(dlogits[:, gates : 2 * gates], orr[...])
        )

    dn[...] += dot_nt(dqk[:, :HEAD], wq[...]) + dot_nt(dqk[:, HEAD:], wk[...])
    rest[...] += dot_nt(dvals[...], wv[...])

    @pl.when(h == pl.num_programs(0) - 1)
    def _():
        scaled, inverse = normalize(tokens[...].astype(F32))
        dscaled = dn[...] * gain[...]
        inside = (
            dscaled
            - jnp.mean(dscaled, axis=1, keepdims=True)
            - scaled * jnp.mean(dscaled * scaled, axis=1, keepdims=True)
        )
        out[...] = (rest[...] + inverse * inside).astype(BF)


def input_call(tokens, gain, dhidden, dqk, dvals, dlogits, wq, wk, wv, vr, orr):
    rows, width = tokens.shape
    many = AEXP * HEAD
    whole = lambda *shape: pl.BlockSpec(shape, lambda h: (0,) * len(shape))
    head = lambda *shape: pl.BlockSpec(shape, lambda h: (0, h))
    return pl.pallas_call(
        input_kernel,
        grid=(HEADS,),
        in_specs=[
            whole(rows, width),
            whole(1, width),
            whole(rows, width),
            head(rows, 2 * HEAD),
            head(rows, many),
            whole(rows, 128),
            head(width, HEAD),
            head(width, HEAD),
            head(width, many),
            whole(width, HEADS * AEXP),
            whole(width, HEADS * AEXP),
        ],
        out_specs=whole(rows, width),
        out_shape=jax.ShapeDtypeStruct((rows, width), BF),
        scratch_shapes=[pltpu.VMEM((rows, width), F32)] * 2,
        compiler_params=pltpu.CompilerParams(vmem_limit_bytes=40 * 1024 * 1024),
        cost_estimate=pl.CostEstimate(
            flops=2 * rows * width * HEADS * (many + 2 * HEAD),
            bytes_accessed=2 * width * HEADS * (many + 2 * HEAD),
            transcendentals=0,
        ),
        name="input_grad",
    )(tokens, gain, dhidden, dqk, dvals, dlogits, wq, wk, wv, vr, orr)


def shards(
    tokens,
    norm_gain,
    query_weight,
    key_weight,
    value_weight,
    output_weight,
    value_router,
    output_router,
    expert_router,
    expert_up,
    expert_down,
    lengths,
    value_choice,
    output_choice,
    expert_choice,
    running_counts,
    cotangent,
):
    seq_rows, model_width = tokens.shape
    groups = lax.axis_size("expert")
    grid = Grid(lax.axis_size("dp"), groups)
    coords = grid.coords()
    me = lax.axis_index("expert")
    local_experts, _, ff = expert_up.shape
    experts_all = local_experts * groups
    picks_per = expert_choice.shape[1]
    cap = 3 * seq_rows * picks_per // (2 * experts_all)
    position = jnp.arange(seq_rows, dtype=jnp.int32)
    seq_length = lengths[0]

    code = jnp.where((position < seq_length)[:, None], expert_choice + 1, 0)
    all_grads, all_codes, all_hidden = {}, {}, {}
    grad_ring = Task(grid.gather_rows(cotangent, all_grads, True))
    code_ring = Task(grid.gather_rows(jnp.transpose(code), all_codes))

    cosine, sine = rope_tables(seq_rows, HEAD)
    gain = norm_gain.reshape(1, model_width)
    vc = value_choice.reshape(seq_rows, -1)
    oc = output_choice.reshape(seq_rows, -1)
    core = coords[0]

    def split(x, axis=1):
        return grid.half(x, axis, core), grid.core_shift(grid.half(x, axis, 1 - core))

    if grid.lo == 2:
        end_round([grad_ring, code_ring])
    forward = forward_call(
        lengths, tokens, gain, cosine, sine, query_weight, key_weight, value_weight, output_weight,
        value_router, output_router, vc, oc,
    )
    forward = end_round([grad_ring, code_ring], forward)
    hidden, hidden_low, normed_low, query_rot, key_rot, mixed, values_all, attended, expanded = (
        forward[:9]
    )
    gates = forward[9:]
    tokens_both, normed_both, expanded_far, hidden_low = end_round(
        [grad_ring, code_ring],
        (split(tokens), split(normed_low), grid.core_shift(expanded), hidden_low),
    )

    ring = Task(grid.gather_rows(hidden_low, all_hidden))
    end_round([ring, code_ring])
    finish([code_ring])
    codes = [all_codes[j] for j in range(groups)]
    slot, slot_low = slot_call(codes, (me * local_experts).reshape(1), local_experts)

    def take(known, j):
        return gather_call([known[j], known[j + 1]], slot, (j, j + 1), cap)

    xs, gs = {}, {}
    if grid.lo == 2:
        gs[0], gs[2] = end_round([ring], (take(all_grads, 0), take(all_grads, 2)))
        gs[4], xs[0] = end_round([ring, grad_ring], (take(all_grads, 4), take(all_hidden, 0)))
        xs[2], xs[4] = end_round([ring, grad_ring], (take(all_hidden, 2), take(all_hidden, 4)))
    finish([ring, grad_ring])
    for j in range(0, groups, 2):
        xs[j] = xs[j] if j in xs else take(all_hidden, j)
        gs[j] = gs[j] if j in gs else take(all_grads, j)
    xs = [xs[j] for j in range(0, groups, 2)]
    gs = [gs[j] for j in range(0, groups, 2)]

    router_mine = lax.dynamic_slice_in_dim(expert_router, me * local_experts, local_experts, 1)
    router_pad = jnp.pad(router_mine, ((0, 0), (0, ff - local_experts)))
    moe_rows, dhid_rows, near, far, grad_router_t = expert_call(
        coords, grid.xs, groups, xs, gs, expert_up, expert_down, router_pad, cap
    )
    dhid, moe = {}, {}

    def scatter(rows, known, places):
        js = [grid.at(*place) for place in places]
        for j, value in zip(js, scatter_call([rows[j] for j in js], slot_low, js)):
            known[j] = value
        return [known[j] for j in js]

    def home(rows, known):
        def part(j):
            if j not in known:
                mate = j ^ 1
                got = scatter_call([rows[j], rows[mate]], slot_low, (j, mate))
                known[j], known[mate] = got
            return known[j]

        return part

    devices = grid.dp * groups
    rows_each = model_width // devices
    labels_all = jnp.arange(experts_all, dtype=jnp.int32)
    local_counts = jnp.sum(
        (code[:, :, None] == labels_all + 1).astype(jnp.int32), axis=(0, 1), dtype=jnp.int32
    )
    bits = (local_counts[:, None] >> jnp.arange(6, dtype=jnp.int32)) & 1
    bits = bits.reshape(devices, experts_all // devices, 6)
    bits = jnp.pad(bits, ((0, 0), (0, rows_each - experts_all // devices), (0, 0)))
    bits = bits.reshape(model_width, 6).astype(BF)
    routers = 2 * HEADS * AEXP
    small = -(-(routers + experts_all + 6) // 256) * 256
    extra = jnp.pad(bits, ((0, 0), (routers + experts_all, small - routers - experts_all - 6)))
    extra = lax.dynamic_update_slice_in_dim(
        extra,
        jnp.transpose(grad_router_t)[:, :local_experts].astype(BF),
        routers + me * local_experts,
        1,
    )
    extra_near, extra_far = split(extra, 0)

    two = grid.lo == 2
    if two:
        scatter(dhid_rows, dhid, [(3, 1), (0, 1)])
    back = Task(grid.sum_rows_hi(home(dhid_rows, dhid)))
    shares = Task(grid.expert_tree(near, far, 4))
    if two:
        end_round([back, shares], scatter(dhid_rows, dhid, [(2, 1), (3, 0)]))
        _, extra_far = end_round([back, shares], (scatter(dhid_rows, dhid, [(2, 0), (1, 1)]), extra_far))
        end_round(
            [back, shares],
            scatter(dhid_rows, dhid, [(1, 0), (0, 0)]) + scatter(moe_rows, moe, [(3, 1), (3, 0)]),
        )
    extra = add(extra_near, extra_far)
    out_ring = Task(grid.sum_rows(home(moe_rows, moe)))
    more = scatter(moe_rows, moe, [(2, 1), (2, 0)]) if two else ()
    _, extra = end_round([back, shares, out_ring], (more, extra))
    finish([back])
    dhidden = total(cotangent, *back.result)
    dbranch_low = dhidden.astype(BF)

    dbranch_both = split(dbranch_low)
    own = backward_call(
        lengths, dbranch_low, cosine, sine, output_weight, query_rot, key_rot, mixed, values_all,
        attended, gates,
    )
    more = scatter(moe_rows, moe, [(1, 1), (1, 0)]) if two else ()
    own, dbranch_both, _ = end_round([out_ring, shares], (own, dbranch_both, more))
    other = [grid.core_shift(v) for v in own]
    output_parts = spread_call(coords, grid, dbranch_both, (expanded, expanded_far), 512, "x")
    more = scatter(moe_rows, moe, [(0, 1), (0, 0)]) if two else ()
    own, other, output_parts, _ = end_round([out_ring, shares], (own, other, output_parts, more))
    finish([shares])
    output_sum = Task(grid.tree(output_parts, ("x", "lo", "hi")))
    dqk, dvalues, dlogits = zip(own, other)
    cut = dvalues[0].shape[1] // 2
    value_parts = [
        spread_call(coords, grid, tokens_both, [v[:, c : c + cut] for v in dvalues], 640, "lo")
        for c in (0, cut)
    ]
    qk_part = spread_call(coords, grid, normed_both, dqk, 512, "hi")
    wide = [jnp.pad(v, ((0, 0), (0, small - v.shape[1]))) for v in dlogits]
    small_part = spread_call(coords, grid, tokens_both, wide, small, "hi", extra)
    value_parts, qk_part, small_part = end_round([out_ring], (value_parts, qk_part, small_part))
    finish([out_ring])

    first_sum = Task(grid.tree(value_parts[0], ("lo", "x", "hi")))
    second_sum = Task(grid.tree(value_parts[1], ("lo", "x", "hi")))
    qk_sum = Task(grid.tree(qk_part, ("hi", "x", "lo")))
    small_sum = Task(grid.tree(small_part, ("hi", "x", "lo")))
    grad_tokens = input_call(
        tokens, gain, dhidden, own[0], own[1], own[2], query_weight, key_weight,
        value_weight, value_router, output_router,
    )
    grad_tokens = end_round([output_sum, first_sum, qk_sum, small_sum], grad_tokens)
    expert_grads = jnp.concatenate([total(*parts) for parts in shares.result], axis=0)
    expert_grads = [jnp.swapaxes(expert_grads[:, i], 1, 2) for i in range(2)]
    expert_grads = end_round([first_sum, second_sum, qk_sum, small_sum], expert_grads)
    output = (hidden + total(*out_ring.result)).astype(BF)
    output = end_round([output_sum, first_sum, second_sum, qk_sum, small_sum], output)
    finish([output_sum, first_sum, second_sum, qk_sum, small_sum])
    sum_output, sum_qk, sum_small = output_sum.result, qk_sum.result, small_sum.result
    sum_value = jnp.concatenate([first_sum.result, second_sum.result], axis=1)
    qk = HEADS * HEAD
    sum_qk = jnp.swapaxes(sum_qk.reshape(rows_each, HEADS, 2, HEAD), 1, 2)
    grad_query = sum_qk[:, 0].reshape(rows_each, qk)
    grad_key = sum_qk[:, 1].reshape(rows_each, qk)
    first = (lax.axis_index("dp") * groups + me) * rows_each
    rows_of = lambda w: lax.dynamic_slice_in_dim(w, first, rows_each, 0)
    grad_gain = jnp.sum(
        grad_query * rows_of(query_weight).astype(F32) + grad_key * rows_of(key_weight).astype(F32),
        axis=1,
    ) / rows_of(norm_gain)
    half = HEADS * AEXP
    got_bits = sum_small[: experts_all // devices, routers + experts_all :][:, :6]
    got_counts = jnp.sum(got_bits * (2.0 ** jnp.arange(6, dtype=F32)), axis=1)
    counts = running_counts + got_counts.astype(jnp.int32)
    return (
        output,
        grad_tokens,
        grad_gain,
        grad_query,
        grad_key,
        sum_value,
        sum_output,
        sum_small[:, :half],
        sum_small[:, half:routers],
        sum_small[:, routers : routers + experts_all],
        *expert_grads,
        counts,
    )


def solution(mesh):
    both = ("dp", "expert")
    in_specs = (
        P(both, None),
        P(),
        P(),
        P(),
        P(),
        P(),
        P(),
        P(),
        P(),
        P("expert", None, None),
        P("expert", None, None),
        P(both),
        P(both, None, None),
        P(both, None, None),
        P(both, None),
        P(both),
        P(both, None),
    )
    out_specs = (
        P(both, None),
        P(both, None),
        P(both),
        P(both, None),
        P(both, None),
        P(both, None),
        P(both, None),
        P(both, None),
        P(both, None),
        P(both, None),
        P("expert", "dp", None),
        P("expert", "dp", None),
        P(both),
    )
    return jax.shard_map(shards, mesh=mesh, in_specs=in_specs, out_specs=out_specs, check_vma=False)
```

```python
import functools
import math

import jax
import jax.numpy as jnp
import numpy as np
from jax import lax
from jax.experimental import pallas as pl
from jax.experimental.pallas import tpu as pltpu
from jax.sharding import PartitionSpec as P

HEADS = 4
HEAD = 128
AEXP = 5
BF = jnp.bfloat16
F32 = jnp.float32
VMEM_LIMIT = 60 * 1024 * 1024
GELU_C = math.sqrt(2.0 / math.pi)
GELU_K = 0.044715


def rope_tables(seq_rows, head_width):
    half_width = head_width // 2
    ladder = np.arange(half_width, dtype=np.float32) * np.float32(2.0 / head_width)
    freqs = np.exp(np.float32(-math.log(10000.0)) * ladder)
    angles = np.arange(seq_rows, dtype=np.float32)[:, None] * freqs[None, :]
    cosine, sine = np.cos(angles), np.sin(angles)
    return np.concatenate([cosine, cosine], axis=1), np.concatenate([-sine, sine], axis=1)


class Task:
    def __init__(self, gen):
        self.gen = gen
        self.done = False
        self.result = None
        self.advance(None)

    def advance(self, value):
        try:
            self.out = self.gen.send(value)
        except StopIteration as stop:
            self.done, self.out, self.result = True, None, stop.value


def end_round(tasks, extra=()):
    tasks = [t for t in tasks if not t.done]
    got, extra = lax.optimization_barrier((tuple(t.out for t in tasks), extra))
    for task, value in zip(tasks, got):
        task.advance(value)
    return extra


def finish(tasks, extra=()):
    while any(not t.done for t in tasks):
        extra = end_round(tasks, extra)
    return extra


def total(*parts):
    return functools.reduce(lambda a, b: a + b, [p.astype(F32) for p in parts])


def add(*parts):
    return total(*parts).astype(BF)


class Grid:
    def __init__(self, dp, size):
        self.dp = dp
        self.xs = dp // 2
        self.hi = 4
        self.lo = size // 4
        self.size = size

    def coords(self):
        dp, ex = lax.axis_index("dp"), lax.axis_index("expert")
        return jnp.stack([dp % 2, dp // 2, ex % self.lo, ex // self.lo])

    def core_shift(self, x):
        return lax.ppermute(x, "dp", [(i, i ^ 1) for i in range(self.dp)])

    def x_shift(self, x):
        pairs = [(i, (i // 2 + 1) % self.xs * 2 + i % 2) for i in range(self.dp)]
        return lax.ppermute(x, "dp", pairs)

    def hi_shift(self, x, by=1):
        pairs = [
            (i, ((i // self.lo + by) % self.hi) * self.lo + i % self.lo) for i in range(self.size)
        ]
        return lax.ppermute(x, "expert", pairs)

    def lo_shift(self, x):
        pairs = [
            (i, (i // self.lo) * self.lo + (i % self.lo + 1) % self.lo) for i in range(self.size)
        ]
        return lax.ppermute(x, "expert", pairs)

    def sources(self):
        me = lax.axis_index("expert")
        h, l = me // self.lo, me % self.lo
        return [
            ((h + self.hi - dh) % self.hi) * self.lo + (l + self.lo - dl) % self.lo
            for dh in range(self.hi)
            for dl in range(self.lo)
        ]

    def gather_rows(self, block, known, last_over_hi=False):
        rows = {(0, 0): block}
        known[0] = block
        steps = self.hi + self.lo - 2
        last = (self.hi - 1, self.lo - 1)
        for step in range(steps):
            fresh = {}
            for dh in range(self.hi):
                for dl in range(self.lo):
                    if dh + dl == step + 1:
                        if dl == 0 or (last_over_hi and (dh, dl) == last):
                            fresh[(dh, dl)] = self.hi_shift(rows[(dh - 1, dl)])
                        else:
                            fresh[(dh, dl)] = self.lo_shift(rows[(dh, dl - 1)])
            got = yield fresh
            for (dh, dl), value in got.items():
                known[dh * self.lo + dl] = value
            if last_over_hi and step == steps - 2:
                got = yield got
            rows.update(got)

    def at(self, a, b):
        return ((self.hi - a) % self.hi) * self.lo + (self.lo - b) % self.lo

    def sum_rows(self, part):
        p = lambda a, b: part(self.at(a, b))
        sums = {}
        for step in range(self.hi + self.lo - 2):
            sent = {}
            for a in range(self.hi):
                for b in range(self.lo):
                    if (self.hi - 1 - a) + (self.lo - 1 - b) == step:
                        mine = add(p(a, b), *sums.pop((a, b), ()))
                        if b > 0:
                            sent[(a, b - 1, 0)] = self.lo_shift(mine)
                        else:
                            sent[(a - 1, b, 1)] = self.hi_shift(mine)
            got = yield sent
            for (a, b, _), value in got.items():
                sums.setdefault((a, b), []).append(value)
        return [p(0, 0), *sums.pop((0, 0))]

    def sum_rows_hi(self, part):
        p = lambda a, b: part(self.at(a, b))
        if self.lo != 2:
            return (yield from self.sum_rows(part))
        one, own = yield self.hi_shift(p(3, 1)), self.lo_shift(p(0, 1))
        one, two = yield self.lo_shift(add(p(2, 1), one)), self.hi_shift(p(3, 0))
        one, two = yield self.hi_shift(add(p(2, 0), one, two)), self.lo_shift(p(1, 1))
        one = yield self.hi_shift(add(p(1, 0), one, two))
        return [p(0, 0), own, one]

    def ring(self, parts, shift):
        acc = parts[-1]
        for b in range(len(parts) - 2, -1, -1):
            acc = yield shift(acc)
            if b:
                acc = add(parts[b], acc)
        return [parts[0], acc]

    def pieces(self, value):
        out, (near, passing) = [value], (yield self.core_shift(value), self.x_shift(value))
        out.append(near)
        for step in range(1, self.xs):
            if step < self.xs - 1:
                near, ahead = yield self.core_shift(passing), self.x_shift(passing)
            else:
                near, ahead = (yield self.core_shift(passing)), None
            out += [passing, near]
            passing = ahead
        return out

    def direct(self, parts):
        got = yield [self.hi_shift(parts[b], b) for b in range(1, self.hi)]
        return [parts[0], *got]

    def lo_hi(self, parts):
        acc = yield from self.ring(parts, self.lo_shift)
        acc = yield from self.direct([add(*[v[b] for v in acc]) for b in range(self.hi)])
        return total(*acc)

    def hi_lo(self, parts):
        acc = yield from self.direct(parts)
        acc = yield from self.ring([add(*[v[b] for v in acc]) for b in range(self.lo)], self.lo_shift)
        return total(*acc)

    def expert_tree(self, near, far, cuts):
        got = yield self.core_shift(far)
        each = near.shape[1] // cuts
        out = []
        for c in range(cuts):
            cut = slice(c * each, (c + 1) * each)
            if c == cuts - 1:
                near, got = yield near, got
            acc = add(near[self.xs - 1, cut], got[self.xs - 1, cut])
            for b in range(self.xs - 2, -1, -1):
                acc, near, got = yield self.x_shift(acc), near, got
                if b:
                    acc = add(near[b, cut], got[b, cut], acc)
            out.append(acc)
        return near, got, out


def gather_kernel(count, cap, base_ref, *refs):
    hidden, grads, (xs, gs, slots) = refs[:count], refs[count : 2 * count], refs[2 * count :]
    step, seq_rows = slots.shape[1:]
    first = base_ref[0] + 1 + pl.program_id(0) * step
    ids = (first + lax.broadcasted_iota(jnp.int32, (step, seq_rows), 0)).astype(F32)
    before = lax.broadcasted_iota(jnp.int32, (seq_rows, seq_rows), 0)
    after = lax.broadcasted_iota(jnp.int32, (seq_rows, seq_rows), 1)
    earlier = (before < after).astype(F32).astype(BF)
    place = lax.broadcasted_iota(jnp.int32, (step, cap, seq_rows), 1).astype(F32)
    for i in range(count):
        digits = hidden[i][seq_rows:, : 2 * seq_rows].astype(F32)
        picks = digits[:, :seq_rows] * 16.0 + digits[:, seq_rows:]
        member = picks[0:1, :] == ids
        for k in range(1, picks.shape[0]):
            member = member | (picks[k : k + 1, :] == ids)
        slot = jnp.where(member, dot(member.astype(F32).astype(BF), earlier), -1.0)
        slots[i] = slot
        pick = (slot[:, None, :] == place).astype(F32).astype(BF).reshape(step * cap, seq_rows)
        for source, out in ((hidden[i], xs), (grads[i], gs)):
            got = dot(pick, source[:seq_rows, :])
            out[:, i * cap : (i + 1) * cap, :] = got.astype(BF).reshape(step, cap, got.shape[1])


def gather_call(base, hidden, grads, experts, cap):
    count = len(hidden)
    seq_rows, width = grads[0].shape
    rows = jax.ShapeDtypeStruct((experts, count * cap, width), BF)
    row_spec = pl.BlockSpec((8, count * cap, width), lambda i, _: (i, 0, 0))
    whole = lambda v: pl.BlockSpec(v.shape, lambda i, _: (0, 0))
    return pl.pallas_call(
        functools.partial(gather_kernel, count, cap),
        grid_spec=pltpu.PrefetchScalarGridSpec(
            num_scalar_prefetch=1,
            grid=(experts // 8,),
            in_specs=[whole(v) for v in (*hidden, *grads)],
            out_specs=[
                row_spec,
                row_spec,
                pl.BlockSpec((count, 8, seq_rows), lambda i, _: (0, i, 0)),
            ],
        ),
        out_shape=[rows, rows, jax.ShapeDtypeStruct((count, experts, seq_rows), F32)],
        compiler_params=pltpu.CompilerParams(vmem_limit_bytes=VMEM_LIMIT),
        cost_estimate=pl.CostEstimate(
            flops=4 * count * experts * cap * seq_rows * width,
            bytes_accessed=4 * experts * count * cap * width,
            transcendentals=0,
        ),
        name="gather_rows",
    )(base, *hidden, *grads)


def expert_kernel(n, groups, cap, many, at_ref, *refs):
    xs_in, gs_in = refs[: n[0]], refs[n[0] : sum(n)]
    up, down, router = refs[sum(n) : sum(n) + 3]
    slots = refs[sum(n) + 3 : sum(n) + 3 + n[0]]
    outs = refs[sum(n) + 3 + n[0] :]
    moe = outs[:groups]
    dhid = outs[groups : 2 * groups]
    near, far, grt = outs[2 * groups : 2 * groups + 3]
    xs, gs, w, d2, gacc, dr = outs[2 * groups + 3 :]
    step = pl.program_id(0)
    ff = up.shape[2]

    @pl.when(step == 0)
    def _():
        for k in range(many):
            w[k, :, ff:] = router[...]
        grt[...] = jnp.zeros_like(grt)

    for k in range(many):
        for whole, pieces in ((xs, xs_in), (gs, gs_in)):
            at = 0
            for piece in pieces:
                whole[k, at : at + piece.shape[1], :] = piece[k]
                at += piece.shape[1]
        w[k, :, :ff] = up[k]
    both = [jnp.dot(xs[k], w[k], preferred_element_type=F32) for k in range(many)]
    us = [jnp.dot(gs[k], down[k], preferred_element_type=F32) for k in range(many)]
    scaled = []
    for k in range(many):
        pre, u = both[k][:, :ff], us[k]
        sel = lax.broadcasted_iota(jnp.int32, pre.shape, 1) == step * many + k
        logit = jnp.sum(jnp.where(sel, both[k][:, ff:], 0.0), axis=1, keepdims=True)
        chosen = jax.nn.sigmoid(logit)
        square = pre * pre
        t = jnp.tanh(GELU_C * (pre + GELU_K * (square * pre)))
        half = 0.5 * (1.0 + t)
        act = (half * pre).astype(BF)
        slope = half + 0.5 * pre * (1.0 - t * t) * (GELU_C * (1.0 + 3.0 * GELU_K * square))
        act32 = act.astype(F32)
        dchosen = jnp.sum(u * act32, axis=1, keepdims=True)
        drl = dchosen * chosen * (1.0 - chosen)
        scaled.append((chosen * act32).astype(BF))
        d2[k, :, :ff] = (chosen * u * slope).astype(BF)
        d2[k, :, ff:] = jnp.where(sel, drl, 0.0).astype(BF)
    for k in range(many):
        dgot = lax.dot_general(
            d2[k], w[k], (((1,), (1,)), ((), ())), preferred_element_type=F32
        ).astype(BF)
        got = lax.dot_general(
            scaled[k], down[k], (((1,), (1,)), ((), ())), preferred_element_type=F32
        ).astype(BF)
        at = pl.multiple_of((step * many + k) * cap, cap)
        for s in range(groups):
            moe[s][k] = got[s * cap : (s + 1) * cap]
            dr[s, pl.ds(at, cap), :] = dgot[s * cap : (s + 1) * cap]
    x_size, _, _, _, lanes = near.shape
    for k in range(many):
        gu = lax.dot_general(d2[k], xs[k], (((0,), (0,)), ((), ())), preferred_element_type=F32)
        gacc[k, 0] = gu[:ff]
        grt[...] += gu[ff : ff + grt.shape[0]]
        gacc[k, 1] = lax.dot_general(
            scaled[k], gs[k], (((0,), (0,)), ((), ())), preferred_element_type=F32
        )
        for xr in range(x_size):
            base = lax.rem(at_ref[1] + xr, x_size) * 2
            for cr, out in enumerate((near, far)):
                cut = pl.multiple_of((base + lax.rem(at_ref[0] + cr, 2)) * lanes, lanes)
                for i in range(2):
                    out[xr, k, i] = gacc[k, i, :, pl.ds(cut, lanes)].astype(BF)

    @pl.when(step == pl.num_programs(0) - 1)
    def _():
        experts = slots[0].shape[1]
        spread = slot_spread(experts, cap)
        source = 0
        for group in slots:
            for i in range(group.shape[0]):
                put = slot_picks(group[i], spread, cap)
                dhid[source][...] = dot(put, dr[source]).astype(BF)
                source += 1


def slot_spread(experts, cap):
    rowi = lax.broadcasted_iota(jnp.int32, (experts, experts * cap), 0)
    coli = lax.broadcasted_iota(jnp.int32, (experts, experts * cap), 1)
    return (coli // cap == rowi).astype(F32).astype(BF)


def slot_picks(slot, spread, cap):
    wide = dot_tn(slot.astype(BF), spread)
    lane = lax.broadcasted_iota(jnp.int32, wide.shape, 1) % cap
    return (wide == lane.astype(F32)).astype(F32).astype(BF)


def expert_call(coords, x_size, groups, xs, gs, up, down, router, slots, cap, many=2):
    experts, width, ff = up.shape
    rows = groups * cap
    pad = -(-experts // 8) * 8
    seq_rows = slots[0].shape[2]
    lanes = width // (2 * x_size)
    row_specs = [
        pl.BlockSpec((many, v.shape[1], width), lambda e, _: (e, 0, 0)) for v in (*xs, *gs)
    ]
    w_spec = pl.BlockSpec((many, width, ff), lambda e, _: (e, 0, 0))
    whole = lambda *shape: pl.BlockSpec(shape, lambda e, _: (0,) * len(shape))
    g_spec = pl.BlockSpec((x_size, many, 2, ff, lanes), lambda e, _: (0, e, 0, 0, 0))
    s_spec = pl.BlockSpec((many, cap, width), lambda e, _: (e, 0, 0))
    one = jax.ShapeDtypeStruct((experts, cap, width), BF)
    outs = pl.pallas_call(
        functools.partial(expert_kernel, (len(xs), len(gs)), groups, cap, many),
        grid_spec=pltpu.PrefetchScalarGridSpec(
            num_scalar_prefetch=1,
            grid=(experts // many,),
            in_specs=[*row_specs, w_spec, w_spec, whole(width, ff)] + [whole(*v.shape) for v in slots],
            out_specs=[s_spec] * groups
            + [whole(seq_rows, width)] * groups
            + [g_spec, g_spec, whole(pad, width)],
            scratch_shapes=[
                pltpu.VMEM((many, rows, width), BF),
                pltpu.VMEM((many, rows, width), BF),
                pltpu.VMEM((many, width, 2 * ff), BF),
                pltpu.VMEM((many, rows, 2 * ff), BF),
                pltpu.VMEM((many, 2, ff, width), F32),
                pltpu.VMEM((groups, experts * cap, width), BF),
            ],
        ),
        out_shape=[one] * groups
        + [jax.ShapeDtypeStruct((seq_rows, width), BF)] * groups
        + [jax.ShapeDtypeStruct((x_size, experts, 2, ff, lanes), BF)] * 2
        + [jax.ShapeDtypeStruct((pad, width), F32)],
        compiler_params=pltpu.CompilerParams(vmem_limit_bytes=VMEM_LIMIT),
        cost_estimate=pl.CostEstimate(
            flops=experts * rows * width * ff * 2 * 8,
            bytes_accessed=experts * rows * width * 8,
            transcendentals=0,
        ),
        name="experts",
    )(coords, *xs, *gs, up, down, router, *slots)
    return outs[:groups], outs[groups : 2 * groups], outs[-3], outs[-2], outs[-1]


def finish_kernel(near, got, *refs):
    accs, (up, down) = refs[:-2], refs[-2:]
    for c, acc in enumerate(accs):

        @pl.when(pl.program_id(0) == c)
        def _(acc=acc):
            for k in range(acc.shape[0]):
                for i, out in enumerate((up, down)):
                    out[k] = jnp.transpose(
                        near[0, k, i].astype(F32) + got[0, k, i].astype(F32) + acc[k, i].astype(F32)
                    )


def finish_call(near, got, accs):
    _, experts, _, ff, lanes = near.shape
    each = accs[0].shape[0]
    mine = pl.BlockSpec((1, each, 2, ff, lanes), lambda c: (0, c, 0, 0, 0))
    out = pl.BlockSpec((each, lanes, ff), lambda c: (c, 0, 0))
    return pl.pallas_call(
        finish_kernel,
        grid=(len(accs),),
        in_specs=[mine, mine]
        + [pl.BlockSpec((each, 2, ff, lanes), lambda c: (0, 0, 0, 0))] * len(accs),
        out_specs=[out, out],
        out_shape=[jax.ShapeDtypeStruct((experts, lanes, ff), F32)] * 2,
        compiler_params=pltpu.CompilerParams(vmem_limit_bytes=VMEM_LIMIT),
        cost_estimate=pl.CostEstimate(
            flops=0, bytes_accessed=20 * experts * lanes * ff, transcendentals=0
        ),
        name="expert_grads",
    )(near, got, *accs)


def scatter_kernel(places, *refs):
    count = len(places)
    rows, slots, outs = refs[:count], refs[count : 2 * count], refs[2 * count :]
    experts, cap, width = rows[0].shape
    spread = slot_spread(experts, cap)
    for s in range(count):
        put = slot_picks(slots[s][places[s]], spread, cap)
        outs[s][...] = dot(put, rows[s][...].reshape(experts * cap, width)).astype(BF)


def scatter_call(rows, slots):
    count = len(rows)
    experts, cap, width = rows[0].shape
    seq_rows = slots[0][0].shape[2]
    return pl.pallas_call(
        functools.partial(scatter_kernel, tuple(j for _, j in slots)),
        out_shape=[jax.ShapeDtypeStruct((seq_rows, width), BF)] * count,
        compiler_params=pltpu.CompilerParams(vmem_limit_bytes=VMEM_LIMIT),
        cost_estimate=pl.CostEstimate(
            flops=2 * count * seq_rows * experts * cap * width,
            bytes_accessed=2 * count * experts * cap * width,
            transcendentals=0,
        ),
        name="scatter_rows",
    )(*rows, *[v for v, _ in slots])


def put_rows(res, outs, sizes, first, rows, at_ref):
    lo, hi = sizes
    for lr in range(lo):
        l = lax.rem(at_ref[2] + lr, lo)
        for hr in range(hi):
            h = lax.rem(at_ref[3] + hr, hi)
            start = pl.multiple_of((h * lo + l) * rows, rows)
            out, place = (outs[lr], hr) if first == "lo" else (outs[hr], lr)
            out[place] = res[pl.ds(start, rows), :].astype(BF)


def gated_kernel(count, sizes, rows, gate_at, at_ref, left, *refs):
    bases, gates, outs, (right, res) = refs[:count], refs[count : 2 * count], refs[2 * count : -2], refs[-2:]
    h = pl.program_id(0)
    seq_rows = bases[0].shape[0]
    lane = lax.broadcasted_iota(jnp.int32, gates[0].shape, 1)
    for p in range(count):
        base, gate = bases[p][...].astype(F32), gates[p][...].astype(F32)
        for e in range(AEXP):
            at = gate_at + h * AEXP + e
            one = (lane == at) | (lane == at + 2 * HEADS * AEXP)
            column_ = jnp.sum(jnp.where(one, gate, 0.0), axis=1, keepdims=True)
            right[p * seq_rows : (p + 1) * seq_rows, e * HEAD : (e + 1) * HEAD] = (
                column_ * base
            ).astype(BF)
    res[...] = dot(left[...], right[...])
    put_rows(res, outs, sizes, "lo", rows, at_ref)


def gated_call(coords, grid, left, bases, base_at, packs, gate_at):
    width, tokens = left.shape
    seq_rows = bases[0].shape[0]
    sizes = (grid.lo, grid.hi)
    rows = width // (grid.lo * grid.hi)
    tile = AEXP * HEAD
    count = len(bases)
    out = (grid.hi, rows, HEADS * tile)
    return pl.pallas_call(
        functools.partial(gated_kernel, count, sizes, rows, gate_at),
        grid_spec=pltpu.PrefetchScalarGridSpec(
            num_scalar_prefetch=1,
            grid=(HEADS,),
            in_specs=[whole_spec(width, tokens)]
            + [pl.BlockSpec((seq_rows, HEAD), lambda h, _: (0, base_at // HEAD + h))] * count
            + [pl.BlockSpec((seq_rows, 128), lambda h, _: (0, HEADS))] * count,
            out_specs=[pl.BlockSpec((grid.hi, rows, tile), lambda h, _: (0, 0, h))] * grid.lo,
            scratch_shapes=[pltpu.VMEM((tokens, tile), BF), pltpu.VMEM((width, tile), F32)],
        ),
        out_shape=[jax.ShapeDtypeStruct(out, BF)] * grid.lo,
        compiler_params=pltpu.CompilerParams(vmem_limit_bytes=VMEM_LIMIT),
        cost_estimate=pl.CostEstimate(
            flops=2 * width * tokens * HEADS * tile,
            bytes_accessed=2 * width * HEADS * tile,
            transcendentals=0,
        ),
        name="gated_grad",
    )(coords, left, *bases, *packs)


def plain_kernel(count, sizes, rows, at_ref, left, last_left, extra, *refs):
    factors, outs, (right, res) = refs[:count], refs[count:-2], refs[-2:]
    step, last = pl.program_id(0), pl.num_programs(0) - 1
    seq_rows = factors[0].shape[0]
    for p in range(count):
        right[p * seq_rows : (p + 1) * seq_rows, :] = factors[p][...]

    @pl.when(step < last)
    def _():
        res[...] = dot(left[...], right[...])

    @pl.when(step == last)
    def _():
        width = res.shape[0]
        mine = pl.ds(pl.multiple_of((at_ref[1] * 2 + at_ref[0]) * width, width), width)
        res[...] = dot(last_left[...], right[...]) + jnp.transpose(extra[:, mine])

    put_rows(res, outs, sizes, "hi", rows, at_ref)


def plain_call(coords, grid, left, last_left, extra, factors, cols):
    width, tokens = left.shape
    seq_rows = factors[0].shape[0]
    tile = extra.shape[0]
    sizes = (grid.lo, grid.hi)
    rows = width // (grid.lo * grid.hi)
    count = len(factors)
    return pl.pallas_call(
        functools.partial(plain_kernel, count, sizes, rows),
        grid_spec=pltpu.PrefetchScalarGridSpec(
            num_scalar_prefetch=1,
            grid=(cols // tile,),
            in_specs=[
                whole_spec(width, tokens),
                whole_spec(width, tokens),
                whole_spec(*extra.shape),
            ]
            + [head_spec(seq_rows, tile)] * count,
            out_specs=[pl.BlockSpec((grid.lo, rows, tile), lambda j, _: (0, 0, j))] * grid.hi,
            scratch_shapes=[pltpu.VMEM((tokens, tile), BF), pltpu.VMEM((width, tile), F32)],
        ),
        out_shape=[jax.ShapeDtypeStruct((grid.lo, rows, cols), BF)] * grid.hi,
        compiler_params=pltpu.CompilerParams(vmem_limit_bytes=VMEM_LIMIT),
        cost_estimate=pl.CostEstimate(
            flops=2 * width * tokens * cols, bytes_accessed=2 * width * cols, transcendentals=0
        ),
        name="plain_grad",
    )(coords, left, last_left, extra, *factors)


def turn_kernel(count, at_ref, *refs):
    for n in range(len(refs) * count // (count + 1)):
        seq_rows, out = refs[n].shape[0], refs[len(refs) * count // (count + 1) + n // count]
        each = out.shape[0]
        mine = pl.ds(pl.multiple_of((at_ref[1] * 2 + at_ref[0]) * each, each), each)
        at = n % count * seq_rows
        out[:, at : at + seq_rows] = jnp.transpose(refs[n][:, mine])


def turn_call(coords, grid, groups):
    seq_rows, width = groups[0][0].shape
    count = len(groups[0])
    vmem = pl.BlockSpec(memory_space=pltpu.VMEM)
    return pl.pallas_call(
        functools.partial(turn_kernel, count),
        in_specs=[pl.BlockSpec(memory_space=pltpu.SMEM)] + [vmem] * (count * len(groups)),
        out_specs=[vmem] * len(groups),
        out_shape=[jax.ShapeDtypeStruct((width // grid.dp, count * seq_rows), BF)] * len(groups),
        compiler_params=pltpu.CompilerParams(vmem_limit_bytes=VMEM_LIMIT),
        name="turn",
    )(coords, *[v for group in groups for v in group])


NT = (((1,), (1,)), ((), ()))
TN = (((0,), (0,)), ((), ()))


def dot_nt(a, b):
    return lax.dot_general(a, b, NT, preferred_element_type=F32)


def dot_tn(a, b):
    return lax.dot_general(a, b, TN, preferred_element_type=F32)


def dot(a, b):
    return jnp.dot(a, b, preferred_element_type=F32)


def column(x, at):
    lane = lax.broadcasted_iota(jnp.int32, x.shape, 1)
    return jnp.sum(jnp.where(lane == at, x, 0.0), axis=1, keepdims=True)


def pick_mask(choice):
    picks = choice.shape[0]
    row = lax.broadcasted_iota(jnp.int32, (picks, HEADS * AEXP), 0)
    head = lax.broadcasted_iota(jnp.int32, (picks, HEADS * AEXP), 1) // AEXP
    low = choice.astype(F32).astype(BF)
    first = dot_tn(low, (row == head).astype(F32).astype(BF))
    second = dot_tn(low, (row == HEADS + head).astype(F32).astype(BF))
    expert = (lax.broadcasted_iota(jnp.int32, first.shape, 1) % AEXP).astype(F32)
    return ((first == expert) | (second == expert)).astype(F32)


def normalize(x):
    mean = jnp.mean(x, axis=1, keepdims=True)
    centered = x - mean
    inverse = lax.rsqrt(jnp.mean(centered * centered, axis=1, keepdims=True) + 1e-05)
    return centered * inverse, inverse


def probabilities(q, k, length):
    scores = dot_nt(q, k) * (1.0 / math.sqrt(HEAD))
    row = lax.broadcasted_iota(jnp.int32, scores.shape, 0)
    col = lax.broadcasted_iota(jnp.int32, scores.shape, 1)
    scores = jnp.where((col <= row) & (col < length), scores, -1e30)
    expo = jnp.exp(scores - jnp.max(scores, axis=1, keepdims=True))
    return expo / jnp.sum(expo, axis=1, keepdims=True)


def forward_head(
    h, length, tokens, normed, cos, sin, wq, wk, wv, wo, vgate, ogate,
    q_out, k_out, mixed_out, vals_out, att_out, expanded,
):
    q = dot(normed[...], wq[...])
    k = dot(normed[...], wk[...])
    q = (q * cos[...] + pltpu.roll(q, HEAD // 2, 1) * sin[...]).astype(BF)
    k = (k * cos[...] + pltpu.roll(k, HEAD // 2, 1) * sin[...]).astype(BF)
    q_out[...] = q
    k_out[...] = k
    vals = dot(tokens[...], wv[...])
    vals_out[...] = vals
    mixed = jnp.zeros_like(q, F32)
    for e in range(AEXP):
        mixed += column(vgate, h * AEXP + e) * vals[:, e * HEAD : (e + 1) * HEAD]
    mixed = mixed.astype(BF)
    mixed_out[...] = mixed
    probs = probabilities(q, k, length).astype(BF)
    att = dot(probs, mixed)
    att_out[...] = att
    for e in range(AEXP):
        expanded[:, e * HEAD : (e + 1) * HEAD] = (column(ogate, h * AEXP + e) * att).astype(BF)
    return dot_nt(expanded[...], wo[...])


def first_heads_kernel(
    length_ref, tokens, cos, sin, wq, wk, wv, wo, gain, vr, orr, vc, oc,
    acc, q_out, k_out, mixed_out, vals_out, att_out, normed, vsig, vmask, osig, omask, expanded,
):
    @pl.when(pl.program_id(0) == 0)
    def _():
        scaled, _ = normalize(tokens[...].astype(F32))
        normed[...] = (scaled * gain[...]).astype(BF)
        vsig[...] = jax.nn.sigmoid(dot_nt(tokens[...], vr[...]))
        osig[...] = jax.nn.sigmoid(dot_nt(tokens[...], orr[...]))
        vmask[...] = pick_mask(vc[...])
        omask[...] = pick_mask(oc[...])
        acc[...] = tokens[...].astype(F32)

    acc[...] += forward_head(
        pl.program_id(0), length_ref[0], tokens, normed, cos, sin, wq, wk, wv, wo,
        vsig[...] * vmask[...], osig[...] * omask[...],
        q_out, k_out, mixed_out, vals_out, att_out, expanded,
    )


def last_heads_kernel(start, *refs):
    length_ref, tokens, cos, sin, wq, wk, wv, wo, normed, vsig, vmask, osig, omask, codes, acc = refs[:15]
    hidden, q_out, k_out, mixed_out, vals_out, att_out, hidden_low, pack, expanded = refs[-9:]
    known_att = refs[15]

    @pl.when(pl.program_id(0) == 0)
    def _():
        hidden[...] = acc[...]

    hidden[...] += forward_head(
        start + pl.program_id(0), length_ref[0], tokens, normed, cos, sin, wq, wk, wv, wo,
        vsig[...] * vmask[...], osig[...] * omask[...],
        q_out, k_out, mixed_out, vals_out, att_out, expanded,
    )

    gates = HEADS * AEXP
    at = (start + pl.program_id(0)) * HEAD
    pack[:, pl.ds(pl.multiple_of(at, HEAD), HEAD)] = att_out[...].astype(BF)

    @pl.when(pl.program_id(0) == 0)
    def _():
        pack[:, : start * HEAD] = known_att[...].astype(BF)
        pack[:, HEADS * HEAD :] = jnp.zeros((pack.shape[0], 128), BF)
        for n, gate in enumerate((vsig[...] * vmask[...], osig[...] * omask[...])):
            high = gate.astype(BF)
            to = HEADS * HEAD + n * gates
            pack[:, to : to + gates] = high
            pack[:, to + 2 * gates : to + 3 * gates] = (gate - high.astype(F32)).astype(BF)

    @pl.when(pl.program_id(0) == pl.num_programs(0) - 1)
    def _():
        rows = hidden.shape[0]
        hidden_low[:rows, :] = hidden[...].astype(BF)
        code = codes[...]
        high = lax.shift_right_logical(code, 4)
        hidden_low[rows:, :rows] = high.astype(F32).astype(BF)
        hidden_low[rows:, rows : 2 * rows] = (code - high * 16).astype(F32).astype(BF)
        hidden_low[rows:, 2 * rows :] = jnp.zeros((code.shape[0], hidden_low.shape[1] - 2 * rows), BF)


def whole_spec(*shape):
    return pl.BlockSpec(shape, lambda h, _: (0,) * len(shape))


def head_spec(rows, cols):
    return pl.BlockSpec((rows, cols), lambda h, _: (0, h))


def heads_common(rows, width, start):
    many = AEXP * HEAD
    head = lambda rows, cols: pl.BlockSpec((rows, cols), lambda h, _: (0, h + start))
    shape = lambda cols, kind: jax.ShapeDtypeStruct((rows, cols), kind)
    in_specs = [
        whole_spec(rows, width),
        whole_spec(rows, HEAD),
        whole_spec(rows, HEAD),
        head(width, HEAD),
        head(width, HEAD),
        head(width, many),
        head(width, many),
    ]
    out_specs = [whole_spec(rows, width)] + [head(rows, HEAD)] * 3
    out_specs += [head(rows, many), head(rows, HEAD)]
    out_shape = [shape(width, F32)] + [shape(HEADS * HEAD, BF)] * 3
    out_shape += [shape(HEADS * many, F32), shape(HEADS * HEAD, F32)]
    cost = pl.CostEstimate(
        flops=rows * width * HEADS * (2 * HEAD + 2 * many),
        bytes_accessed=width * HEADS * (2 * HEAD + 2 * many),
        transcendentals=0,
    )
    return in_specs, out_specs, out_shape, cost


def first_heads(lengths, tokens, cos, sin, wq, wk, wv, wo, gain, vr, orr, vc, oc):
    rows, width = tokens.shape
    gates = HEADS * AEXP
    in_specs, out_specs, out_shape, cost = heads_common(rows, width, 0)
    return pl.pallas_call(
        first_heads_kernel,
        grid_spec=pltpu.PrefetchScalarGridSpec(
            num_scalar_prefetch=1,
            grid=(HEADS // 2,),
            in_specs=in_specs + [whole_spec(*v.shape) for v in (gain, vr, orr, vc, oc)],
            out_specs=out_specs + [whole_spec(rows, width)] + [whole_spec(rows, gates)] * 4,
            scratch_shapes=[pltpu.VMEM((rows, AEXP * HEAD), BF)],
        ),
        out_shape=out_shape
        + [jax.ShapeDtypeStruct((rows, width), BF)]
        + [jax.ShapeDtypeStruct((rows, gates), F32)] * 4,
        compiler_params=pltpu.CompilerParams(vmem_limit_bytes=VMEM_LIMIT),
        cost_estimate=cost,
        name="attention_forward",
    )(lengths, tokens, cos, sin, wq, wk, wv, wo, gain, vr, orr, vc, oc)


def last_heads(lengths, tokens, cos, sin, wq, wk, wv, wo, normed, gates, codes, acc, known):
    rows, width = tokens.shape
    start = HEADS // 2
    in_specs, out_specs, out_shape, cost = heads_common(rows, width, start)
    operands = [lengths, tokens, cos, sin, wq, wk, wv, wo, normed, *gates, codes, acc]
    in_specs += [whole_spec(*v.shape) for v in operands[8:]]
    operands.append(known[-1])
    in_specs.append(whole_spec(rows, start * HEAD))
    low = (rows + codes.shape[0], width)
    packed = (rows, HEADS * HEAD + 128)
    return pl.pallas_call(
        functools.partial(last_heads_kernel, start),
        grid_spec=pltpu.PrefetchScalarGridSpec(
            num_scalar_prefetch=1,
            grid=(HEADS - start,),
            in_specs=in_specs + [pl.BlockSpec(memory_space=pl.ANY)] * len(known),
            out_specs=out_specs + [whole_spec(*low), whole_spec(*packed)],
            scratch_shapes=[pltpu.VMEM((rows, AEXP * HEAD), BF)],
        ),
        out_shape=out_shape + [jax.ShapeDtypeStruct(low, BF), jax.ShapeDtypeStruct(packed, BF)],
        input_output_aliases={len(operands) + i: 1 + i for i in range(len(known))},
        compiler_params=pltpu.CompilerParams(vmem_limit_bytes=VMEM_LIMIT),
        cost_estimate=cost,
        name="attention_forward_rest",
    )(*operands, *known)


def backward_kernel(
    length_ref, cos, sin, wo, q_in, k_in, mixed_in, vals, att, vsig, vmask, osig, omask, dbranch,
    factors, dvals, dl,
):
    h = pl.program_id(0)
    qk_at, logit_at, mixed_at = factor_places(factors.shape[1])

    @pl.when(h == 0)
    def _():
        dl[...] = jnp.zeros_like(dl)
        factors[:, logit_at:mixed_at] = jnp.zeros((dl.shape[0], mixed_at - logit_at), BF)

    lane = lax.broadcasted_iota(jnp.int32, dl.shape, 1)
    scale = 1.0 / math.sqrt(HEAD)
    dexp = dot(dbranch[...], wo[...])
    datt = jnp.zeros_like(att)
    for e in range(AEXP):
        at = h * AEXP + e
        part = dexp[:, e * HEAD : (e + 1) * HEAD]
        sig, mask = column(osig[...], at), column(omask[...], at)
        datt += (sig * mask) * part
        logit = jnp.sum(part * att[...], axis=1, keepdims=True) * mask * sig * (1.0 - sig)
        dl[...] += jnp.where(lane == HEADS * AEXP + at, logit, 0.0)
    datt = datt.astype(BF)
    q, k, mixed = q_in[...], k_in[...], mixed_in[...]
    probs = probabilities(q, k, length_ref[0])
    dp = dot_nt(datt, mixed)
    inner = jnp.sum(probs * dp, axis=1, keepdims=True)
    dscore = (probs * (dp - inner)).astype(BF)
    dq = dot(dscore, k) * scale
    dk = dot_tn(dscore, q) * scale
    dmixed = dot_tn(probs.astype(BF), datt)
    dq = (dq * cos[...] - pltpu.roll(dq, HEAD // 2, 1) * sin[...]).astype(BF)
    dk = (dk * cos[...] - pltpu.roll(dk, HEAD // 2, 1) * sin[...]).astype(BF)
    put = lambda at, value: factors.__setitem__(
        (slice(None), pl.ds(pl.multiple_of(at, HEAD), HEAD)), value
    )
    put(qk_at + h * 2 * HEAD, dq)
    put(qk_at + h * 2 * HEAD + HEAD, dk)
    put(mixed_at + h * HEAD, dmixed.astype(BF))
    for e in range(AEXP):
        at = h * AEXP + e
        part = vals[:, e * HEAD : (e + 1) * HEAD]
        sig, mask = column(vsig[...], at), column(vmask[...], at)
        dvals[:, e * HEAD : (e + 1) * HEAD] = ((sig * mask) * dmixed).astype(BF)
        logit = jnp.sum(part * dmixed, axis=1, keepdims=True) * mask * sig * (1.0 - sig)
        dl[...] += jnp.where(lane == at, logit, 0.0)

    @pl.when(h == pl.num_programs(0) - 1)
    def _():
        factors[:, logit_at : logit_at + dl.shape[1]] = dl[...].astype(BF)


def factor_places(cols):
    return 0, 2 * HEADS * HEAD, cols - HEADS * HEAD


def backward_call(small, lengths, dbranch, cos, sin, wo, q, k, mixed, vals, att, gates):
    rows, width = dbranch.shape
    many = AEXP * HEAD
    cols = HEADS * 3 * HEAD + small
    return pl.pallas_call(
        backward_kernel,
        grid_spec=pltpu.PrefetchScalarGridSpec(
            num_scalar_prefetch=1,
            grid=(HEADS,),
            in_specs=[
                whole_spec(rows, HEAD),
                whole_spec(rows, HEAD),
                head_spec(width, many),
                head_spec(rows, HEAD),
                head_spec(rows, HEAD),
                head_spec(rows, HEAD),
                head_spec(rows, many),
                head_spec(rows, HEAD),
            ]
            + [whole_spec(rows, HEADS * AEXP)] * 4
            + [whole_spec(rows, width)],
            out_specs=[whole_spec(rows, cols), head_spec(rows, many)],
            scratch_shapes=[pltpu.VMEM((rows, 128), F32)],
        ),
        out_shape=[
            jax.ShapeDtypeStruct((rows, cols), BF),
            jax.ShapeDtypeStruct((rows, HEADS * many), BF),
        ],
        compiler_params=pltpu.CompilerParams(vmem_limit_bytes=VMEM_LIMIT),
        cost_estimate=pl.CostEstimate(
            flops=2 * rows * width * HEADS * many * 2,
            bytes_accessed=2 * width * HEADS * many,
            transcendentals=0,
        ),
        name="attention_backward",
    )(lengths, cos, sin, wo, q, k, mixed, vals, att, *gates, dbranch)


def input_kernel(tokens, gain, dhidden, factors, dvals, wq, wk, wv, vr, orr, out, dn, rest):
    h = pl.program_id(0)
    qk_at, logit_at, _ = factor_places(factors.shape[1])

    @pl.when(h == 0)
    def _():
        gates = HEADS * AEXP
        dlogits = factors[:, logit_at : logit_at + 2 * gates]
        dn[...] = jnp.zeros_like(dn)
        rest[...] = (
            dhidden[...]
            + dot(dlogits[:, :gates], vr[...])
            + dot(dlogits[:, gates:], orr[...])
        )

    take = lambda at, size: factors[:, pl.ds(pl.multiple_of(at, HEAD), size)]
    dn[...] += dot_nt(take(qk_at + h * 2 * HEAD, HEAD), wq[...])
    dn[...] += dot_nt(take(qk_at + h * 2 * HEAD + HEAD, HEAD), wk[...])
    rest[...] += dot_nt(dvals[...], wv[...])

    @pl.when(h == pl.num_programs(0) - 1)
    def _():
        scaled, inverse = normalize(tokens[...].astype(F32))
        dscaled = dn[...] * gain[...]
        inside = (
            dscaled
            - jnp.mean(dscaled, axis=1, keepdims=True)
            - scaled * jnp.mean(dscaled * scaled, axis=1, keepdims=True)
        )
        out[...] = (rest[...] + inverse * inside).astype(BF)


def input_call(tokens, gain, dhidden, factors, dvals, wq, wk, wv, vr, orr):
    rows, width = tokens.shape
    many = AEXP * HEAD
    whole = lambda *shape: pl.BlockSpec(shape, lambda h: (0,) * len(shape))
    head = lambda *shape: pl.BlockSpec(shape, lambda h: (0, h))
    return pl.pallas_call(
        input_kernel,
        grid=(HEADS,),
        in_specs=[
            whole(rows, width),
            whole(1, width),
            whole(rows, width),
            whole(*factors.shape),
            head(rows, many),
            head(width, HEAD),
            head(width, HEAD),
            head(width, many),
            whole(HEADS * AEXP, width),
            whole(HEADS * AEXP, width),
        ],
        out_specs=whole(rows, width),
        out_shape=jax.ShapeDtypeStruct((rows, width), BF),
        scratch_shapes=[pltpu.VMEM((rows, width), F32)] * 2,
        compiler_params=pltpu.CompilerParams(vmem_limit_bytes=VMEM_LIMIT),
        cost_estimate=pl.CostEstimate(
            flops=2 * rows * width * HEADS * (many + 2 * HEAD),
            bytes_accessed=2 * width * HEADS * (many + 2 * HEAD),
            transcendentals=0,
        ),
        name="input_grad",
    )(tokens, gain, dhidden, factors, dvals, wq, wk, wv, vr, orr)


def shards(
    tokens,
    norm_gain,
    query_weight,
    key_weight,
    value_weight,
    output_weight,
    value_router,
    output_router,
    expert_router,
    expert_up,
    expert_down,
    lengths,
    value_choice,
    output_choice,
    expert_choice,
    running_counts,
    cotangent,
):
    seq_rows, model_width = tokens.shape
    groups = lax.axis_size("expert")
    grid = Grid(lax.axis_size("dp"), groups)
    coords = grid.coords()
    me = lax.axis_index("expert")
    local_experts, _, ff = expert_up.shape
    experts_all = local_experts * groups
    picks_per = expert_choice.shape[1]
    cap = 3 * seq_rows * picks_per // (2 * experts_all)
    position = jnp.arange(seq_rows, dtype=jnp.int32)
    seq_length = lengths[0]

    code = jnp.where((position < seq_length)[:, None], expert_choice + 1, 0)
    all_grads, all_hidden = {}, {}
    grad_ring = Task(grid.gather_rows(cotangent, all_grads, True))

    cosine, sine = rope_tables(seq_rows, HEAD)
    gain = norm_gain.reshape(1, model_width)
    vc, oc = (
        jnp.transpose(v, (2, 1, 0)).reshape(-1, seq_rows) for v in (value_choice, output_choice)
    )
    turned_routers = (jnp.transpose(value_router), jnp.transpose(output_router))
    weights = (query_weight, key_weight, value_weight, output_weight)
    tokens_task = Task(grid.pieces(tokens))
    got = first_heads(
        lengths, tokens, cosine, sine, *weights, gain, *turned_routers, vc, oc
    )
    acc, *known, normed_low, vsig, vmask, osig, omask = end_round([grad_ring, tokens_task], got)
    gates = (vsig, vmask, osig, omask)
    normed_task = Task(grid.pieces(normed_low))
    got = last_heads(
        lengths, tokens, cosine, sine, *weights, normed_low, gates, jnp.transpose(code), acc, known
    )
    got = end_round([grad_ring, tokens_task, normed_task], got)
    hidden, query_rot, key_rot, mixed, values_all, attended, hidden_low, pack = got
    pack_task = Task(grid.pieces(pack))
    hidden_low = end_round([grad_ring, tokens_task, normed_task, pack_task], hidden_low)

    ring = Task(grid.gather_rows(hidden_low, all_hidden))
    end_round([ring, tokens_task, normed_task, pack_task])
    finish([tokens_task, normed_task, pack_task])
    turned = turn_call(coords, grid, [normed_task.result, tokens_task.result])
    packs = pack_task.result
    base = (me * local_experts).reshape(1)
    xs, gs, slots, slot_groups = [], [], {}, []

    def gather(js):
        return gather_call(
            base, [all_hidden[j] for j in js], [all_grads[j] for j in js], local_experts, cap
        )

    def keep(js, got):
        xs.append(got[0])
        gs.append(got[1])
        slot_groups.append(got[2])
        for i, j in enumerate(js):
            slots[j] = (got[2], i)

    if grid.lo == 2:
        got, turned = end_round([ring], (gather(range(3)), turned))
        keep(range(3), got)
        keep((3, 4), end_round([ring, grad_ring], gather((3, 4))))
        keep((5, 6), end_round([ring, grad_ring], gather((5, 6))))
        finish([ring, grad_ring])
        keep((7,), gather((7,)))
    else:
        finish([ring, grad_ring])
        for j in range(0, groups, 4):
            keep(range(j, j + 4), gather(range(j, j + 4)))

    router_mine = lax.dynamic_slice_in_dim(expert_router, me * local_experts, local_experts, 1)
    router_pad = jnp.pad(router_mine, ((0, 0), (0, ff - local_experts)))
    moe_rows, dhid, near, far, grad_router_t = expert_call(
        coords, grid.xs, groups, xs, gs, expert_up, expert_down, router_pad, slot_groups, cap
    )
    moe = {}

    moe = {}

    def scatter(places):
        js = [grid.at(*place) for place in places]
        moe.update(zip(js, scatter_call([moe_rows[j] for j in js], [slots[j] for j in js])))

    def moe_part(j):
        if j not in moe:
            mate = j ^ 1
            got = scatter_call([moe_rows[j], moe_rows[mate]], [slots[j], slots[mate]])
            moe[j], moe[mate] = got
        return moe[j]

    devices = grid.dp * groups
    rows_each = model_width // devices
    labels_all = jnp.arange(experts_all, dtype=jnp.int32)
    local_counts = jnp.sum(
        (code[:, :, None] == labels_all + 1).astype(jnp.int32), axis=(0, 1), dtype=jnp.int32
    )
    bits = (local_counts[None, :] >> jnp.arange(6, dtype=jnp.int32)[:, None]) & 1
    bits = bits.reshape(6, devices, experts_all // devices)
    bits = jnp.pad(bits, ((0, 0), (0, 0), (0, rows_each - experts_all // devices)))
    bits = bits.reshape(6, model_width).astype(BF)
    routers = 2 * HEADS * AEXP
    small = -(-(routers + experts_all + 6) // 256) * 256
    held = -(-(local_experts + 6) // 16) * 16
    compact = jnp.concatenate(
        [
            grad_router_t[:local_experts].astype(BF),
            jnp.pad(bits, ((0, held - local_experts - 6), (0, 0))),
        ],
        axis=0,
    )

    two = grid.lo == 2
    back = Task(grid.sum_rows_hi(lambda j: dhid[j]))
    shares = Task(grid.expert_tree(near, far, 4))
    if two:
        scatter([(3, 1), (3, 0)])
        moe.update(end_round([back, shares], moe))
        scatter([(2, 1), (2, 0)])
        ready, compact = end_round([back, shares], (moe, compact))
        moe.update(ready)
        scatter([(1, 1), (1, 0)])
    small_task = Task(grid.pieces(compact))
    if two:
        moe.update(end_round([back, shares, small_task], moe))
        scatter([(0, 1), (0, 0)])
    out_ring = Task(grid.sum_rows(moe_part))
    moe.update(end_round([back, shares, small_task, out_ring], moe))
    finish([back, small_task])
    extra = total(*small_task.result)
    extra = lax.dynamic_update_slice_in_dim(
        jnp.pad(
            extra[local_experts : local_experts + 6],
            ((routers + experts_all, small - routers - experts_all - 6), (0, 0)),
        ),
        extra[:local_experts],
        routers + me * local_experts,
        0,
    )

    dhidden = total(cotangent, *back.result)
    dbranch = dhidden.astype(BF)
    branch_task = Task(grid.pieces(dbranch))
    factors, dvalues = backward_call(
        small, lengths, dbranch, cosine, sine, output_weight, query_rot, key_rot, mixed, values_all,
        attended, gates,
    )
    factors, dvalues, extra = end_round([out_ring, branch_task], (factors, dvalues, extra))
    factor_task = Task(grid.pieces(factors))
    finish([branch_task])
    [branch_turned] = turn_call(coords, grid, [branch_task.result])
    output_parts = gated_call(coords, grid, branch_turned, packs, 0, packs, HEADS * AEXP)
    grad_tokens = input_call(
        tokens, gain, dhidden, factors, dvalues, query_weight, key_weight, value_weight,
        *turned_routers,
    )
    output_parts, grad_tokens = end_round(
        [out_ring, factor_task, shares], (output_parts, grad_tokens)
    )

    output_sum = Task(grid.lo_hi(output_parts))
    finish([factor_task])
    factor_pieces = factor_task.result
    _, logit_at, mixed_at = factor_places(factors.shape[1])
    value_parts = gated_call(coords, grid, turned[1], factor_pieces, mixed_at, packs, 0)
    value_parts, factor_pieces = lax.optimization_barrier((value_parts, factor_pieces))
    value_sum = Task(grid.lo_hi(value_parts))
    qk_part = plain_call(coords, grid, *turned, extra, factor_pieces, logit_at + small)
    qk_part = end_round([out_ring, output_sum, shares], qk_part)
    finish([out_ring, shares])
    near, got, accs = shares.result
    qk_sum = Task(grid.hi_lo(qk_part))
    expert_grads = finish_call(near, got, accs)
    output = (hidden + total(*out_ring.result)).astype(BF)
    expert_grads, output = end_round([output_sum, value_sum], (expert_grads, output))
    finish([output_sum])
    finish([value_sum, qk_sum])
    sum_output, sum_value = output_sum.result, value_sum.result
    split_at = logit_at
    sum_qk, sum_small = qk_sum.result[:, :split_at], qk_sum.result[:, split_at:]
    qk = HEADS * HEAD
    sum_qk = jnp.swapaxes(sum_qk.reshape(rows_each, HEADS, 2, HEAD), 1, 2)
    grad_query = sum_qk[:, 0].reshape(rows_each, qk)
    grad_key = sum_qk[:, 1].reshape(rows_each, qk)
    first = (lax.axis_index("dp") * groups + me) * rows_each
    rows_of = lambda w: lax.dynamic_slice_in_dim(w, first, rows_each, 0)
    grad_gain = jnp.sum(
        grad_query * rows_of(query_weight).astype(F32) + grad_key * rows_of(key_weight).astype(F32),
        axis=1,
    ) / rows_of(norm_gain)
    half = HEADS * AEXP
    got_bits = sum_small[: experts_all // devices, routers + experts_all :][:, :6]
    got_counts = jnp.sum(got_bits * (2.0 ** jnp.arange(6, dtype=F32)), axis=1)
    counts = running_counts + got_counts.astype(jnp.int32)
    return (
        output,
        grad_tokens,
        grad_gain,
        grad_query,
        grad_key,
        sum_value,
        sum_output,
        sum_small[:, :half],
        sum_small[:, half:routers],
        sum_small[:, routers : routers + experts_all],
        *expert_grads,
        counts,
    )


def solution(mesh):
    both = ("dp", "expert")
    in_specs = (
        P(both, None),
        P(),
        P(),
        P(),
        P(),
        P(),
        P(),
        P(),
        P(),
        P("expert", None, None),
        P("expert", None, None),
        P(both),
        P(both, None, None),
        P(both, None, None),
        P(both, None),
        P(both),
        P(both, None),
    )
    out_specs = (
        P(both, None),
        P(both, None),
        P(both),
        P(both, None),
        P(both, None),
        P(both, None),
        P(both, None),
        P(both, None),
        P(both, None),
        P(both, None),
        P("expert", "dp", None),
        P("expert", "dp", None),
        P(both),
    )
    return jax.shard_map(shards, mesh=mesh, in_specs=in_specs, out_specs=out_specs, check_vma=False)
```

```python
import functools
import math

import jax
import jax.numpy as jnp
import numpy as np
from jax import lax
from jax.experimental import pallas as pl
from jax.experimental.pallas import tpu as pltpu
from jax.sharding import PartitionSpec as P

HEADS = 4
HEAD = 128
AEXP = 5
BF = jnp.bfloat16
F32 = jnp.float32
VMEM_LIMIT = 60 * 1024 * 1024
GELU_C = math.sqrt(2.0 / math.pi)
GELU_K = 0.044715


def rope_tables(seq_rows, head_width):
    half_width = head_width // 2
    ladder = np.arange(half_width, dtype=np.float32) * np.float32(2.0 / head_width)
    freqs = np.exp(np.float32(-math.log(10000.0)) * ladder)
    angles = np.arange(seq_rows, dtype=np.float32)[:, None] * freqs[None, :]
    cosine, sine = np.cos(angles), np.sin(angles)
    return np.concatenate([cosine, cosine], axis=1), np.concatenate([-sine, sine], axis=1)


class Task:
    def __init__(self, gen):
        self.gen = gen
        self.done = False
        self.result = None
        self.advance(None)

    def advance(self, value):
        try:
            self.out = self.gen.send(value)
        except StopIteration as stop:
            self.done, self.out, self.result = True, None, stop.value


def end_round(tasks, extra=()):
    tasks = [t for t in tasks if not t.done]
    got, extra = lax.optimization_barrier((tuple(t.out for t in tasks), extra))
    for task, value in zip(tasks, got):
        task.advance(value)
    return extra


def finish(tasks, extra=()):
    while any(not t.done for t in tasks):
        extra = end_round(tasks, extra)
    return extra


def total(*parts):
    return functools.reduce(lambda a, b: a + b, [p.astype(F32) for p in parts])


def add(*parts):
    return total(*parts).astype(BF)


class Grid:
    def __init__(self, dp, size):
        self.dp = dp
        self.xs = dp // 2
        self.hi = 4
        self.lo = size // 4
        self.size = size

    def coords(self):
        dp, ex = lax.axis_index("dp"), lax.axis_index("expert")
        return jnp.stack([dp % 2, dp // 2, ex % self.lo, ex // self.lo])

    def core_shift(self, x):
        return lax.ppermute(x, "dp", [(i, i ^ 1) for i in range(self.dp)])

    def x_shift(self, x):
        pairs = [(i, (i // 2 + 1) % self.xs * 2 + i % 2) for i in range(self.dp)]
        return lax.ppermute(x, "dp", pairs)

    def hi_shift(self, x, by=1):
        pairs = [
            (i, ((i // self.lo + by) % self.hi) * self.lo + i % self.lo) for i in range(self.size)
        ]
        return lax.ppermute(x, "expert", pairs)

    def lo_shift(self, x):
        pairs = [
            (i, (i // self.lo) * self.lo + (i % self.lo + 1) % self.lo) for i in range(self.size)
        ]
        return lax.ppermute(x, "expert", pairs)

    def sources(self):
        me = lax.axis_index("expert")
        h, l = me // self.lo, me % self.lo
        return [
            ((h + self.hi - dh) % self.hi) * self.lo + (l + self.lo - dl) % self.lo
            for dh in range(self.hi)
            for dl in range(self.lo)
        ]

    def gather_rows(self, block, known, last_over_hi=False):
        rows = {(0, 0): block}
        known[0] = block
        steps = self.hi + self.lo - 2
        last = (self.hi - 1, self.lo - 1)
        for step in range(steps):
            fresh = {}
            for dh in range(self.hi):
                for dl in range(self.lo):
                    if dh + dl == step + 1:
                        if dl == 0 or (last_over_hi and (dh, dl) == last):
                            fresh[(dh, dl)] = self.hi_shift(rows[(dh - 1, dl)])
                        else:
                            fresh[(dh, dl)] = self.lo_shift(rows[(dh, dl - 1)])
            got = yield fresh
            for (dh, dl), value in got.items():
                known[dh * self.lo + dl] = value
            if last_over_hi and step == steps - 2:
                got = yield got
            rows.update(got)

    def at(self, a, b):
        return ((self.hi - a) % self.hi) * self.lo + (self.lo - b) % self.lo

    def sum_rows(self, part):
        p = lambda a, b: part(self.at(a, b))
        sums = {}
        for step in range(self.hi + self.lo - 2):
            sent = {}
            for a in range(self.hi):
                for b in range(self.lo):
                    if (self.hi - 1 - a) + (self.lo - 1 - b) == step:
                        mine = add(p(a, b), *sums.pop((a, b), ()))
                        if b > 0:
                            sent[(a, b - 1, 0)] = self.lo_shift(mine)
                        else:
                            sent[(a - 1, b, 1)] = self.hi_shift(mine)
            got = yield sent
            for (a, b, _), value in got.items():
                sums.setdefault((a, b), []).append(value)
        return [p(0, 0), *sums.pop((0, 0))]

    def sum_rows_hi(self, part):
        p = lambda a, b: part(self.at(a, b))
        if self.lo != 2:
            return (yield from self.sum_rows(part))
        one, own = yield self.hi_shift(p(3, 1)), self.lo_shift(p(0, 1))
        one, two = yield self.lo_shift(add(p(2, 1), one)), self.hi_shift(p(3, 0))
        one, two = yield self.hi_shift(add(p(2, 0), one, two)), self.lo_shift(p(1, 1))
        one = yield self.hi_shift(add(p(1, 0), one, two))
        return [p(0, 0), own, one]

    def ring(self, parts, shift):
        acc = parts[-1]
        for b in range(len(parts) - 2, -1, -1):
            acc = yield shift(acc)
            if b:
                acc = add(parts[b], acc)
        return [parts[0], acc]

    def pieces(self, value):
        out, (near, passing) = [value], (yield self.core_shift(value), self.x_shift(value))
        out.append(near)
        for step in range(1, self.xs):
            if step < self.xs - 1:
                near, ahead = yield self.core_shift(passing), self.x_shift(passing)
            else:
                near, ahead = (yield self.core_shift(passing)), None
            out += [passing, near]
            passing = ahead
        return out

    def direct(self, parts):
        got = yield [self.hi_shift(parts[b], b) for b in range(1, self.hi)]
        return [parts[0], *got]

    def over_lo(self, parts):
        acc = yield from self.ring(parts, self.lo_shift)
        return [add(*[v[b] for v in acc]) for b in range(self.hi)]

    def over_lo_hi(self, parts):
        parts = yield from self.over_lo(parts)
        return total(*(yield from self.ring(parts, self.hi_shift)))

    def over_hi(self, chunks):
        parts = [jnp.concatenate(rows, axis=1) for rows in zip(*chunks)]
        acc = yield from self.direct(parts)
        ends = np.cumsum([chunk[0].shape[1] for chunk in chunks])
        return [total(*[v[:, b - c[0].shape[1] : b] for v in acc]) for b, c in zip(ends, chunks)]

    def expert_tree(self, near, far, sizes, known):
        got = yield self.core_shift(far)
        out, at = [], 0
        for c, size in enumerate(sizes):
            cut = slice(at, at + size)
            at += size
            if c == len(sizes) - 1:
                near, got = yield near, got
            acc = add(near[self.xs - 1, cut], got[self.xs - 1, cut])
            for b in range(self.xs - 2, -1, -1):
                acc, near, got = yield self.x_shift(acc), near, got
                if b:
                    acc = add(near[b, cut], got[b, cut], acc)
            out.append(acc)
            known.append((near, got, tuple(out)))
        return known[-1]


def gather_kernel(count, cap, base_ref, *refs):
    hidden, grads, (xs, gs, slots) = refs[:count], refs[count : 2 * count], refs[2 * count :]
    step, seq_rows = slots.shape[1:]
    first = base_ref[0] + 1 + pl.program_id(0) * step
    ids = (first + lax.broadcasted_iota(jnp.int32, (step, seq_rows), 0)).astype(F32)
    before = lax.broadcasted_iota(jnp.int32, (seq_rows, seq_rows), 0)
    after = lax.broadcasted_iota(jnp.int32, (seq_rows, seq_rows), 1)
    earlier = (before < after).astype(F32).astype(BF)
    place = lax.broadcasted_iota(jnp.int32, (step, cap, seq_rows), 1).astype(F32)
    for i in range(count):
        digits = hidden[i][seq_rows:, : 2 * seq_rows].astype(F32)
        picks = digits[:, :seq_rows] * 16.0 + digits[:, seq_rows:]
        member = picks[0:1, :] == ids
        for k in range(1, picks.shape[0]):
            member = member | (picks[k : k + 1, :] == ids)
        slot = jnp.where(member, dot(member.astype(F32).astype(BF), earlier), -1.0)
        slots[i] = slot
        pick = (slot[:, None, :] == place).astype(F32).astype(BF).reshape(step * cap, seq_rows)
        for source, out in ((hidden[i], xs), (grads[i], gs)):
            got = dot(pick, source[:seq_rows, :])
            out[:, i * cap : (i + 1) * cap, :] = got.astype(BF).reshape(step, cap, got.shape[1])


def gather_call(base, hidden, grads, experts, cap):
    count = len(hidden)
    seq_rows, width = grads[0].shape
    rows = jax.ShapeDtypeStruct((experts, count * cap, width), BF)
    row_spec = pl.BlockSpec((8, count * cap, width), lambda i, _: (i, 0, 0))
    whole = lambda v: pl.BlockSpec(v.shape, lambda i, _: (0, 0))
    return pl.pallas_call(
        functools.partial(gather_kernel, count, cap),
        grid_spec=pltpu.PrefetchScalarGridSpec(
            num_scalar_prefetch=1,
            grid=(experts // 8,),
            in_specs=[whole(v) for v in (*hidden, *grads)],
            out_specs=[
                row_spec,
                row_spec,
                pl.BlockSpec((count, 8, seq_rows), lambda i, _: (0, i, 0)),
            ],
        ),
        out_shape=[rows, rows, jax.ShapeDtypeStruct((count, experts, seq_rows), F32)],
        compiler_params=pltpu.CompilerParams(vmem_limit_bytes=VMEM_LIMIT),
        cost_estimate=pl.CostEstimate(
            flops=4 * count * experts * cap * seq_rows * width,
            bytes_accessed=4 * experts * count * cap * width,
            transcendentals=0,
        ),
        name="gather_rows",
    )(base, *hidden, *grads)


def expert_kernel(n, groups, cap, many, at_ref, *refs):
    xs_in, gs_in = refs[: n[0]], refs[n[0] : sum(n)]
    up, down, router = refs[sum(n) : sum(n) + 3]
    slots = refs[sum(n) + 3 : sum(n) + 3 + n[0]]
    outs = refs[sum(n) + 3 + n[0] :]
    moe = outs[:groups]
    dhid = outs[groups : 2 * groups]
    near, far, grt = outs[2 * groups : 2 * groups + 3]
    xs, gs, w, d2, gacc, dr = outs[2 * groups + 3 :]
    step = pl.program_id(0)
    ff = up.shape[2]

    @pl.when(step == 0)
    def _():
        for k in range(many):
            w[k, :, ff:] = router[...]
        grt[...] = jnp.zeros_like(grt)

    for k in range(many):
        for whole, pieces in ((xs, xs_in), (gs, gs_in)):
            at = 0
            for piece in pieces:
                whole[k, at : at + piece.shape[1], :] = piece[k]
                at += piece.shape[1]
        w[k, :, :ff] = up[k]
    both = [jnp.dot(xs[k], w[k], preferred_element_type=F32) for k in range(many)]
    us = [jnp.dot(gs[k], down[k], preferred_element_type=F32) for k in range(many)]
    scaled = []
    for k in range(many):
        pre, u = both[k][:, :ff], us[k]
        sel = lax.broadcasted_iota(jnp.int32, pre.shape, 1) == step * many + k
        logit = jnp.sum(jnp.where(sel, both[k][:, ff:], 0.0), axis=1, keepdims=True)
        chosen = jax.nn.sigmoid(logit)
        square = pre * pre
        t = jnp.tanh(GELU_C * (pre + GELU_K * (square * pre)))
        half = 0.5 * (1.0 + t)
        act = (half * pre).astype(BF)
        slope = half + 0.5 * pre * (1.0 - t * t) * (GELU_C * (1.0 + 3.0 * GELU_K * square))
        act32 = act.astype(F32)
        dchosen = jnp.sum(u * act32, axis=1, keepdims=True)
        drl = dchosen * chosen * (1.0 - chosen)
        scaled.append((chosen * act32).astype(BF))
        d2[k, :, :ff] = (chosen * u * slope).astype(BF)
        d2[k, :, ff:] = jnp.where(sel, drl, 0.0).astype(BF)
    for k in range(many):
        dgot = lax.dot_general(
            d2[k], w[k], (((1,), (1,)), ((), ())), preferred_element_type=F32
        ).astype(BF)
        got = lax.dot_general(
            scaled[k], down[k], (((1,), (1,)), ((), ())), preferred_element_type=F32
        ).astype(BF)
        at = pl.multiple_of((step * many + k) * cap, cap)
        for s in range(groups):
            moe[s][k] = got[s * cap : (s + 1) * cap]
            dr[s, pl.ds(at, cap), :] = dgot[s * cap : (s + 1) * cap]
    x_size, _, _, _, lanes = near.shape
    for k in range(many):
        gu = lax.dot_general(d2[k], xs[k], (((0,), (0,)), ((), ())), preferred_element_type=F32)
        gacc[k, 0] = gu[:ff]
        grt[...] += gu[ff : ff + grt.shape[0]]
        gacc[k, 1] = lax.dot_general(
            scaled[k], gs[k], (((0,), (0,)), ((), ())), preferred_element_type=F32
        )
        for xr in range(x_size):
            base = lax.rem(at_ref[1] + xr, x_size) * 2
            for cr, out in enumerate((near, far)):
                cut = pl.multiple_of((base + lax.rem(at_ref[0] + cr, 2)) * lanes, lanes)
                for i in range(2):
                    out[xr, k, i] = gacc[k, i, :, pl.ds(cut, lanes)].astype(BF)

    @pl.when(step == pl.num_programs(0) - 1)
    def _():
        experts = slots[0].shape[1]
        spread = slot_spread(experts, cap)
        source = 0
        for group in slots:
            for i in range(group.shape[0]):
                put = slot_picks(group[i], spread, cap)
                dhid[source][...] = dot(put, dr[source]).astype(BF)
                source += 1


def slot_spread(experts, cap):
    rowi = lax.broadcasted_iota(jnp.int32, (experts, experts * cap), 0)
    coli = lax.broadcasted_iota(jnp.int32, (experts, experts * cap), 1)
    return (coli // cap == rowi).astype(F32).astype(BF)


def slot_picks(slot, spread, cap):
    wide = dot_tn(slot.astype(BF), spread)
    lane = lax.broadcasted_iota(jnp.int32, wide.shape, 1) % cap
    return (wide == lane.astype(F32)).astype(F32).astype(BF)


def expert_call(coords, x_size, groups, xs, gs, up, down, router, slots, cap, many=2):
    experts, width, ff = up.shape
    rows = groups * cap
    pad = -(-experts // 8) * 8
    seq_rows = slots[0].shape[2]
    lanes = width // (2 * x_size)
    row_specs = [
        pl.BlockSpec((many, v.shape[1], width), lambda e, _: (e, 0, 0)) for v in (*xs, *gs)
    ]
    w_spec = pl.BlockSpec((many, width, ff), lambda e, _: (e, 0, 0))
    whole = lambda *shape: pl.BlockSpec(shape, lambda e, _: (0,) * len(shape))
    g_spec = pl.BlockSpec((x_size, many, 2, ff, lanes), lambda e, _: (0, e, 0, 0, 0))
    s_spec = pl.BlockSpec((many, cap, width), lambda e, _: (e, 0, 0))
    one = jax.ShapeDtypeStruct((experts, cap, width), BF)
    outs = pl.pallas_call(
        functools.partial(expert_kernel, (len(xs), len(gs)), groups, cap, many),
        grid_spec=pltpu.PrefetchScalarGridSpec(
            num_scalar_prefetch=1,
            grid=(experts // many,),
            in_specs=[*row_specs, w_spec, w_spec, whole(width, ff)] + [whole(*v.shape) for v in slots],
            out_specs=[s_spec] * groups
            + [whole(seq_rows, width)] * groups
            + [g_spec, g_spec, whole(pad, width)],
            scratch_shapes=[
                pltpu.VMEM((many, rows, width), BF),
                pltpu.VMEM((many, rows, width), BF),
                pltpu.VMEM((many, width, 2 * ff), BF),
                pltpu.VMEM((many, rows, 2 * ff), BF),
                pltpu.VMEM((many, 2, ff, width), F32),
                pltpu.VMEM((groups, experts * cap, width), BF),
            ],
        ),
        out_shape=[one] * groups
        + [jax.ShapeDtypeStruct((seq_rows, width), BF)] * groups
        + [jax.ShapeDtypeStruct((x_size, experts, 2, ff, lanes), BF)] * 2
        + [jax.ShapeDtypeStruct((pad, width), F32)],
        compiler_params=pltpu.CompilerParams(vmem_limit_bytes=VMEM_LIMIT),
        cost_estimate=pl.CostEstimate(
            flops=experts * rows * width * ff * 2 * 8,
            bytes_accessed=experts * rows * width * 8,
            transcendentals=0,
        ),
        name="experts",
    )(coords, *xs, *gs, up, down, router, *slots)
    return outs[:groups], outs[groups : 2 * groups], outs[-3], outs[-2], outs[-1]


def finish_kernel(starts, near, got, *refs):
    accs, (up, down) = refs[: len(starts) - 1], refs[-2:]
    step = pl.program_id(0)
    for acc, first, after in zip(accs, starts, starts[1:]):

        @pl.when((step >= first) & (step < after))
        def _(acc=acc):
            for k in range(acc.shape[0]):
                for i, out in enumerate((up, down)):
                    out[k] = jnp.transpose(
                        near[0, k, i].astype(F32) + got[0, k, i].astype(F32) + acc[k, i].astype(F32)
                    )


def finish_call(near, got, accs, skip=0, known=()):
    _, experts, _, ff, lanes = near.shape
    each = accs[0].shape[0]
    starts = [sum(v.shape[0] for v in accs[:i]) // each for i in range(skip, len(accs) + 1)]
    before = starts[0]
    mine = pl.BlockSpec((1, each, 2, ff, lanes), lambda c: (0, c + before, 0, 0, 0))
    out = pl.BlockSpec((each, lanes, ff), lambda c: (c + before, 0, 0))
    starts = [v - before for v in starts]
    accs = accs[skip:]

    def acc_spec(first, after):
        return pl.BlockSpec(
            (each, 2, ff, lanes), lambda c: (jnp.clip(c - first, 0, after - first - 1), 0, 0, 0)
        )

    return pl.pallas_call(
        functools.partial(finish_kernel, starts),
        grid=(starts[-1],),
        in_specs=[mine, mine]
        + [acc_spec(*pair) for pair in zip(starts, starts[1:])]
        + [pl.BlockSpec(memory_space=pl.ANY)] * len(known),
        out_specs=[out, out],
        out_shape=[jax.ShapeDtypeStruct((experts, lanes, ff), F32)] * 2,
        input_output_aliases={2 + len(accs) + i: i for i in range(len(known))},
        compiler_params=pltpu.CompilerParams(vmem_limit_bytes=VMEM_LIMIT),
        cost_estimate=pl.CostEstimate(
            flops=0, bytes_accessed=20 * experts * lanes * ff, transcendentals=0
        ),
        name="expert_grads",
    )(near, got, *accs, *known)


def scatter_kernel(places, *refs):
    count = len(places)
    rows, slots, outs = refs[:count], refs[count : 2 * count], refs[2 * count :]
    experts, cap, width = rows[0].shape
    spread = slot_spread(experts, cap)
    for s in range(count):
        put = slot_picks(slots[s][places[s]], spread, cap)
        outs[s][...] = dot(put, rows[s][...].reshape(experts * cap, width)).astype(BF)


def scatter_call(rows, slots):
    count = len(rows)
    experts, cap, width = rows[0].shape
    seq_rows = slots[0][0].shape[2]
    return pl.pallas_call(
        functools.partial(scatter_kernel, tuple(j for _, j in slots)),
        out_shape=[jax.ShapeDtypeStruct((seq_rows, width), BF)] * count,
        compiler_params=pltpu.CompilerParams(vmem_limit_bytes=VMEM_LIMIT),
        cost_estimate=pl.CostEstimate(
            flops=2 * count * seq_rows * experts * cap * width,
            bytes_accessed=2 * count * experts * cap * width,
            transcendentals=0,
        ),
        name="scatter_rows",
    )(*rows, *[v for v, _ in slots])


def put_rows(res, outs, sizes, rows, at_ref):
    lo, hi = sizes
    for lr in range(lo):
        l = lax.rem(at_ref[2] + lr, lo)
        for hr in range(hi):
            h = lax.rem(at_ref[3] + hr, hi)
            start = pl.multiple_of((h * lo + l) * rows, rows)
            outs[lr][hr] = res[pl.ds(start, rows), :].astype(BF)


def gate_widener(at):
    shape = (128, AEXP * HEAD)
    row = lax.broadcasted_iota(jnp.int32, shape, 0)
    want = at + lax.broadcasted_iota(jnp.int32, shape, 1) // HEAD
    return ((row == want) | (row == want + 2 * HEADS * AEXP)).astype(F32).astype(BF)


def gated_kernel(count, sizes, rows, gate_at, at_ref, left, *refs):
    bases, gates, outs, (right, res) = refs[:count], refs[count : 2 * count], refs[2 * count : -2], refs[-2:]
    seq_rows = bases[0].shape[0]
    widen = gate_widener(gate_at + pl.program_id(0) * AEXP)
    for p in range(count):
        base, wide = bases[p][...].astype(F32), dot(gates[p][...], widen)
        for e in range(AEXP):
            cut = slice(e * HEAD, (e + 1) * HEAD)
            right[p * seq_rows : (p + 1) * seq_rows, cut] = (wide[:, cut] * base).astype(BF)
    res[...] = dot(left[...], right[...])
    put_rows(res, outs, sizes, rows, at_ref)


def gated_call(coords, grid, left, bases, base_at, packs, gate_at):
    width, tokens = left.shape
    seq_rows = bases[0].shape[0]
    sizes = (grid.lo, grid.hi)
    rows = width // (grid.lo * grid.hi)
    tile = AEXP * HEAD
    count = len(bases)
    out = (grid.hi, rows, HEADS * tile)
    return pl.pallas_call(
        functools.partial(gated_kernel, count, sizes, rows, gate_at),
        grid_spec=pltpu.PrefetchScalarGridSpec(
            num_scalar_prefetch=1,
            grid=(HEADS,),
            in_specs=[whole_spec(width, tokens)]
            + [pl.BlockSpec((seq_rows, HEAD), lambda h, _: (0, base_at // HEAD + h))] * count
            + [pl.BlockSpec((seq_rows, 128), lambda h, _: (0, HEADS))] * count,
            out_specs=[pl.BlockSpec((grid.hi, rows, tile), lambda h, _: (0, 0, h))] * grid.lo,
            scratch_shapes=[pltpu.VMEM((tokens, tile), BF), pltpu.VMEM((width, tile), F32)],
        ),
        out_shape=[jax.ShapeDtypeStruct(out, BF)] * grid.lo,
        compiler_params=pltpu.CompilerParams(vmem_limit_bytes=VMEM_LIMIT),
        cost_estimate=pl.CostEstimate(
            flops=2 * width * tokens * HEADS * tile,
            bytes_accessed=2 * width * HEADS * tile,
            transcendentals=0,
        ),
        name="gated_grad",
    )(coords, left, *bases, *packs)


def plain_kernel(count, sizes, rows, at_ref, left, last_left, extra, *refs):
    factors, outs, (right, res) = refs[:count], refs[count:-2], refs[-2:]
    step, last = pl.program_id(0), pl.num_programs(0) - 1
    seq_rows = factors[0].shape[0]
    for p in range(count):
        right[p * seq_rows : (p + 1) * seq_rows, :] = factors[p][...]

    @pl.when(step < last)
    def _():
        res[...] = dot(left[...], right[...])

    @pl.when(step == last)
    def _():
        width = res.shape[0]
        mine = pl.ds(pl.multiple_of((at_ref[1] * 2 + at_ref[0]) * width, width), width)
        res[...] = dot(last_left[...], right[...]) + jnp.transpose(extra[:, mine])

    put_rows(res, outs, sizes, rows, at_ref)


def plain_call(coords, grid, left, last_left, extra, factors, cols):
    width, tokens = left.shape
    seq_rows = factors[0].shape[0]
    tile = extra.shape[0]
    sizes = (grid.lo, grid.hi)
    rows = width // (grid.lo * grid.hi)
    count = len(factors)
    return pl.pallas_call(
        functools.partial(plain_kernel, count, sizes, rows),
        grid_spec=pltpu.PrefetchScalarGridSpec(
            num_scalar_prefetch=1,
            grid=(cols // tile,),
            in_specs=[
                whole_spec(width, tokens),
                whole_spec(width, tokens),
                whole_spec(*extra.shape),
            ]
            + [head_spec(seq_rows, tile)] * count,
            out_specs=[pl.BlockSpec((grid.hi, rows, tile), lambda j, _: (0, 0, j))] * grid.lo,
            scratch_shapes=[pltpu.VMEM((tokens, tile), BF), pltpu.VMEM((width, tile), F32)],
        ),
        out_shape=[jax.ShapeDtypeStruct((grid.hi, rows, cols), BF)] * grid.lo,
        compiler_params=pltpu.CompilerParams(vmem_limit_bytes=VMEM_LIMIT),
        cost_estimate=pl.CostEstimate(
            flops=2 * width * tokens * cols, bytes_accessed=2 * width * cols, transcendentals=0
        ),
        name="plain_grad",
    )(coords, left, last_left, extra, *factors)


def turn_kernel(count, at_ref, *refs):
    for n in range(len(refs) * count // (count + 1)):
        seq_rows, out = refs[n].shape[0], refs[len(refs) * count // (count + 1) + n // count]
        each = out.shape[0]
        mine = pl.ds(pl.multiple_of((at_ref[1] * 2 + at_ref[0]) * each, each), each)
        at = n % count * seq_rows
        out[:, at : at + seq_rows] = jnp.transpose(refs[n][:, mine])


def turn_call(coords, grid, groups):
    seq_rows, width = groups[0][0].shape
    count = len(groups[0])
    vmem = pl.BlockSpec(memory_space=pltpu.VMEM)
    return pl.pallas_call(
        functools.partial(turn_kernel, count),
        in_specs=[pl.BlockSpec(memory_space=pltpu.SMEM)] + [vmem] * (count * len(groups)),
        out_specs=[vmem] * len(groups),
        out_shape=[jax.ShapeDtypeStruct((width // grid.dp, count * seq_rows), BF)] * len(groups),
        compiler_params=pltpu.CompilerParams(vmem_limit_bytes=VMEM_LIMIT),
        name="turn",
    )(coords, *[v for group in groups for v in group])


NT = (((1,), (1,)), ((), ()))
TN = (((0,), (0,)), ((), ()))


def dot_nt(a, b):
    return lax.dot_general(a, b, NT, preferred_element_type=F32)


def dot_tn(a, b):
    return lax.dot_general(a, b, TN, preferred_element_type=F32)


def dot(a, b):
    return jnp.dot(a, b, preferred_element_type=F32)


def pick_mask(choice):
    picks = choice.shape[0]
    row = lax.broadcasted_iota(jnp.int32, (picks, HEADS * AEXP), 0)
    head = lax.broadcasted_iota(jnp.int32, (picks, HEADS * AEXP), 1) // AEXP
    low = choice.astype(F32).astype(BF)
    first = dot_tn(low, (row == head).astype(F32).astype(BF))
    second = dot_tn(low, (row == HEADS + head).astype(F32).astype(BF))
    expert = (lax.broadcasted_iota(jnp.int32, first.shape, 1) % AEXP).astype(F32)
    return ((first == expert) | (second == expert)).astype(F32)


def normalize(x):
    mean = jnp.mean(x, axis=1, keepdims=True)
    centered = x - mean
    inverse = lax.rsqrt(jnp.mean(centered * centered, axis=1, keepdims=True) + 1e-05)
    return centered * inverse, inverse


def probabilities(q, k, length):
    scores = dot_nt(q, k) * (1.0 / math.sqrt(HEAD))
    row = lax.broadcasted_iota(jnp.int32, scores.shape, 0)
    col = lax.broadcasted_iota(jnp.int32, scores.shape, 1)
    scores = jnp.where((col <= row) & (col < length), scores, -1e30)
    expo = jnp.exp(scores - jnp.max(scores, axis=1, keepdims=True))
    return expo / jnp.sum(expo, axis=1, keepdims=True)


def forward_head(
    h, length, tokens, normed, cos, sin, wq, wk, wv, wo, gates,
    q_out, k_out, mixed_out, vals_out, att_out, expanded,
):
    q = dot(normed[...], wq[...])
    k = dot(normed[...], wk[...])
    q = (q * cos[...] + pltpu.roll(q, HEAD // 2, 1) * sin[...]).astype(BF)
    k = (k * cos[...] + pltpu.roll(k, HEAD // 2, 1) * sin[...]).astype(BF)
    q_out[...] = q
    k_out[...] = k
    vals = dot(tokens[...], wv[...])
    vals_out[...] = vals
    mixed = jnp.zeros_like(q, F32)
    wide = dot(gates[...], gate_widener(h * AEXP))
    for e in range(AEXP):
        cut = slice(e * HEAD, (e + 1) * HEAD)
        mixed += wide[:, cut] * vals[:, cut]
    mixed = mixed.astype(BF)
    mixed_out[...] = mixed
    probs = probabilities(q, k, length).astype(BF)
    att = dot(probs, mixed)
    att_out[...] = att
    wide = dot(gates[...], gate_widener((HEADS + h) * AEXP))
    for e in range(AEXP):
        cut = slice(e * HEAD, (e + 1) * HEAD)
        expanded[:, cut] = (wide[:, cut] * att).astype(BF)
    return dot_nt(expanded[...], wo[...])


def first_heads_kernel(
    length_ref, tokens, cos, sin, wq, wk, wv, wo, gain, vr, orr, vc, oc,
    acc, q_out, k_out, mixed_out, vals_out, att_out, normed, gates, slopes, expanded,
):
    @pl.when(pl.program_id(0) == 0)
    def _():
        scaled, _ = normalize(tokens[...].astype(F32))
        normed[...] = (scaled * gain[...]).astype(BF)
        gates[...] = jnp.zeros_like(gates)
        slopes[...] = jnp.zeros_like(slopes)
        for n, (router, choice) in enumerate(((vr, vc), (orr, oc))):
            sig, mask = jax.nn.sigmoid(dot_nt(tokens[...], router[...])), pick_mask(choice[...])
            high = (sig * mask).astype(BF)
            many = HEADS * AEXP
            gates[:, n * many : (n + 1) * many] = high
            gates[:, (n + 2) * many : (n + 3) * many] = (sig * mask - high.astype(F32)).astype(BF)
            slopes[:, n * many : (n + 1) * many] = mask * sig * (1.0 - sig)
        acc[...] = tokens[...].astype(F32)

    acc[...] += forward_head(
        pl.program_id(0), length_ref[0], tokens, normed, cos, sin, wq, wk, wv, wo,
        gates,
        q_out, k_out, mixed_out, vals_out, att_out, expanded,
    )


def last_heads_kernel(start, *refs):
    length_ref, tokens, cos, sin, wq, wk, wv, wo, normed, gates, codes, acc, known_att = refs[:13]
    hidden, q_out, k_out, mixed_out, vals_out, att_out, hidden_low, pack, expanded = refs[-9:]

    @pl.when(pl.program_id(0) == 0)
    def _():
        hidden[...] = acc[...]

    hidden[...] += forward_head(
        start + pl.program_id(0), length_ref[0], tokens, normed, cos, sin, wq, wk, wv, wo,
        gates,
        q_out, k_out, mixed_out, vals_out, att_out, expanded,
    )

    at = (start + pl.program_id(0)) * HEAD
    pack[:, pl.ds(pl.multiple_of(at, HEAD), HEAD)] = att_out[...].astype(BF)

    @pl.when(pl.program_id(0) == 0)
    def _():
        pack[:, : start * HEAD] = known_att[...].astype(BF)
        pack[:, HEADS * HEAD :] = gates[...]

    @pl.when(pl.program_id(0) == pl.num_programs(0) - 1)
    def _():
        rows = hidden.shape[0]
        hidden_low[:rows, :] = hidden[...].astype(BF)
        code = codes[...]
        high = lax.shift_right_logical(code, 4)
        hidden_low[rows:, :rows] = high.astype(F32).astype(BF)
        hidden_low[rows:, rows : 2 * rows] = (code - high * 16).astype(F32).astype(BF)
        hidden_low[rows:, 2 * rows :] = jnp.zeros((code.shape[0], hidden_low.shape[1] - 2 * rows), BF)


def whole_spec(*shape):
    return pl.BlockSpec(shape, lambda h, _: (0,) * len(shape))


def head_spec(rows, cols):
    return pl.BlockSpec((rows, cols), lambda h, _: (0, h))


def heads_common(rows, width, start):
    many = AEXP * HEAD
    head = lambda rows, cols: pl.BlockSpec((rows, cols), lambda h, _: (0, h + start))
    shape = lambda cols, kind: jax.ShapeDtypeStruct((rows, cols), kind)
    in_specs = [
        whole_spec(rows, width),
        whole_spec(rows, HEAD),
        whole_spec(rows, HEAD),
        head(width, HEAD),
        head(width, HEAD),
        head(width, many),
        head(width, many),
    ]
    out_specs = [whole_spec(rows, width)] + [head(rows, HEAD)] * 3
    out_specs += [head(rows, many), head(rows, HEAD)]
    out_shape = [shape(width, F32)] + [shape(HEADS * HEAD, BF)] * 3
    out_shape += [shape(HEADS * many, F32), shape(HEADS * HEAD, F32)]
    cost = pl.CostEstimate(
        flops=rows * width * HEADS * (2 * HEAD + 2 * many),
        bytes_accessed=width * HEADS * (2 * HEAD + 2 * many),
        transcendentals=0,
    )
    return in_specs, out_specs, out_shape, cost


def first_heads(lengths, tokens, cos, sin, wq, wk, wv, wo, gain, vr, orr, vc, oc):
    rows, width = tokens.shape
    in_specs, out_specs, out_shape, cost = heads_common(rows, width, 0)
    return pl.pallas_call(
        first_heads_kernel,
        grid_spec=pltpu.PrefetchScalarGridSpec(
            num_scalar_prefetch=1,
            grid=(HEADS // 2,),
            in_specs=in_specs + [whole_spec(*v.shape) for v in (gain, vr, orr, vc, oc)],
            out_specs=out_specs + [whole_spec(rows, width)] + [whole_spec(rows, 128)] * 2,
            scratch_shapes=[pltpu.VMEM((rows, AEXP * HEAD), BF)],
        ),
        out_shape=out_shape
        + [jax.ShapeDtypeStruct((rows, width), BF)]
        + [jax.ShapeDtypeStruct((rows, 128), kind) for kind in (BF, F32)],
        compiler_params=pltpu.CompilerParams(vmem_limit_bytes=VMEM_LIMIT),
        cost_estimate=cost,
        name="attention_forward",
    )(lengths, tokens, cos, sin, wq, wk, wv, wo, gain, vr, orr, vc, oc)


def last_heads(lengths, tokens, cos, sin, wq, wk, wv, wo, normed, gates, codes, acc, known):
    rows, width = tokens.shape
    start = HEADS // 2
    in_specs, out_specs, out_shape, cost = heads_common(rows, width, start)
    operands = [lengths, tokens, cos, sin, wq, wk, wv, wo, normed, gates, codes, acc]
    in_specs += [whole_spec(*v.shape) for v in operands[8:]]
    operands.append(known[-1])
    in_specs.append(whole_spec(rows, start * HEAD))
    low = (rows + codes.shape[0], width)
    packed = (rows, HEADS * HEAD + 128)
    return pl.pallas_call(
        functools.partial(last_heads_kernel, start),
        grid_spec=pltpu.PrefetchScalarGridSpec(
            num_scalar_prefetch=1,
            grid=(HEADS - start,),
            in_specs=in_specs + [pl.BlockSpec(memory_space=pl.ANY)] * len(known),
            out_specs=out_specs + [whole_spec(*low), whole_spec(*packed)],
            scratch_shapes=[pltpu.VMEM((rows, AEXP * HEAD), BF)],
        ),
        out_shape=out_shape + [jax.ShapeDtypeStruct(low, BF), jax.ShapeDtypeStruct(packed, BF)],
        input_output_aliases={len(operands) + i: 1 + i for i in range(len(known))},
        compiler_params=pltpu.CompilerParams(vmem_limit_bytes=VMEM_LIMIT),
        cost_estimate=cost,
        name="attention_forward_rest",
    )(*operands, *known)


def backward_kernel(
    length_ref, cos, sin, wo, q_in, k_in, mixed_in, vals, att, gates, slopes, dbranch,
    factors, mixes, dvals, dl,
):
    h = pl.program_id(0)
    logit_at = 2 * HEADS * HEAD

    @pl.when(h == 0)
    def _():
        dl[...] = jnp.zeros_like(dl)
        factors[:, logit_at:] = jnp.zeros((dl.shape[0], factors.shape[1] - logit_at), BF)

    lane = lax.broadcasted_iota(jnp.int32, dl.shape, 1)
    scale = 1.0 / math.sqrt(HEAD)
    dexp = dot(dbranch[...], wo[...])
    datt = jnp.zeros_like(att)
    wide = dot(gates[...], gate_widener((HEADS + h) * AEXP))
    sums = jnp.zeros_like(dl)
    for e in range(AEXP):
        part = dexp[:, e * HEAD : (e + 1) * HEAD]
        datt += wide[:, e * HEAD : (e + 1) * HEAD] * part
        logit = jnp.sum(part * att[...], axis=1, keepdims=True)
        sums = jnp.where(lane == (HEADS + h) * AEXP + e, logit, sums)
    datt = datt.astype(BF)
    q, k, mixed = q_in[...], k_in[...], mixed_in[...]
    probs = probabilities(q, k, length_ref[0])
    dp = dot_nt(datt, mixed)
    inner = jnp.sum(probs * dp, axis=1, keepdims=True)
    dscore = (probs * (dp - inner)).astype(BF)
    dq = dot(dscore, k) * scale
    dk = dot_tn(dscore, q) * scale
    dmixed = dot_tn(probs.astype(BF), datt)
    dq = (dq * cos[...] - pltpu.roll(dq, HEAD // 2, 1) * sin[...]).astype(BF)
    dk = (dk * cos[...] - pltpu.roll(dk, HEAD // 2, 1) * sin[...]).astype(BF)
    put = lambda at, value: factors.__setitem__(
        (slice(None), pl.ds(pl.multiple_of(at, HEAD), HEAD)), value
    )
    put(h * 2 * HEAD, dq)
    put(h * 2 * HEAD + HEAD, dk)
    mixes[...] = dmixed.astype(BF)
    wide = dot(gates[...], gate_widener(h * AEXP))
    for e in range(AEXP):
        part = vals[:, e * HEAD : (e + 1) * HEAD]
        dvals[:, e * HEAD : (e + 1) * HEAD] = (wide[:, e * HEAD : (e + 1) * HEAD] * dmixed).astype(BF)
        logit = jnp.sum(part * dmixed, axis=1, keepdims=True)
        sums = jnp.where(lane == h * AEXP + e, logit, sums)
    dl[...] += sums * slopes[...]

    @pl.when(h == pl.num_programs(0) - 1)
    def _():
        factors[:, logit_at : logit_at + dl.shape[1]] = dl[...].astype(BF)


def backward_call(small, lengths, dbranch, cos, sin, wo, q, k, mixed, vals, att, gates, slopes):
    rows, width = dbranch.shape
    many = AEXP * HEAD
    cols = HEADS * 2 * HEAD + small
    return pl.pallas_call(
        backward_kernel,
        grid_spec=pltpu.PrefetchScalarGridSpec(
            num_scalar_prefetch=1,
            grid=(HEADS,),
            in_specs=[
                whole_spec(rows, HEAD),
                whole_spec(rows, HEAD),
                head_spec(width, many),
                head_spec(rows, HEAD),
                head_spec(rows, HEAD),
                head_spec(rows, HEAD),
                head_spec(rows, many),
                head_spec(rows, HEAD),
            ]
            + [whole_spec(rows, 128)] * 2
            + [whole_spec(rows, width)],
            out_specs=[whole_spec(rows, cols), head_spec(rows, HEAD), head_spec(rows, many)],
            scratch_shapes=[pltpu.VMEM((rows, 128), F32)],
        ),
        out_shape=[
            jax.ShapeDtypeStruct((rows, cols), BF),
            jax.ShapeDtypeStruct((rows, HEADS * HEAD), BF),
            jax.ShapeDtypeStruct((rows, HEADS * many), BF),
        ],
        compiler_params=pltpu.CompilerParams(vmem_limit_bytes=VMEM_LIMIT),
        cost_estimate=pl.CostEstimate(
            flops=2 * rows * width * HEADS * many * 2,
            bytes_accessed=2 * width * HEADS * many,
            transcendentals=0,
        ),
        name="attention_backward",
    )(lengths, cos, sin, wo, q, k, mixed, vals, att, gates, slopes, dbranch)


def input_kernel(tokens, gain, dhidden, factors, dvals, wq, wk, wv, vr, orr, out, dn, rest):
    h = pl.program_id(0)
    logit_at = 2 * HEADS * HEAD

    @pl.when(h == 0)
    def _():
        gates = HEADS * AEXP
        dlogits = factors[:, logit_at : logit_at + 2 * gates]
        dn[...] = jnp.zeros_like(dn)
        rest[...] = (
            dhidden[...]
            + dot(dlogits[:, :gates], vr[...])
            + dot(dlogits[:, gates:], orr[...])
        )

    take = lambda at, size: factors[:, pl.ds(pl.multiple_of(at, HEAD), size)]
    dn[...] += dot_nt(take(h * 2 * HEAD, HEAD), wq[...])
    dn[...] += dot_nt(take(h * 2 * HEAD + HEAD, HEAD), wk[...])
    rest[...] += dot_nt(dvals[...], wv[...])

    @pl.when(h == pl.num_programs(0) - 1)
    def _():
        scaled, inverse = normalize(tokens[...].astype(F32))
        dscaled = dn[...] * gain[...]
        inside = (
            dscaled
            - jnp.mean(dscaled, axis=1, keepdims=True)
            - scaled * jnp.mean(dscaled * scaled, axis=1, keepdims=True)
        )
        out[...] = (rest[...] + inverse * inside).astype(BF)


def input_call(tokens, gain, dhidden, factors, dvals, wq, wk, wv, vr, orr):
    rows, width = tokens.shape
    many = AEXP * HEAD
    whole = lambda *shape: pl.BlockSpec(shape, lambda h: (0,) * len(shape))
    head = lambda *shape: pl.BlockSpec(shape, lambda h: (0, h))
    return pl.pallas_call(
        input_kernel,
        grid=(HEADS,),
        in_specs=[
            whole(rows, width),
            whole(1, width),
            whole(rows, width),
            whole(*factors.shape),
            head(rows, many),
            head(width, HEAD),
            head(width, HEAD),
            head(width, many),
            whole(HEADS * AEXP, width),
            whole(HEADS * AEXP, width),
        ],
        out_specs=whole(rows, width),
        out_shape=jax.ShapeDtypeStruct((rows, width), BF),
        scratch_shapes=[pltpu.VMEM((rows, width), F32)] * 2,
        compiler_params=pltpu.CompilerParams(vmem_limit_bytes=VMEM_LIMIT),
        cost_estimate=pl.CostEstimate(
            flops=2 * rows * width * HEADS * (many + 2 * HEAD),
            bytes_accessed=2 * width * HEADS * (many + 2 * HEAD),
            transcendentals=0,
        ),
        name="input_grad",
    )(tokens, gain, dhidden, factors, dvals, wq, wk, wv, vr, orr)


def shards(
    tokens,
    norm_gain,
    query_weight,
    key_weight,
    value_weight,
    output_weight,
    value_router,
    output_router,
    expert_router,
    expert_up,
    expert_down,
    lengths,
    value_choice,
    output_choice,
    expert_choice,
    running_counts,
    cotangent,
):
    seq_rows, model_width = tokens.shape
    groups = lax.axis_size("expert")
    grid = Grid(lax.axis_size("dp"), groups)
    coords = grid.coords()
    me = lax.axis_index("expert")
    local_experts, _, ff = expert_up.shape
    experts_all = local_experts * groups
    picks_per = expert_choice.shape[1]
    cap = 3 * seq_rows * picks_per // (2 * experts_all)
    position = jnp.arange(seq_rows, dtype=jnp.int32)
    seq_length = lengths[0]

    code = jnp.where((position < seq_length)[:, None], expert_choice + 1, 0)
    all_grads, all_hidden = {}, {}
    grad_ring = Task(grid.gather_rows(cotangent, all_grads, True))

    cosine, sine = rope_tables(seq_rows, HEAD)
    gain = norm_gain.reshape(1, model_width)
    vc, oc = (
        jnp.transpose(v, (2, 1, 0)).reshape(-1, seq_rows) for v in (value_choice, output_choice)
    )
    turned_routers = (jnp.transpose(value_router), jnp.transpose(output_router))
    weights = (query_weight, key_weight, value_weight, output_weight)
    tokens_task = Task(grid.pieces(tokens))
    got = first_heads(
        lengths, tokens, cosine, sine, *weights, gain, *turned_routers, vc, oc
    )
    acc, *known, normed_low, gates, slopes = end_round([grad_ring, tokens_task], got)
    normed_task = Task(grid.pieces(normed_low))
    got = last_heads(
        lengths, tokens, cosine, sine, *weights, normed_low, gates, jnp.transpose(code), acc, known
    )
    got = end_round([grad_ring, tokens_task, normed_task], got)
    hidden, query_rot, key_rot, mixed, values_all, attended, hidden_low, pack = got
    pack_task = Task(grid.pieces(pack))
    hidden_low = end_round([grad_ring, tokens_task, normed_task, pack_task], hidden_low)

    ring = Task(grid.gather_rows(hidden_low, all_hidden))
    end_round([ring, tokens_task, normed_task, pack_task])
    finish([tokens_task, normed_task, pack_task])
    turned = turn_call(coords, grid, [normed_task.result, tokens_task.result])
    packs = pack_task.result
    base = (me * local_experts).reshape(1)
    xs, gs, slots, slot_groups = [], [], {}, []

    def gather(js):
        return gather_call(
            base, [all_hidden[j] for j in js], [all_grads[j] for j in js], local_experts, cap
        )

    def keep(js, got):
        xs.append(got[0])
        gs.append(got[1])
        slot_groups.append(got[2])
        for i, j in enumerate(js):
            slots[j] = (got[2], i)

    if grid.lo == 2:
        got, turned = end_round([ring], (gather(range(3)), turned))
        keep(range(3), got)
        keep((3, 4), end_round([ring, grad_ring], gather((3, 4))))
        keep((5, 6), end_round([ring, grad_ring], gather((5, 6))))
        finish([ring, grad_ring])
        keep((7,), gather((7,)))
    else:
        finish([ring, grad_ring])
        for j in range(0, groups, 4):
            keep(range(j, j + 4), gather(range(j, j + 4)))

    router_mine = lax.dynamic_slice_in_dim(expert_router, me * local_experts, local_experts, 1)
    router_pad = jnp.pad(router_mine, ((0, 0), (0, ff - local_experts)))
    moe_rows, dhid, near, far, grad_router_t = expert_call(
        coords, grid.xs, groups, xs, gs, expert_up, expert_down, router_pad, slot_groups, cap
    )
    moe = {}

    moe = {}

    def scatter(places):
        js = [grid.at(*place) for place in places]
        moe.update(zip(js, scatter_call([moe_rows[j] for j in js], [slots[j] for j in js])))

    def moe_part(j):
        if j not in moe:
            mate = j ^ 1
            got = scatter_call([moe_rows[j], moe_rows[mate]], [slots[j], slots[mate]])
            moe[j], moe[mate] = got
        return moe[j]

    devices = grid.dp * groups
    rows_each = model_width // devices
    labels_all = jnp.arange(experts_all, dtype=jnp.int32)
    local_counts = jnp.sum(
        (code[:, :, None] == labels_all + 1).astype(jnp.int32), axis=(0, 1), dtype=jnp.int32
    )
    bits = (local_counts[None, :] >> jnp.arange(6, dtype=jnp.int32)[:, None]) & 1
    bits = bits.reshape(6, devices, experts_all // devices)
    bits = jnp.pad(bits, ((0, 0), (0, 0), (0, rows_each - experts_all // devices)))
    bits = bits.reshape(6, model_width).astype(BF)
    routers = 2 * HEADS * AEXP
    small = -(-(routers + experts_all + 6) // 256) * 256
    held = -(-(local_experts + 6) // 16) * 16
    compact = jnp.concatenate(
        [
            grad_router_t[:local_experts].astype(BF),
            jnp.pad(bits, ((0, held - local_experts - 6), (0, 0))),
        ],
        axis=0,
    )

    two = grid.lo == 2
    back = Task(grid.sum_rows_hi(lambda j: dhid[j]))
    sixth = local_experts // 6
    summed = []
    cuts = (sixth,) * 3 + (local_experts - 3 * sixth,)
    shares = Task(grid.expert_tree(near, far, cuts, summed))
    if two:
        scatter([(3, 1), (3, 0)])
        moe.update(end_round([back, shares], moe))
        scatter([(2, 1), (2, 0)])
        ready, compact = end_round([back, shares], (moe, compact))
        moe.update(ready)
        scatter([(1, 1), (1, 0)])
    small_task = Task(grid.pieces(compact))
    if two:
        moe.update(end_round([back, shares, small_task], moe))
        scatter([(0, 1), (0, 0)])
    out_ring = Task(grid.sum_rows(moe_part))
    early = 2 if two else 0
    done = finish_call(*summed[early - 1]) if early else ()
    ready, done = end_round([back, shares, small_task, out_ring], (moe, done))
    moe.update(ready)
    finish([back, small_task])
    extra = total(*small_task.result)
    extra = lax.dynamic_update_slice_in_dim(
        jnp.pad(
            extra[local_experts : local_experts + 6],
            ((routers + experts_all, small - routers - experts_all - 6), (0, 0)),
        ),
        extra[:local_experts],
        routers + me * local_experts,
        0,
    )

    dhidden = total(cotangent, *back.result)
    dbranch = dhidden.astype(BF)
    branch_task = Task(grid.pieces(dbranch))
    factors, mixes, dvalues = backward_call(
        small, lengths, dbranch, cosine, sine, output_weight, query_rot, key_rot, mixed, values_all,
        attended, gates, slopes,
    )
    factors, mixes, dvalues, extra = end_round(
        [out_ring, branch_task], (factors, mixes, dvalues, extra)
    )
    mix_task = Task(grid.pieces(mixes))
    finish([branch_task])
    factors = end_round([mix_task], factors)
    factor_task = Task(grid.pieces(factors))
    [branch_turned] = turn_call(coords, grid, [branch_task.result])
    output_parts = gated_call(coords, grid, branch_turned, packs, 0, packs, HEADS * AEXP)

    output_sum = Task(grid.over_lo_hi(output_parts))
    finish([mix_task])
    value_parts = gated_call(coords, grid, turned[1], mix_task.result, 0, packs, 0)
    value_parts = end_round([out_ring], value_parts)
    value_sum = Task(grid.over_lo(value_parts))
    end_round([factor_task, shares])
    finish([factor_task])
    qk_part = plain_call(coords, grid, *turned, extra, factor_task.result, factors.shape[1])
    qk_part, factors = end_round([out_ring, output_sum], (qk_part, factors))
    finish([out_ring])
    qk_sum = Task(grid.over_lo(qk_part))
    grad_tokens = input_call(
        tokens, gain, dhidden, factors, dvalues, query_weight, key_weight, value_weight,
        *turned_routers,
    )
    grad_tokens = end_round([output_sum], grad_tokens)
    output = (hidden + total(*out_ring.result)).astype(BF)
    output = end_round([value_sum, qk_sum, output_sum], output)
    finish([value_sum, qk_sum])
    last = Task(grid.over_hi([qk_sum.result, value_sum.result]))
    finish([shares])
    expert_grads = finish_call(*shares.result, early, done)
    expert_grads = end_round([output_sum, last], expert_grads)
    finish([output_sum, last])
    sum_qk, sum_value = last.result
    sum_output = output_sum.result
    split_at = 2 * HEADS * HEAD
    sum_qk, sum_small = sum_qk[:, :split_at], sum_qk[:, split_at:]
    qk = HEADS * HEAD
    sum_qk = jnp.swapaxes(sum_qk.reshape(rows_each, HEADS, 2, HEAD), 1, 2)
    grad_query = sum_qk[:, 0].reshape(rows_each, qk)
    grad_key = sum_qk[:, 1].reshape(rows_each, qk)
    first = (lax.axis_index("dp") * groups + me) * rows_each
    rows_of = lambda w: lax.dynamic_slice_in_dim(w, first, rows_each, 0)
    grad_gain = jnp.sum(
        grad_query * rows_of(query_weight).astype(F32) + grad_key * rows_of(key_weight).astype(F32),
        axis=1,
    ) / rows_of(norm_gain)
    half = HEADS * AEXP
    got_bits = sum_small[: experts_all // devices, routers + experts_all :][:, :6]
    got_counts = jnp.sum(got_bits * (2.0 ** jnp.arange(6, dtype=F32)), axis=1)
    counts = running_counts + got_counts.astype(jnp.int32)
    return (
        output,
        grad_tokens,
        grad_gain,
        grad_query,
        grad_key,
        sum_value,
        sum_output,
        sum_small[:, :half],
        sum_small[:, half:routers],
        sum_small[:, routers : routers + experts_all],
        *expert_grads,
        counts,
    )


def solution(mesh):
    both = ("dp", "expert")
    in_specs = (
        P(both, None),
        P(),
        P(),
        P(),
        P(),
        P(),
        P(),
        P(),
        P(),
        P("expert", None, None),
        P("expert", None, None),
        P(both),
        P(both, None, None),
        P(both, None, None),
        P(both, None),
        P(both),
        P(both, None),
    )
    out_specs = (
        P(both, None),
        P(both, None),
        P(both),
        P(both, None),
        P(both, None),
        P(both, None),
        P(both, None),
        P(both, None),
        P(both, None),
        P(both, None),
        P("expert", "dp", None),
        P("expert", "dp", None),
        P(both),
    )
    return jax.shard_map(shards, mesh=mesh, in_specs=in_specs, out_specs=out_specs, check_vma=False)
```

```python
import functools
import math

import jax
import jax.numpy as jnp
import numpy as np
from jax import lax
from jax.experimental import pallas as pl
from jax.experimental.pallas import tpu as pltpu
from jax.sharding import PartitionSpec as P

HEADS = 4
HEAD = 128
AEXP = 5
BF = jnp.bfloat16
F32 = jnp.float32
VMEM_LIMIT = 60 * 1024 * 1024
GELU_C = math.sqrt(2.0 / math.pi)
GELU_K = 0.044715


def rope_tables(seq_rows, head_width):
    half_width = head_width // 2
    ladder = np.arange(half_width, dtype=np.float32) * np.float32(2.0 / head_width)
    freqs = np.exp(np.float32(-math.log(10000.0)) * ladder)
    angles = np.arange(seq_rows, dtype=np.float32)[:, None] * freqs[None, :]
    cosine, sine = np.cos(angles), np.sin(angles)
    return np.concatenate([cosine, cosine], axis=1), np.concatenate([-sine, sine], axis=1)


class Task:
    def __init__(self, gen):
        self.gen = gen
        self.done = False
        self.result = None
        self.advance(None)

    def advance(self, value):
        try:
            self.out = self.gen.send(value)
        except StopIteration as stop:
            self.done, self.out, self.result = True, None, stop.value


def end_round(tasks, extra=()):
    tasks = [t for t in tasks if not t.done]
    got, extra = lax.optimization_barrier((tuple(t.out for t in tasks), extra))
    for task, value in zip(tasks, got):
        task.advance(value)
    return extra


def finish(tasks, extra=()):
    while any(not t.done for t in tasks):
        extra = end_round(tasks, extra)
    return extra


def total(*parts):
    return functools.reduce(lambda a, b: a + b, [p.astype(F32) for p in parts])


def add(*parts):
    return total(*parts).astype(BF)


class Grid:
    def __init__(self, dp, size):
        self.dp = dp
        self.xs = dp // 2
        self.hi = 4
        self.lo = size // 4
        self.size = size

    def coords(self):
        dp, ex = lax.axis_index("dp"), lax.axis_index("expert")
        return jnp.stack([dp % 2, dp // 2, ex % self.lo, ex // self.lo])

    def core_shift(self, x):
        return lax.ppermute(x, "dp", [(i, i ^ 1) for i in range(self.dp)])

    def x_shift(self, x):
        pairs = [(i, (i // 2 + 1) % self.xs * 2 + i % 2) for i in range(self.dp)]
        return lax.ppermute(x, "dp", pairs)

    def hi_shift(self, x, by=1):
        pairs = [
            (i, ((i // self.lo + by) % self.hi) * self.lo + i % self.lo) for i in range(self.size)
        ]
        return lax.ppermute(x, "expert", pairs)

    def lo_shift(self, x):
        pairs = [
            (i, (i // self.lo) * self.lo + (i % self.lo + 1) % self.lo) for i in range(self.size)
        ]
        return lax.ppermute(x, "expert", pairs)

    def sources(self):
        me = lax.axis_index("expert")
        h, l = me // self.lo, me % self.lo
        return [
            ((h + self.hi - dh) % self.hi) * self.lo + (l + self.lo - dl) % self.lo
            for dh in range(self.hi)
            for dl in range(self.lo)
        ]

    def gather_rows(self, block, known, last_over_hi=False):
        rows = {(0, 0): block}
        known[0] = block
        steps = self.hi + self.lo - 2
        last = (self.hi - 1, self.lo - 1)
        for step in range(steps):
            fresh = {}
            for dh in range(self.hi):
                for dl in range(self.lo):
                    if dh + dl == step + 1:
                        if dl == 0 or (last_over_hi and (dh, dl) == last):
                            fresh[(dh, dl)] = self.hi_shift(rows[(dh - 1, dl)])
                        else:
                            fresh[(dh, dl)] = self.lo_shift(rows[(dh, dl - 1)])
            got = yield fresh
            for (dh, dl), value in got.items():
                known[dh * self.lo + dl] = value
            if last_over_hi and step == steps - 2:
                got = yield got
            rows.update(got)

    def at(self, a, b):
        return ((self.hi - a) % self.hi) * self.lo + (self.lo - b) % self.lo

    def sum_rows(self, part):
        p = lambda a, b: part(self.at(a, b))
        sums = {}
        for step in range(self.hi + self.lo - 2):
            sent = {}
            for a in range(self.hi):
                for b in range(self.lo):
                    if (self.hi - 1 - a) + (self.lo - 1 - b) == step:
                        mine = add(p(a, b), *sums.pop((a, b), ()))
                        if b > 0:
                            sent[(a, b - 1, 0)] = self.lo_shift(mine)
                        else:
                            sent[(a - 1, b, 1)] = self.hi_shift(mine)
            got = yield sent
            for (a, b, _), value in got.items():
                sums.setdefault((a, b), []).append(value)
        return [p(0, 0), *sums.pop((0, 0))]

    def sum_rows_hi(self, part):
        p = lambda a, b: part(self.at(a, b))
        if self.lo != 2:
            return (yield from self.sum_rows(part))
        one, own = yield self.hi_shift(p(3, 1)), self.lo_shift(p(0, 1))
        one, two = yield self.lo_shift(add(p(2, 1), one)), self.hi_shift(p(3, 0))
        one, two = yield self.hi_shift(add(p(2, 0), one, two)), self.lo_shift(p(1, 1))
        one = yield self.hi_shift(add(p(1, 0), one, two))
        return [p(0, 0), own, one]

    def ring(self, parts, shift):
        acc = parts[-1]
        for b in range(len(parts) - 2, -1, -1):
            acc = yield shift(acc)
            if b:
                acc = add(parts[b], acc)
        return [parts[0], acc]

    def pieces(self, value):
        out, (near, passing) = [value], (yield self.core_shift(value), self.x_shift(value))
        out.append(near)
        for step in range(1, self.xs):
            if step < self.xs - 1:
                near, ahead = yield self.core_shift(passing), self.x_shift(passing)
            else:
                near, ahead = (yield self.core_shift(passing)), None
            out += [passing, near]
            passing = ahead
        return out

    def direct(self, parts):
        got = yield [self.hi_shift(parts[b], b) for b in range(1, self.hi)]
        return [parts[0], *got]

    def over_lo(self, parts):
        acc = yield from self.ring(parts, self.lo_shift)
        return [add(*[v[b] for v in acc]) for b in range(self.hi)]

    def over_lo_hi(self, parts):
        parts = yield from self.over_lo(parts)
        return total(*(yield from self.ring(parts, self.hi_shift)))

    def over_hi(self, chunks):
        parts = [jnp.concatenate(rows, axis=1) for rows in zip(*chunks)]
        return (yield from self.direct(parts))

    def expert_tree(self, near, far, sizes, known):
        got = yield self.core_shift(far)
        out, at = [], 0
        for c, size in enumerate(sizes):
            cut = slice(at, at + size)
            at += size
            if c == len(sizes) - 1:
                near, got = yield near, got
            acc = add(near[self.xs - 1, cut], got[self.xs - 1, cut])
            for b in range(self.xs - 2, -1, -1):
                acc, near, got = yield self.x_shift(acc), near, got
                if b:
                    acc = add(near[b, cut], got[b, cut], acc)
            out.append(acc)
            known.append((near, got, tuple(out)))
        return known[-1]


def gather_kernel(count, cap, base_ref, *refs):
    hidden, grads, (xs, gs, slots) = refs[:count], refs[count : 2 * count], refs[2 * count :]
    step, seq_rows = slots.shape[1:]
    first = base_ref[0] + 1 + pl.program_id(0) * step
    ids = (first + lax.broadcasted_iota(jnp.int32, (step, seq_rows), 0)).astype(F32)
    before = lax.broadcasted_iota(jnp.int32, (seq_rows, seq_rows), 0)
    after = lax.broadcasted_iota(jnp.int32, (seq_rows, seq_rows), 1)
    earlier = (before < after).astype(F32).astype(BF)
    place = lax.broadcasted_iota(jnp.int32, (step, cap, seq_rows), 1).astype(F32)
    for i in range(count):
        digits = hidden[i][seq_rows:, : 2 * seq_rows].astype(F32)
        picks = digits[:, :seq_rows] * 16.0 + digits[:, seq_rows:]
        member = picks[0:1, :] == ids
        for k in range(1, picks.shape[0]):
            member = member | (picks[k : k + 1, :] == ids)
        slot = jnp.where(member, dot(member.astype(F32).astype(BF), earlier), -1.0)
        slots[i] = slot
        pick = (slot[:, None, :] == place).astype(F32).astype(BF).reshape(step * cap, seq_rows)
        for source, out in ((hidden[i], xs), (grads[i], gs)):
            got = dot(pick, source[:seq_rows, :])
            out[:, i * cap : (i + 1) * cap, :] = got.astype(BF).reshape(step, cap, got.shape[1])


def gather_call(base, hidden, grads, experts, cap):
    count = len(hidden)
    seq_rows, width = grads[0].shape
    rows = jax.ShapeDtypeStruct((experts, count * cap, width), BF)
    row_spec = pl.BlockSpec((8, count * cap, width), lambda i, _: (i, 0, 0))
    whole = lambda v: pl.BlockSpec(v.shape, lambda i, _: (0, 0))
    return pl.pallas_call(
        functools.partial(gather_kernel, count, cap),
        grid_spec=pltpu.PrefetchScalarGridSpec(
            num_scalar_prefetch=1,
            grid=(experts // 8,),
            in_specs=[whole(v) for v in (*hidden, *grads)],
            out_specs=[
                row_spec,
                row_spec,
                pl.BlockSpec((count, 8, seq_rows), lambda i, _: (0, i, 0)),
            ],
        ),
        out_shape=[rows, rows, jax.ShapeDtypeStruct((count, experts, seq_rows), F32)],
        compiler_params=pltpu.CompilerParams(vmem_limit_bytes=VMEM_LIMIT),
        cost_estimate=pl.CostEstimate(
            flops=4 * count * experts * cap * seq_rows * width,
            bytes_accessed=4 * experts * count * cap * width,
            transcendentals=0,
        ),
        name="gather_rows",
    )(base, *hidden, *grads)


def expert_kernel(n, groups, cap, many, at_ref, *refs):
    xs_in, gs_in = refs[: n[0]], refs[n[0] : sum(n)]
    up, down, router = refs[sum(n) : sum(n) + 3]
    slots = refs[sum(n) + 3 : sum(n) + 3 + n[0]]
    outs = refs[sum(n) + 3 + n[0] :]
    moe = outs[:groups]
    dhid = outs[groups : 2 * groups]
    near, far, grt = outs[2 * groups : 2 * groups + 3]
    xs, gs, w, d2, gacc, dr = outs[2 * groups + 3 :]
    step = pl.program_id(0)
    ff = up.shape[2]

    @pl.when(step == 0)
    def _():
        for k in range(many):
            w[k, :, ff:] = router[...]
        grt[...] = jnp.zeros_like(grt)

    for k in range(many):
        for whole, pieces in ((xs, xs_in), (gs, gs_in)):
            at = 0
            for piece in pieces:
                whole[k, at : at + piece.shape[1], :] = piece[k]
                at += piece.shape[1]
        w[k, :, :ff] = up[k]
    both = [jnp.dot(xs[k], w[k], preferred_element_type=F32) for k in range(many)]
    us = [jnp.dot(gs[k], down[k], preferred_element_type=F32) for k in range(many)]
    scaled = []
    for k in range(many):
        pre, u = both[k][:, :ff], us[k]
        sel = lax.broadcasted_iota(jnp.int32, pre.shape, 1) == step * many + k
        logit = jnp.sum(jnp.where(sel, both[k][:, ff:], 0.0), axis=1, keepdims=True)
        chosen = jax.nn.sigmoid(logit)
        square = pre * pre
        t = jnp.tanh(GELU_C * (pre + GELU_K * (square * pre)))
        half = 0.5 * (1.0 + t)
        act = (half * pre).astype(BF)
        slope = half + 0.5 * pre * (1.0 - t * t) * (GELU_C * (1.0 + 3.0 * GELU_K * square))
        act32 = act.astype(F32)
        dchosen = jnp.sum(u * act32, axis=1, keepdims=True)
        drl = dchosen * chosen * (1.0 - chosen)
        scaled.append((chosen * act32).astype(BF))
        d2[k, :, :ff] = (chosen * u * slope).astype(BF)
        d2[k, :, ff:] = jnp.where(sel, drl, 0.0).astype(BF)
    for k in range(many):
        dgot = lax.dot_general(
            d2[k], w[k], (((1,), (1,)), ((), ())), preferred_element_type=F32
        ).astype(BF)
        got = lax.dot_general(
            scaled[k], down[k], (((1,), (1,)), ((), ())), preferred_element_type=F32
        ).astype(BF)
        at = pl.multiple_of((step * many + k) * cap, cap)
        for s in range(groups):
            moe[s][k] = got[s * cap : (s + 1) * cap]
            dr[s, pl.ds(at, cap), :] = dgot[s * cap : (s + 1) * cap]
    x_size, _, _, _, lanes = near.shape
    for k in range(many):
        gu = lax.dot_general(d2[k], xs[k], (((0,), (0,)), ((), ())), preferred_element_type=F32)
        gacc[k, 0] = gu[:ff]
        grt[...] += gu[ff : ff + grt.shape[0]]
        gacc[k, 1] = lax.dot_general(
            scaled[k], gs[k], (((0,), (0,)), ((), ())), preferred_element_type=F32
        )
        for xr in range(x_size):
            base = lax.rem(at_ref[1] + xr, x_size) * 2
            for cr, out in enumerate((near, far)):
                cut = pl.multiple_of((base + lax.rem(at_ref[0] + cr, 2)) * lanes, lanes)
                for i in range(2):
                    out[xr, k, i] = gacc[k, i, :, pl.ds(cut, lanes)].astype(BF)

    @pl.when(step == pl.num_programs(0) - 1)
    def _():
        experts = slots[0].shape[1]
        spread = slot_spread(experts, cap)
        source = 0
        for group in slots:
            for i in range(group.shape[0]):
                put = slot_picks(group[i], spread, cap)
                dhid[source][...] = dot(put, dr[source]).astype(BF)
                source += 1


def slot_spread(experts, cap):
    rowi = lax.broadcasted_iota(jnp.int32, (experts, experts * cap), 0)
    coli = lax.broadcasted_iota(jnp.int32, (experts, experts * cap), 1)
    return (coli // cap == rowi).astype(F32).astype(BF)


def slot_picks(slot, spread, cap):
    wide = dot_tn(slot.astype(BF), spread)
    lane = lax.broadcasted_iota(jnp.int32, wide.shape, 1) % cap
    return (wide == lane.astype(F32)).astype(F32).astype(BF)


def expert_call(coords, x_size, groups, xs, gs, up, down, router, slots, cap, many=2):
    experts, width, ff = up.shape
    rows = groups * cap
    pad = -(-experts // 8) * 8
    seq_rows = slots[0].shape[2]
    lanes = width // (2 * x_size)
    row_specs = [
        pl.BlockSpec((many, v.shape[1], width), lambda e, _: (e, 0, 0)) for v in (*xs, *gs)
    ]
    w_spec = pl.BlockSpec((many, width, ff), lambda e, _: (e, 0, 0))
    whole = lambda *shape: pl.BlockSpec(shape, lambda e, _: (0,) * len(shape))
    g_spec = pl.BlockSpec((x_size, many, 2, ff, lanes), lambda e, _: (0, e, 0, 0, 0))
    s_spec = pl.BlockSpec((many, cap, width), lambda e, _: (e, 0, 0))
    one = jax.ShapeDtypeStruct((experts, cap, width), BF)
    outs = pl.pallas_call(
        functools.partial(expert_kernel, (len(xs), len(gs)), groups, cap, many),
        grid_spec=pltpu.PrefetchScalarGridSpec(
            num_scalar_prefetch=1,
            grid=(experts // many,),
            in_specs=[*row_specs, w_spec, w_spec, whole(width, ff)] + [whole(*v.shape) for v in slots],
            out_specs=[s_spec] * groups
            + [whole(seq_rows, width)] * groups
            + [g_spec, g_spec, whole(pad, width)],
            scratch_shapes=[
                pltpu.VMEM((many, rows, width), BF),
                pltpu.VMEM((many, rows, width), BF),
                pltpu.VMEM((many, width, 2 * ff), BF),
                pltpu.VMEM((many, rows, 2 * ff), BF),
                pltpu.VMEM((many, 2, ff, width), F32),
                pltpu.VMEM((groups, experts * cap, width), BF),
            ],
        ),
        out_shape=[one] * groups
        + [jax.ShapeDtypeStruct((seq_rows, width), BF)] * groups
        + [jax.ShapeDtypeStruct((x_size, experts, 2, ff, lanes), BF)] * 2
        + [jax.ShapeDtypeStruct((pad, width), F32)],
        compiler_params=pltpu.CompilerParams(vmem_limit_bytes=VMEM_LIMIT),
        cost_estimate=pl.CostEstimate(
            flops=experts * rows * width * ff * 2 * 8,
            bytes_accessed=experts * rows * width * 8,
            transcendentals=0,
        ),
        name="experts",
    )(coords, *xs, *gs, up, down, router, *slots)
    return outs[:groups], outs[groups : 2 * groups], outs[-3], outs[-2], outs[-1]


def finish_kernel(starts, near, got, *refs):
    accs, (up, down) = refs[: len(starts) - 1], refs[-2:]
    step = pl.program_id(0)
    for acc, first, after in zip(accs, starts, starts[1:]):

        @pl.when((step >= first) & (step < after))
        def _(acc=acc):
            for k in range(acc.shape[0]):
                for i, out in enumerate((up, down)):
                    out[k] = jnp.transpose(
                        near[0, k, i].astype(F32) + got[0, k, i].astype(F32) + acc[k, i].astype(F32)
                    )


def finish_call(near, got, accs, skip=0, known=()):
    _, experts, _, ff, lanes = near.shape
    each = accs[0].shape[0]
    starts = [sum(v.shape[0] for v in accs[:i]) // each for i in range(skip, len(accs) + 1)]
    before = starts[0]
    mine = pl.BlockSpec((1, each, 2, ff, lanes), lambda c: (0, c + before, 0, 0, 0))
    out = pl.BlockSpec((each, lanes, ff), lambda c: (c + before, 0, 0))
    starts = [v - before for v in starts]
    accs = accs[skip:]

    def acc_spec(first, after):
        return pl.BlockSpec(
            (each, 2, ff, lanes), lambda c: (jnp.clip(c - first, 0, after - first - 1), 0, 0, 0)
        )

    return pl.pallas_call(
        functools.partial(finish_kernel, starts),
        grid=(starts[-1],),
        in_specs=[mine, mine]
        + [acc_spec(*pair) for pair in zip(starts, starts[1:])]
        + [pl.BlockSpec(memory_space=pl.ANY)] * len(known),
        out_specs=[out, out],
        out_shape=[jax.ShapeDtypeStruct((experts, lanes, ff), F32)] * 2,
        input_output_aliases={2 + len(accs) + i: i for i in range(len(known))},
        compiler_params=pltpu.CompilerParams(vmem_limit_bytes=VMEM_LIMIT),
        cost_estimate=pl.CostEstimate(
            flops=0, bytes_accessed=20 * experts * lanes * ff, transcendentals=0
        ),
        name="expert_grads",
    )(near, got, *accs, *known)


def scatter_kernel(places, *refs):
    count = len(places)
    rows, slots, outs = refs[:count], refs[count : 2 * count], refs[2 * count :]
    experts, cap, width = rows[0].shape
    spread = slot_spread(experts, cap)
    for s in range(count):
        put = slot_picks(slots[s][places[s]], spread, cap)
        outs[s][...] = dot(put, rows[s][...].reshape(experts * cap, width)).astype(BF)


def scatter_call(rows, slots):
    count = len(rows)
    experts, cap, width = rows[0].shape
    seq_rows = slots[0][0].shape[2]
    return pl.pallas_call(
        functools.partial(scatter_kernel, tuple(j for _, j in slots)),
        out_shape=[jax.ShapeDtypeStruct((seq_rows, width), BF)] * count,
        compiler_params=pltpu.CompilerParams(vmem_limit_bytes=VMEM_LIMIT),
        cost_estimate=pl.CostEstimate(
            flops=2 * count * seq_rows * experts * cap * width,
            bytes_accessed=2 * count * experts * cap * width,
            transcendentals=0,
        ),
        name="scatter_rows",
    )(*rows, *[v for v, _ in slots])


def put_rows(res, outs, sizes, rows, at_ref):
    lo, hi = sizes
    for lr in range(lo):
        l = lax.rem(at_ref[2] + lr, lo)
        for hr in range(hi):
            h = lax.rem(at_ref[3] + hr, hi)
            start = pl.multiple_of((h * lo + l) * rows, rows)
            outs[lr][hr] = res[pl.ds(start, rows), :].astype(BF)


def gate_widener(at):
    shape = (128, AEXP * HEAD)
    row = lax.broadcasted_iota(jnp.int32, shape, 0)
    want = at + lax.broadcasted_iota(jnp.int32, shape, 1) // HEAD
    return ((row == want) | (row == want + 2 * HEADS * AEXP)).astype(F32).astype(BF)


def gated_kernel(count, sizes, rows, gate_at, at_ref, left, *refs):
    bases, gates, outs, (right, res) = refs[:count], refs[count : 2 * count], refs[2 * count : -2], refs[-2:]
    seq_rows = bases[0].shape[0]
    widen = gate_widener(gate_at + pl.program_id(0) * AEXP)
    for p in range(count):
        base, wide = bases[p][...].astype(F32), dot(gates[p][...], widen)
        for e in range(AEXP):
            cut = slice(e * HEAD, (e + 1) * HEAD)
            right[p * seq_rows : (p + 1) * seq_rows, cut] = (wide[:, cut] * base).astype(BF)
    res[...] = dot(left[...], right[...])
    put_rows(res, outs, sizes, rows, at_ref)


def gated_call(coords, grid, left, bases, base_at, packs, gate_at):
    width, tokens = left.shape
    seq_rows = bases[0].shape[0]
    sizes = (grid.lo, grid.hi)
    rows = width // (grid.lo * grid.hi)
    tile = AEXP * HEAD
    count = len(bases)
    out = (grid.hi, rows, HEADS * tile)
    return pl.pallas_call(
        functools.partial(gated_kernel, count, sizes, rows, gate_at),
        grid_spec=pltpu.PrefetchScalarGridSpec(
            num_scalar_prefetch=1,
            grid=(HEADS,),
            in_specs=[whole_spec(width, tokens)]
            + [pl.BlockSpec((seq_rows, HEAD), lambda h, _: (0, base_at // HEAD + h))] * count
            + [pl.BlockSpec((seq_rows, 128), lambda h, _: (0, HEADS))] * count,
            out_specs=[pl.BlockSpec((grid.hi, rows, tile), lambda h, _: (0, 0, h))] * grid.lo,
            scratch_shapes=[pltpu.VMEM((tokens, tile), BF), pltpu.VMEM((width, tile), F32)],
        ),
        out_shape=[jax.ShapeDtypeStruct(out, BF)] * grid.lo,
        compiler_params=pltpu.CompilerParams(vmem_limit_bytes=VMEM_LIMIT),
        cost_estimate=pl.CostEstimate(
            flops=2 * width * tokens * HEADS * tile,
            bytes_accessed=2 * width * HEADS * tile,
            transcendentals=0,
        ),
        name="gated_grad",
    )(coords, left, *bases, *packs)


def plain_kernel(count, sizes, rows, at_ref, left, last_left, extra, *refs):
    factors, outs, (right, res) = refs[:count], refs[count:-2], refs[-2:]
    step, last = pl.program_id(0), pl.num_programs(0) - 1
    seq_rows = factors[0].shape[0]
    for p in range(count):
        right[p * seq_rows : (p + 1) * seq_rows, :] = factors[p][...]

    @pl.when(step < last)
    def _():
        res[...] = dot(left[...], right[...])

    @pl.when(step == last)
    def _():
        width = res.shape[0]
        mine = pl.ds(pl.multiple_of((at_ref[1] * 2 + at_ref[0]) * width, width), width)
        res[...] = dot(last_left[...], right[...]) + jnp.transpose(extra[:, mine])

    put_rows(res, outs, sizes, rows, at_ref)


def plain_call(coords, grid, left, last_left, extra, factors, cols):
    width, tokens = left.shape
    seq_rows = factors[0].shape[0]
    tile = extra.shape[0]
    sizes = (grid.lo, grid.hi)
    rows = width // (grid.lo * grid.hi)
    count = len(factors)
    return pl.pallas_call(
        functools.partial(plain_kernel, count, sizes, rows),
        grid_spec=pltpu.PrefetchScalarGridSpec(
            num_scalar_prefetch=1,
            grid=(cols // tile,),
            in_specs=[
                whole_spec(width, tokens),
                whole_spec(width, tokens),
                whole_spec(*extra.shape),
            ]
            + [head_spec(seq_rows, tile)] * count,
            out_specs=[pl.BlockSpec((grid.hi, rows, tile), lambda j, _: (0, 0, j))] * grid.lo,
            scratch_shapes=[pltpu.VMEM((tokens, tile), BF), pltpu.VMEM((width, tile), F32)],
        ),
        out_shape=[jax.ShapeDtypeStruct((grid.hi, rows, cols), BF)] * grid.lo,
        compiler_params=pltpu.CompilerParams(vmem_limit_bytes=VMEM_LIMIT),
        cost_estimate=pl.CostEstimate(
            flops=2 * width * tokens * cols, bytes_accessed=2 * width * cols, transcendentals=0
        ),
        name="plain_grad",
    )(coords, left, last_left, extra, *factors)


def turn_kernel(count, at_ref, *refs):
    for n in range(len(refs) * count // (count + 1)):
        seq_rows, out = refs[n].shape[0], refs[len(refs) * count // (count + 1) + n // count]
        each = out.shape[0]
        mine = pl.ds(pl.multiple_of((at_ref[1] * 2 + at_ref[0]) * each, each), each)
        at = n % count * seq_rows
        out[:, at : at + seq_rows] = jnp.transpose(refs[n][:, mine])


def turn_call(coords, grid, groups):
    seq_rows, width = groups[0][0].shape
    count = len(groups[0])
    vmem = pl.BlockSpec(memory_space=pltpu.VMEM)
    return pl.pallas_call(
        functools.partial(turn_kernel, count),
        in_specs=[pl.BlockSpec(memory_space=pltpu.SMEM)] + [vmem] * (count * len(groups)),
        out_specs=[vmem] * len(groups),
        out_shape=[jax.ShapeDtypeStruct((width // grid.dp, count * seq_rows), BF)] * len(groups),
        compiler_params=pltpu.CompilerParams(vmem_limit_bytes=VMEM_LIMIT),
        name="turn",
    )(coords, *[v for group in groups for v in group])


NT = (((1,), (1,)), ((), ()))
TN = (((0,), (0,)), ((), ()))


def dot_nt(a, b):
    return lax.dot_general(a, b, NT, preferred_element_type=F32)


def dot_tn(a, b):
    return lax.dot_general(a, b, TN, preferred_element_type=F32)


def dot(a, b):
    return jnp.dot(a, b, preferred_element_type=F32)


def pick_mask(choice):
    picks = choice.shape[0]
    row = lax.broadcasted_iota(jnp.int32, (picks, HEADS * AEXP), 0)
    head = lax.broadcasted_iota(jnp.int32, (picks, HEADS * AEXP), 1) // AEXP
    low = choice.astype(F32).astype(BF)
    first = dot_tn(low, (row == head).astype(F32).astype(BF))
    second = dot_tn(low, (row == HEADS + head).astype(F32).astype(BF))
    expert = (lax.broadcasted_iota(jnp.int32, first.shape, 1) % AEXP).astype(F32)
    return ((first == expert) | (second == expert)).astype(F32)


def normalize(x):
    mean = jnp.mean(x, axis=1, keepdims=True)
    centered = x - mean
    inverse = lax.rsqrt(jnp.mean(centered * centered, axis=1, keepdims=True) + 1e-05)
    return centered * inverse, inverse


def probabilities(q, k, length):
    scores = dot_nt(q, k) * (1.0 / math.sqrt(HEAD))
    row = lax.broadcasted_iota(jnp.int32, scores.shape, 0)
    col = lax.broadcasted_iota(jnp.int32, scores.shape, 1)
    scores = jnp.where((col <= row) & (col < length), scores, -1e30)
    expo = jnp.exp(scores - jnp.max(scores, axis=1, keepdims=True))
    return expo / jnp.sum(expo, axis=1, keepdims=True)


def forward_head(
    h, length, tokens, normed, cos, sin, wq, wk, wv, wo, gates,
    q_out, k_out, mixed_out, vals_out, att_out, expanded,
):
    q = dot(normed[...], wq[...])
    k = dot(normed[...], wk[...])
    q = (q * cos[...] + pltpu.roll(q, HEAD // 2, 1) * sin[...]).astype(BF)
    k = (k * cos[...] + pltpu.roll(k, HEAD // 2, 1) * sin[...]).astype(BF)
    q_out[...] = q
    k_out[...] = k
    vals = dot(tokens[...], wv[...])
    vals_out[...] = vals
    mixed = jnp.zeros_like(q, F32)
    wide = dot(gates[...], gate_widener(h * AEXP))
    for e in range(AEXP):
        cut = slice(e * HEAD, (e + 1) * HEAD)
        mixed += wide[:, cut] * vals[:, cut]
    mixed = mixed.astype(BF)
    mixed_out[...] = mixed
    probs = probabilities(q, k, length).astype(BF)
    att = dot(probs, mixed)
    att_out[...] = att
    wide = dot(gates[...], gate_widener((HEADS + h) * AEXP))
    for e in range(AEXP):
        cut = slice(e * HEAD, (e + 1) * HEAD)
        expanded[:, cut] = (wide[:, cut] * att).astype(BF)
    return dot_nt(expanded[...], wo[...])


def first_heads_kernel(
    length_ref, tokens, cos, sin, wq, wk, wv, wo, gain, vr, orr, vc, oc,
    acc, q_out, k_out, mixed_out, vals_out, att_out, normed, gates, slopes, expanded,
):
    @pl.when(pl.program_id(0) == 0)
    def _():
        scaled, _ = normalize(tokens[...].astype(F32))
        normed[...] = (scaled * gain[...]).astype(BF)
        gates[...] = jnp.zeros_like(gates)
        slopes[...] = jnp.zeros_like(slopes)
        for n, (router, choice) in enumerate(((vr, vc), (orr, oc))):
            sig, mask = jax.nn.sigmoid(dot_nt(tokens[...], router[...])), pick_mask(choice[...])
            high = (sig * mask).astype(BF)
            many = HEADS * AEXP
            gates[:, n * many : (n + 1) * many] = high
            gates[:, (n + 2) * many : (n + 3) * many] = (sig * mask - high.astype(F32)).astype(BF)
            slopes[:, n * many : (n + 1) * many] = mask * sig * (1.0 - sig)
        acc[...] = tokens[...].astype(F32)

    acc[...] += forward_head(
        pl.program_id(0), length_ref[0], tokens, normed, cos, sin, wq, wk, wv, wo,
        gates,
        q_out, k_out, mixed_out, vals_out, att_out, expanded,
    )


def last_heads_kernel(start, *refs):
    length_ref, tokens, cos, sin, wq, wk, wv, wo, normed, gates, codes, acc, known_att = refs[:13]
    hidden, q_out, k_out, mixed_out, vals_out, att_out, hidden_low, pack, expanded = refs[-9:]

    @pl.when(pl.program_id(0) == 0)
    def _():
        hidden[...] = acc[...]

    hidden[...] += forward_head(
        start + pl.program_id(0), length_ref[0], tokens, normed, cos, sin, wq, wk, wv, wo,
        gates,
        q_out, k_out, mixed_out, vals_out, att_out, expanded,
    )

    at = (start + pl.program_id(0)) * HEAD
    pack[:, pl.ds(pl.multiple_of(at, HEAD), HEAD)] = att_out[...].astype(BF)

    @pl.when(pl.program_id(0) == 0)
    def _():
        pack[:, : start * HEAD] = known_att[...].astype(BF)
        pack[:, HEADS * HEAD :] = gates[...]

    @pl.when(pl.program_id(0) == pl.num_programs(0) - 1)
    def _():
        rows = hidden.shape[0]
        hidden_low[:rows, :] = hidden[...].astype(BF)
        code = codes[...]
        high = lax.shift_right_logical(code, 4)
        hidden_low[rows:, :rows] = high.astype(F32).astype(BF)
        hidden_low[rows:, rows : 2 * rows] = (code - high * 16).astype(F32).astype(BF)
        hidden_low[rows:, 2 * rows :] = jnp.zeros((code.shape[0], hidden_low.shape[1] - 2 * rows), BF)


def whole_spec(*shape):
    return pl.BlockSpec(shape, lambda h, _: (0,) * len(shape))


def head_spec(rows, cols):
    return pl.BlockSpec((rows, cols), lambda h, _: (0, h))


def heads_common(rows, width, start):
    many = AEXP * HEAD
    head = lambda rows, cols: pl.BlockSpec((rows, cols), lambda h, _: (0, h + start))
    shape = lambda cols, kind: jax.ShapeDtypeStruct((rows, cols), kind)
    in_specs = [
        whole_spec(rows, width),
        whole_spec(rows, HEAD),
        whole_spec(rows, HEAD),
        head(width, HEAD),
        head(width, HEAD),
        head(width, many),
        head(width, many),
    ]
    out_specs = [whole_spec(rows, width)] + [head(rows, HEAD)] * 3
    out_specs += [head(rows, many), head(rows, HEAD)]
    out_shape = [shape(width, F32)] + [shape(HEADS * HEAD, BF)] * 3
    out_shape += [shape(HEADS * many, F32), shape(HEADS * HEAD, F32)]
    cost = pl.CostEstimate(
        flops=rows * width * HEADS * (2 * HEAD + 2 * many),
        bytes_accessed=width * HEADS * (2 * HEAD + 2 * many),
        transcendentals=0,
    )
    return in_specs, out_specs, out_shape, cost


def first_heads(lengths, tokens, cos, sin, wq, wk, wv, wo, gain, vr, orr, vc, oc):
    rows, width = tokens.shape
    in_specs, out_specs, out_shape, cost = heads_common(rows, width, 0)
    return pl.pallas_call(
        first_heads_kernel,
        grid_spec=pltpu.PrefetchScalarGridSpec(
            num_scalar_prefetch=1,
            grid=(HEADS // 2,),
            in_specs=in_specs + [whole_spec(*v.shape) for v in (gain, vr, orr, vc, oc)],
            out_specs=out_specs + [whole_spec(rows, width)] + [whole_spec(rows, 128)] * 2,
            scratch_shapes=[pltpu.VMEM((rows, AEXP * HEAD), BF)],
        ),
        out_shape=out_shape
        + [jax.ShapeDtypeStruct((rows, width), BF)]
        + [jax.ShapeDtypeStruct((rows, 128), kind) for kind in (BF, F32)],
        compiler_params=pltpu.CompilerParams(vmem_limit_bytes=VMEM_LIMIT),
        cost_estimate=cost,
        name="attention_forward",
    )(lengths, tokens, cos, sin, wq, wk, wv, wo, gain, vr, orr, vc, oc)


def last_heads(lengths, tokens, cos, sin, wq, wk, wv, wo, normed, gates, codes, acc, known):
    rows, width = tokens.shape
    start = HEADS // 2
    in_specs, out_specs, out_shape, cost = heads_common(rows, width, start)
    operands = [lengths, tokens, cos, sin, wq, wk, wv, wo, normed, gates, codes, acc]
    in_specs += [whole_spec(*v.shape) for v in operands[8:]]
    operands.append(known[-1])
    in_specs.append(whole_spec(rows, start * HEAD))
    low = (rows + codes.shape[0], width)
    packed = (rows, HEADS * HEAD + 128)
    return pl.pallas_call(
        functools.partial(last_heads_kernel, start),
        grid_spec=pltpu.PrefetchScalarGridSpec(
            num_scalar_prefetch=1,
            grid=(HEADS - start,),
            in_specs=in_specs + [pl.BlockSpec(memory_space=pl.ANY)] * len(known),
            out_specs=out_specs + [whole_spec(*low), whole_spec(*packed)],
            scratch_shapes=[pltpu.VMEM((rows, AEXP * HEAD), BF)],
        ),
        out_shape=out_shape + [jax.ShapeDtypeStruct(low, BF), jax.ShapeDtypeStruct(packed, BF)],
        input_output_aliases={len(operands) + i: 1 + i for i in range(len(known))},
        compiler_params=pltpu.CompilerParams(vmem_limit_bytes=VMEM_LIMIT),
        cost_estimate=cost,
        name="attention_forward_rest",
    )(*operands, *known)


def backward_kernel(
    length_ref, cos, sin, wo, q_in, k_in, mixed_in, vals, att, gates, slopes, dbranch,
    factors, mixes, dvals, dl,
):
    h = pl.program_id(0)
    logit_at = 2 * HEADS * HEAD

    @pl.when(h == 0)
    def _():
        dl[...] = jnp.zeros_like(dl)
        factors[:, logit_at:] = jnp.zeros((dl.shape[0], factors.shape[1] - logit_at), BF)

    lane = lax.broadcasted_iota(jnp.int32, dl.shape, 1)
    scale = 1.0 / math.sqrt(HEAD)
    dexp = dot(dbranch[...], wo[...])
    datt = jnp.zeros_like(att)
    wide = dot(gates[...], gate_widener((HEADS + h) * AEXP))
    sums = jnp.zeros_like(dl)
    for e in range(AEXP):
        part = dexp[:, e * HEAD : (e + 1) * HEAD]
        datt += wide[:, e * HEAD : (e + 1) * HEAD] * part
        logit = jnp.sum(part * att[...], axis=1, keepdims=True)
        sums = jnp.where(lane == (HEADS + h) * AEXP + e, logit, sums)
    datt = datt.astype(BF)
    q, k, mixed = q_in[...], k_in[...], mixed_in[...]
    probs = probabilities(q, k, length_ref[0])
    dp = dot_nt(datt, mixed)
    inner = jnp.sum(probs * dp, axis=1, keepdims=True)
    dscore = (probs * (dp - inner)).astype(BF)
    dq = dot(dscore, k) * scale
    dk = dot_tn(dscore, q) * scale
    dmixed = dot_tn(probs.astype(BF), datt)
    dq = (dq * cos[...] - pltpu.roll(dq, HEAD // 2, 1) * sin[...]).astype(BF)
    dk = (dk * cos[...] - pltpu.roll(dk, HEAD // 2, 1) * sin[...]).astype(BF)
    put = lambda at, value: factors.__setitem__(
        (slice(None), pl.ds(pl.multiple_of(at, HEAD), HEAD)), value
    )
    put(h * 2 * HEAD, dq)
    put(h * 2 * HEAD + HEAD, dk)
    mixes[...] = dmixed.astype(BF)
    wide = dot(gates[...], gate_widener(h * AEXP))
    for e in range(AEXP):
        part = vals[:, e * HEAD : (e + 1) * HEAD]
        dvals[:, e * HEAD : (e + 1) * HEAD] = (wide[:, e * HEAD : (e + 1) * HEAD] * dmixed).astype(BF)
        logit = jnp.sum(part * dmixed, axis=1, keepdims=True)
        sums = jnp.where(lane == h * AEXP + e, logit, sums)
    dl[...] += sums * slopes[...]

    @pl.when(h == pl.num_programs(0) - 1)
    def _():
        factors[:, logit_at : logit_at + dl.shape[1]] = dl[...].astype(BF)


def backward_call(small, lengths, dbranch, cos, sin, wo, q, k, mixed, vals, att, gates, slopes):
    rows, width = dbranch.shape
    many = AEXP * HEAD
    cols = HEADS * 2 * HEAD + small
    return pl.pallas_call(
        backward_kernel,
        grid_spec=pltpu.PrefetchScalarGridSpec(
            num_scalar_prefetch=1,
            grid=(HEADS,),
            in_specs=[
                whole_spec(rows, HEAD),
                whole_spec(rows, HEAD),
                head_spec(width, many),
                head_spec(rows, HEAD),
                head_spec(rows, HEAD),
                head_spec(rows, HEAD),
                head_spec(rows, many),
                head_spec(rows, HEAD),
            ]
            + [whole_spec(rows, 128)] * 2
            + [whole_spec(rows, width)],
            out_specs=[whole_spec(rows, cols), head_spec(rows, HEAD), head_spec(rows, many)],
            scratch_shapes=[pltpu.VMEM((rows, 128), F32)],
        ),
        out_shape=[
            jax.ShapeDtypeStruct((rows, cols), BF),
            jax.ShapeDtypeStruct((rows, HEADS * HEAD), BF),
            jax.ShapeDtypeStruct((rows, HEADS * many), BF),
        ],
        compiler_params=pltpu.CompilerParams(vmem_limit_bytes=VMEM_LIMIT),
        cost_estimate=pl.CostEstimate(
            flops=2 * rows * width * HEADS * many * 2,
            bytes_accessed=2 * width * HEADS * many,
            transcendentals=0,
        ),
        name="attention_backward",
    )(lengths, cos, sin, wo, q, k, mixed, vals, att, gates, slopes, dbranch)


def input_kernel(tokens, gain, dhidden, factors, dvals, wq, wk, wv, vr, orr, out, dn, rest):
    h = pl.program_id(0)
    logit_at = 2 * HEADS * HEAD

    @pl.when(h == 0)
    def _():
        gates = HEADS * AEXP
        dlogits = factors[:, logit_at : logit_at + 2 * gates]
        dn[...] = jnp.zeros_like(dn)
        rest[...] = (
            dhidden[...]
            + dot(dlogits[:, :gates], vr[...])
            + dot(dlogits[:, gates:], orr[...])
        )

    take = lambda at, size: factors[:, pl.ds(pl.multiple_of(at, HEAD), size)]
    dn[...] += dot_nt(take(h * 2 * HEAD, HEAD), wq[...])
    dn[...] += dot_nt(take(h * 2 * HEAD + HEAD, HEAD), wk[...])
    rest[...] += dot_nt(dvals[...], wv[...])

    @pl.when(h == pl.num_programs(0) - 1)
    def _():
        scaled, inverse = normalize(tokens[...].astype(F32))
        dscaled = dn[...] * gain[...]
        inside = (
            dscaled
            - jnp.mean(dscaled, axis=1, keepdims=True)
            - scaled * jnp.mean(dscaled * scaled, axis=1, keepdims=True)
        )
        out[...] = (rest[...] + inverse * inside).astype(BF)


def input_call(tokens, gain, dhidden, factors, dvals, wq, wk, wv, vr, orr):
    rows, width = tokens.shape
    many = AEXP * HEAD
    whole = lambda *shape: pl.BlockSpec(shape, lambda h: (0,) * len(shape))
    head = lambda *shape: pl.BlockSpec(shape, lambda h: (0, h))
    return pl.pallas_call(
        input_kernel,
        grid=(HEADS,),
        in_specs=[
            whole(rows, width),
            whole(1, width),
            whole(rows, width),
            whole(*factors.shape),
            head(rows, many),
            head(width, HEAD),
            head(width, HEAD),
            head(width, many),
            whole(HEADS * AEXP, width),
            whole(HEADS * AEXP, width),
        ],
        out_specs=whole(rows, width),
        out_shape=jax.ShapeDtypeStruct((rows, width), BF),
        scratch_shapes=[pltpu.VMEM((rows, width), F32)] * 2,
        compiler_params=pltpu.CompilerParams(vmem_limit_bytes=VMEM_LIMIT),
        cost_estimate=pl.CostEstimate(
            flops=2 * rows * width * HEADS * (many + 2 * HEAD),
            bytes_accessed=2 * width * HEADS * (many + 2 * HEAD),
            transcendentals=0,
        ),
        name="input_grad",
    )(tokens, gain, dhidden, factors, dvals, wq, wk, wv, vr, orr)


def last_kernel(count, experts_all, *refs):
    terms, (wq, wk, gain) = refs[:count], refs[count : count + 3]
    query, key, value, vr, orr, er, dgain, counts = refs[count + 3 :]
    summed = total(*[t[...] for t in terms])
    gates, pair = HEADS * AEXP, 2 * HEAD
    at = HEADS * pair
    small = summed.shape[1] - at - value.shape[1]
    value[...] = summed[:, at + small :]
    of_gain = jnp.zeros((query.shape[0], HEAD), F32)
    for h in range(HEADS):
        cut = slice(h * HEAD, (h + 1) * HEAD)
        q = summed[:, h * pair : h * pair + HEAD]
        k = summed[:, h * pair + HEAD : (h + 1) * pair]
        query[:, cut], key[:, cut] = q, k
        of_gain += q * wq[:, cut].astype(F32) + k * wk[:, cut].astype(F32)
    dgain[...] = jnp.sum(jnp.transpose(of_gain), axis=0, keepdims=True) / gain[...]
    tile = summed[:, at : at + small]
    turned = jnp.transpose(tile)
    vr[...] = turned[:gates]
    orr[...] = turned[gates : 2 * gates]
    er[...] = tile[:, 2 * gates : 2 * gates + experts_all]
    bit = lax.broadcasted_iota(jnp.int32, turned.shape, 0) - 2 * gates - experts_all
    worth = jnp.where((bit >= 0) & (bit < 6), jnp.left_shift(1, jnp.clip(bit, 0, 5)), 0)
    counts[...] = jnp.sum(turned * worth.astype(F32), axis=0, keepdims=True)


def last_call(terms, wq, wk, gain, experts_all):
    rows, qk = wq.shape
    gates = HEADS * AEXP
    shapes = [(rows, qk), (rows, qk), (rows, HEADS * AEXP * HEAD), (gates, rows), (gates, rows)]
    shapes += [(rows, experts_all), (1, rows), (1, rows)]
    return pl.pallas_call(
        functools.partial(last_kernel, len(terms), experts_all),
        out_shape=[jax.ShapeDtypeStruct(v, F32) for v in shapes],
        compiler_params=pltpu.CompilerParams(vmem_limit_bytes=VMEM_LIMIT),
        name="last_sums",
    )(*terms, wq, wk, gain)


def shards(
    tokens,
    norm_gain,
    query_weight,
    key_weight,
    value_weight,
    output_weight,
    value_router,
    output_router,
    expert_router,
    expert_up,
    expert_down,
    lengths,
    value_choice,
    output_choice,
    expert_choice,
    running_counts,
    cotangent,
):
    seq_rows, model_width = tokens.shape
    groups = lax.axis_size("expert")
    grid = Grid(lax.axis_size("dp"), groups)
    coords = grid.coords()
    me = lax.axis_index("expert")
    local_experts, _, ff = expert_up.shape
    experts_all = local_experts * groups
    picks_per = expert_choice.shape[1]
    cap = 3 * seq_rows * picks_per // (2 * experts_all)
    position = jnp.arange(seq_rows, dtype=jnp.int32)
    seq_length = lengths[0]

    code = jnp.where((position < seq_length)[:, None], expert_choice + 1, 0)
    all_grads, all_hidden = {}, {}
    grad_ring = Task(grid.gather_rows(cotangent, all_grads, True))

    cosine, sine = rope_tables(seq_rows, HEAD)
    gain = norm_gain.reshape(1, model_width)
    vc, oc = (
        jnp.transpose(v, (2, 1, 0)).reshape(-1, seq_rows) for v in (value_choice, output_choice)
    )
    turned_routers = (jnp.transpose(value_router), jnp.transpose(output_router))
    weights = (query_weight, key_weight, value_weight, output_weight)
    tokens_task = Task(grid.pieces(tokens))
    got = first_heads(
        lengths, tokens, cosine, sine, *weights, gain, *turned_routers, vc, oc
    )
    acc, *known, normed_low, gates, slopes = end_round([grad_ring, tokens_task], got)
    normed_task = Task(grid.pieces(normed_low))
    got = last_heads(
        lengths, tokens, cosine, sine, *weights, normed_low, gates, jnp.transpose(code), acc, known
    )
    got = end_round([grad_ring, tokens_task, normed_task], got)
    hidden, query_rot, key_rot, mixed, values_all, attended, hidden_low, pack = got
    pack_task = Task(grid.pieces(pack))
    hidden_low = end_round([grad_ring, tokens_task, normed_task, pack_task], hidden_low)

    ring = Task(grid.gather_rows(hidden_low, all_hidden))
    end_round([ring, tokens_task, normed_task, pack_task])
    finish([tokens_task, normed_task, pack_task])
    turned = turn_call(coords, grid, [normed_task.result, tokens_task.result])
    packs = pack_task.result
    base = (me * local_experts).reshape(1)
    xs, gs, slots, slot_groups = [], [], {}, []

    def gather(js):
        return gather_call(
            base, [all_hidden[j] for j in js], [all_grads[j] for j in js], local_experts, cap
        )

    def keep(js, got):
        xs.append(got[0])
        gs.append(got[1])
        slot_groups.append(got[2])
        for i, j in enumerate(js):
            slots[j] = (got[2], i)

    if grid.lo == 2:
        got, turned = end_round([ring], (gather(range(3)), turned))
        keep(range(3), got)
        keep((3, 4), end_round([ring, grad_ring], gather((3, 4))))
        keep((5, 6), end_round([ring, grad_ring], gather((5, 6))))
        finish([ring, grad_ring])
        keep((7,), gather((7,)))
    else:
        finish([ring, grad_ring])
        for j in range(0, groups, 4):
            keep(range(j, j + 4), gather(range(j, j + 4)))

    router_mine = lax.dynamic_slice_in_dim(expert_router, me * local_experts, local_experts, 1)
    router_pad = jnp.pad(router_mine, ((0, 0), (0, ff - local_experts)))
    moe_rows, dhid, near, far, grad_router_t = expert_call(
        coords, grid.xs, groups, xs, gs, expert_up, expert_down, router_pad, slot_groups, cap
    )
    moe = {}

    moe = {}

    def scatter(places):
        js = [grid.at(*place) for place in places]
        moe.update(zip(js, scatter_call([moe_rows[j] for j in js], [slots[j] for j in js])))

    def moe_part(j):
        if j not in moe:
            mate = j ^ 1
            got = scatter_call([moe_rows[j], moe_rows[mate]], [slots[j], slots[mate]])
            moe[j], moe[mate] = got
        return moe[j]

    devices = grid.dp * groups
    rows_each = model_width // devices
    labels_all = jnp.arange(experts_all, dtype=jnp.int32)
    local_counts = jnp.sum(
        (code[:, :, None] == labels_all + 1).astype(jnp.int32), axis=(0, 1), dtype=jnp.int32
    )
    bits = (local_counts[None, :] >> jnp.arange(6, dtype=jnp.int32)[:, None]) & 1
    bits = bits.reshape(6, devices, experts_all // devices)
    bits = jnp.pad(bits, ((0, 0), (0, 0), (0, rows_each - experts_all // devices)))
    bits = bits.reshape(6, model_width).astype(BF)
    routers = 2 * HEADS * AEXP
    small = -(-(routers + experts_all + 6) // 256) * 256
    held = -(-(local_experts + 6) // 16) * 16
    compact = jnp.concatenate(
        [
            grad_router_t[:local_experts].astype(BF),
            jnp.pad(bits, ((0, held - local_experts - 6), (0, 0))),
        ],
        axis=0,
    )

    two = grid.lo == 2
    back = Task(grid.sum_rows_hi(lambda j: dhid[j]))
    sixth = local_experts // 6
    summed = []
    cuts = (sixth,) * 3 + (local_experts - 3 * sixth,)
    shares = Task(grid.expert_tree(near, far, cuts, summed))
    if two:
        scatter([(3, 1), (3, 0)])
        moe.update(end_round([back, shares], moe))
        scatter([(2, 1), (2, 0)])
        ready, compact = end_round([back, shares], (moe, compact))
        moe.update(ready)
        scatter([(1, 1), (1, 0)])
    small_task = Task(grid.pieces(compact))
    if two:
        moe.update(end_round([back, shares, small_task], moe))
        scatter([(0, 1), (0, 0)])
    out_ring = Task(grid.sum_rows(moe_part))
    early = 2 if two else 0
    done = finish_call(*summed[early - 1]) if early else ()
    ready, done = end_round([back, shares, small_task, out_ring], (moe, done))
    moe.update(ready)
    finish([back, small_task])
    extra = total(*small_task.result)
    extra = lax.dynamic_update_slice_in_dim(
        jnp.pad(
            extra[local_experts : local_experts + 6],
            ((routers + experts_all, small - routers - experts_all - 6), (0, 0)),
        ),
        extra[:local_experts],
        routers + me * local_experts,
        0,
    )

    dhidden = total(cotangent, *back.result)
    dbranch = dhidden.astype(BF)
    branch_task = Task(grid.pieces(dbranch))
    factors, mixes, dvalues = backward_call(
        small, lengths, dbranch, cosine, sine, output_weight, query_rot, key_rot, mixed, values_all,
        attended, gates, slopes,
    )
    factors, mixes, dvalues, extra = end_round(
        [out_ring, branch_task], (factors, mixes, dvalues, extra)
    )
    mix_task = Task(grid.pieces(mixes))
    finish([branch_task])
    factors = end_round([mix_task], factors)
    factor_task = Task(grid.pieces(factors))
    [branch_turned] = turn_call(coords, grid, [branch_task.result])
    output_parts = gated_call(coords, grid, branch_turned, packs, 0, packs, HEADS * AEXP)

    output_sum = Task(grid.over_lo_hi(output_parts))
    finish([mix_task])
    value_parts = gated_call(coords, grid, turned[1], mix_task.result, 0, packs, 0)
    value_parts = end_round([out_ring], value_parts)
    value_sum = Task(grid.over_lo(value_parts))
    end_round([factor_task, shares])
    finish([factor_task])
    qk_part = plain_call(coords, grid, *turned, extra, factor_task.result, factors.shape[1])
    qk_part, factors = end_round([out_ring, output_sum], (qk_part, factors))
    finish([out_ring])
    qk_sum = Task(grid.over_lo(qk_part))
    grad_tokens = input_call(
        tokens, gain, dhidden, factors, dvalues, query_weight, key_weight, value_weight,
        *turned_routers,
    )
    grad_tokens = end_round([output_sum], grad_tokens)
    output = (hidden + total(*out_ring.result)).astype(BF)
    output = end_round([value_sum, qk_sum, output_sum], output)
    finish([value_sum, qk_sum])
    last = Task(grid.over_hi([qk_sum.result, value_sum.result]))
    finish([shares])
    expert_grads = finish_call(*shares.result, early, done)
    finish([output_sum])
    expert_grads, sum_output = end_round([last], (expert_grads, output_sum.result))
    finish([last])
    first = (lax.axis_index("dp") * groups + me) * rows_each
    rows_of = lambda w: lax.dynamic_slice_in_dim(w, first, rows_each, 0)
    grad_query, grad_key, grad_value, grad_vr, grad_or, grad_er, grad_gain, got_counts = last_call(
        last.result, rows_of(query_weight), rows_of(key_weight), rows_of(norm_gain)[None],
        experts_all,
    )
    counts = running_counts + got_counts[0, : experts_all // devices].astype(jnp.int32)
    return (
        output,
        grad_tokens,
        grad_gain[0],
        grad_query,
        grad_key,
        grad_value,
        sum_output,
        jnp.transpose(grad_vr),
        jnp.transpose(grad_or),
        grad_er,
        *expert_grads,
        counts,
    )


def solution(mesh):
    both = ("dp", "expert")
    in_specs = (
        P(both, None),
        P(),
        P(),
        P(),
        P(),
        P(),
        P(),
        P(),
        P(),
        P("expert", None, None),
        P("expert", None, None),
        P(both),
        P(both, None, None),
        P(both, None, None),
        P(both, None),
        P(both),
        P(both, None),
    )
    out_specs = (
        P(both, None),
        P(both, None),
        P(both),
        P(both, None),
        P(both, None),
        P(both, None),
        P(both, None),
        P(both, None),
        P(both, None),
        P(both, None),
        P("expert", "dp", None),
        P("expert", "dp", None),
        P(both),
    )
    return jax.shard_map(shards, mesh=mesh, in_specs=in_specs, out_specs=out_specs, check_vma=False)
```

```python
import functools
import math

import jax
import jax.numpy as jnp
import numpy as np
from jax import lax
from jax.experimental import pallas as pl
from jax.experimental.pallas import tpu as pltpu
from jax.sharding import PartitionSpec as P

HEADS = 4
HEAD = 128
AEXP = 5
BF = jnp.bfloat16
F32 = jnp.float32
VMEM_LIMIT = 60 * 1024 * 1024
GELU_C = math.sqrt(2.0 / math.pi)
GELU_K = 0.044715


def rope_tables(seq_rows, head_width):
    half_width = head_width // 2
    ladder = np.arange(half_width, dtype=np.float32) * np.float32(2.0 / head_width)
    freqs = np.exp(np.float32(-math.log(10000.0)) * ladder)
    angles = np.arange(seq_rows, dtype=np.float32)[:, None] * freqs[None, :]
    cosine, sine = np.cos(angles), np.sin(angles)
    return np.concatenate([cosine, cosine], axis=1), np.concatenate([-sine, sine], axis=1)


class Task:
    def __init__(self, gen):
        self.gen = gen
        self.done = False
        self.result = None
        self.advance(None)

    def advance(self, value):
        try:
            self.out = self.gen.send(value)
        except StopIteration as stop:
            self.done, self.out, self.result = True, None, stop.value


def end_round(tasks, extra=()):
    tasks = [t for t in tasks if not t.done]
    got, extra = lax.optimization_barrier((tuple(t.out for t in tasks), extra))
    for task, value in zip(tasks, got):
        task.advance(value)
    return extra


def finish(tasks, extra=()):
    while any(not t.done for t in tasks):
        extra = end_round(tasks, extra)
    return extra


def total(*parts):
    return functools.reduce(lambda a, b: a + b, [p.astype(F32) for p in parts])


def add(*parts):
    return total(*parts).astype(BF)


class Grid:
    def __init__(self, dp, size):
        self.dp = dp
        self.xs = dp // 2
        self.hi = 4
        self.lo = size // 4
        self.size = size

    def coords(self):
        dp, ex = lax.axis_index("dp"), lax.axis_index("expert")
        return jnp.stack([dp % 2, dp // 2, ex % self.lo, ex // self.lo])

    def core_shift(self, x):
        return lax.ppermute(x, "dp", [(i, i ^ 1) for i in range(self.dp)])

    def x_shift(self, x):
        pairs = [(i, (i // 2 + 1) % self.xs * 2 + i % 2) for i in range(self.dp)]
        return lax.ppermute(x, "dp", pairs)

    def hi_shift(self, x, by=1):
        pairs = [
            (i, ((i // self.lo + by) % self.hi) * self.lo + i % self.lo) for i in range(self.size)
        ]
        return lax.ppermute(x, "expert", pairs)

    def lo_shift(self, x):
        pairs = [
            (i, (i // self.lo) * self.lo + (i % self.lo + 1) % self.lo) for i in range(self.size)
        ]
        return lax.ppermute(x, "expert", pairs)

    def sources(self):
        me = lax.axis_index("expert")
        h, l = me // self.lo, me % self.lo
        return [
            ((h + self.hi - dh) % self.hi) * self.lo + (l + self.lo - dl) % self.lo
            for dh in range(self.hi)
            for dl in range(self.lo)
        ]

    def gather_rows(self, block, known, last_over_hi=False):
        rows = {(0, 0): block}
        known[0] = block
        steps = self.hi + self.lo - 2
        last = (self.hi - 1, self.lo - 1)
        for step in range(steps):
            fresh = {}
            for dh in range(self.hi):
                for dl in range(self.lo):
                    if dh + dl == step + 1:
                        if dl == 0 or (last_over_hi and (dh, dl) == last):
                            fresh[(dh, dl)] = self.hi_shift(rows[(dh - 1, dl)])
                        else:
                            fresh[(dh, dl)] = self.lo_shift(rows[(dh, dl - 1)])
            got = yield fresh
            for (dh, dl), value in got.items():
                known[dh * self.lo + dl] = value
            if last_over_hi and step == steps - 2:
                got = yield got
            rows.update(got)

    def at(self, a, b):
        return ((self.hi - a) % self.hi) * self.lo + (self.lo - b) % self.lo

    def sum_rows(self, part):
        p = lambda a, b: part(self.at(a, b))
        sums = {}
        for step in range(self.hi + self.lo - 2):
            sent = {}
            for a in range(self.hi):
                for b in range(self.lo):
                    if (self.hi - 1 - a) + (self.lo - 1 - b) == step:
                        mine = add(p(a, b), *sums.pop((a, b), ()))
                        if b > 0:
                            sent[(a, b - 1, 0)] = self.lo_shift(mine)
                        else:
                            sent[(a - 1, b, 1)] = self.hi_shift(mine)
            got = yield sent
            for (a, b, _), value in got.items():
                sums.setdefault((a, b), []).append(value)
        return [p(0, 0), *sums.pop((0, 0))]

    def sum_rows_hi(self, part):
        p = lambda a, b: part(self.at(a, b))
        if self.lo != 2:
            return (yield from self.sum_rows(part))
        one, own = yield self.hi_shift(p(3, 1)), self.lo_shift(p(0, 1))
        one, two = yield self.lo_shift(add(p(2, 1), one)), self.hi_shift(p(3, 0))
        one, two = yield self.hi_shift(add(p(2, 0), one, two)), self.lo_shift(p(1, 1))
        one = yield self.hi_shift(add(p(1, 0), one, two))
        return [p(0, 0), own, one]

    def ring(self, parts, shift):
        acc = parts[-1]
        for b in range(len(parts) - 2, -1, -1):
            acc = yield shift(acc)
            if b:
                acc = add(parts[b], acc)
        return [parts[0], acc]

    def pieces(self, value):
        out, (near, passing) = [value], (yield self.core_shift(value), self.x_shift(value))
        out.append(near)
        for step in range(1, self.xs):
            if step < self.xs - 1:
                near, ahead = yield self.core_shift(passing), self.x_shift(passing)
            else:
                near, ahead = (yield self.core_shift(passing)), None
            out += [passing, near]
            passing = ahead
        return out

    def direct(self, parts):
        got = yield [self.hi_shift(parts[b], b) for b in range(1, self.hi)]
        return [parts[0], *got]

    def over_lo(self, parts):
        acc = yield from self.ring(parts, self.lo_shift)
        return [add(*[v[b] for v in acc]) for b in range(self.hi)]

    def over_lo_hi(self, parts):
        parts = yield from self.over_lo(parts)
        return total(*(yield from self.ring(parts, self.hi_shift)))

    def over_hi(self, chunks):
        parts = [jnp.concatenate(rows, axis=1) for rows in zip(*chunks)]
        return (yield from self.direct(parts))

    def expert_tree(self, near, far, sizes, known):
        got = yield self.core_shift(far)
        out, at = [], 0
        for c, size in enumerate(sizes):
            cut = slice(at, at + size)
            at += size
            if c == len(sizes) - 1:
                near, got = yield near, got
            acc = add(near[self.xs - 1, cut], got[self.xs - 1, cut])
            for b in range(self.xs - 2, -1, -1):
                acc, near, got = yield self.x_shift(acc), near, got
                if b:
                    acc = add(near[b, cut], got[b, cut], acc)
            out.append(acc)
            known.append((near, got, tuple(out)))
        return known[-1]


def gather_kernel(count, cap, base_ref, *refs):
    hidden, grads, (xs, gs, slots) = refs[:count], refs[count : 2 * count], refs[2 * count :]
    step, seq_rows = slots.shape[1:]
    first = base_ref[0] + 1 + pl.program_id(0) * step
    ids = (first + lax.broadcasted_iota(jnp.int32, (step, seq_rows), 0)).astype(F32)
    before = lax.broadcasted_iota(jnp.int32, (seq_rows, seq_rows), 0)
    after = lax.broadcasted_iota(jnp.int32, (seq_rows, seq_rows), 1)
    earlier = (before < after).astype(F32).astype(BF)
    place = lax.broadcasted_iota(jnp.int32, (step, cap, seq_rows), 1).astype(F32)
    for i in range(count):
        digits = hidden[i][seq_rows:, : 2 * seq_rows].astype(F32)
        picks = digits[:, :seq_rows] * 16.0 + digits[:, seq_rows:]
        member = picks[0:1, :] == ids
        for k in range(1, picks.shape[0]):
            member = member | (picks[k : k + 1, :] == ids)
        slot = jnp.where(member, dot(member.astype(F32).astype(BF), earlier), -1.0)
        slots[i] = slot
        pick = (slot[:, None, :] == place).astype(F32).astype(BF).reshape(step * cap, seq_rows)
        for source, out in ((hidden[i], xs), (grads[i], gs)):
            got = dot(pick, source[:seq_rows, :])
            out[:, i * cap : (i + 1) * cap, :] = got.astype(BF).reshape(step, cap, got.shape[1])


def gather_call(base, hidden, grads, experts, cap):
    count = len(hidden)
    seq_rows, width = grads[0].shape
    rows = jax.ShapeDtypeStruct((experts, count * cap, width), BF)
    row_spec = pl.BlockSpec((8, count * cap, width), lambda i, _: (i, 0, 0))
    whole = lambda v: pl.BlockSpec(v.shape, lambda i, _: (0, 0))
    return pl.pallas_call(
        functools.partial(gather_kernel, count, cap),
        grid_spec=pltpu.PrefetchScalarGridSpec(
            num_scalar_prefetch=1,
            grid=(experts // 8,),
            in_specs=[whole(v) for v in (*hidden, *grads)],
            out_specs=[
                row_spec,
                row_spec,
                pl.BlockSpec((count, 8, seq_rows), lambda i, _: (0, i, 0)),
            ],
        ),
        out_shape=[rows, rows, jax.ShapeDtypeStruct((count, experts, seq_rows), F32)],
        compiler_params=pltpu.CompilerParams(vmem_limit_bytes=VMEM_LIMIT),
        cost_estimate=pl.CostEstimate(
            flops=4 * count * experts * cap * seq_rows * width,
            bytes_accessed=4 * experts * count * cap * width,
            transcendentals=0,
        ),
        name="gather_rows",
    )(base, *hidden, *grads)


def expert_kernel(n, groups, cap, many, at_ref, *refs):
    xs_in, gs_in = refs[: n[0]], refs[n[0] : sum(n)]
    up, down, router = refs[sum(n) : sum(n) + 3]
    slots = refs[sum(n) + 3 : sum(n) + 3 + n[0]]
    outs = refs[sum(n) + 3 + n[0] :]
    moe = outs[:groups]
    dhid = outs[groups : 2 * groups]
    near, far, grt = outs[2 * groups : 2 * groups + 3]
    xs, gs, w, d2, gacc, dr = outs[2 * groups + 3 :]
    step = pl.program_id(0)
    ff = up.shape[2]

    @pl.when(step == 0)
    def _():
        for k in range(many):
            w[k, :, ff:] = router[...]
        grt[...] = jnp.zeros_like(grt)

    for k in range(many):
        for whole, pieces in ((xs, xs_in), (gs, gs_in)):
            at = 0
            for piece in pieces:
                whole[k, at : at + piece.shape[1], :] = piece[k]
                at += piece.shape[1]
        w[k, :, :ff] = up[k]
    both = [jnp.dot(xs[k], w[k], preferred_element_type=F32) for k in range(many)]
    us = [jnp.dot(gs[k], down[k], preferred_element_type=F32) for k in range(many)]
    scaled = []
    for k in range(many):
        pre, u = both[k][:, :ff], us[k]
        sel = lax.broadcasted_iota(jnp.int32, pre.shape, 1) == step * many + k
        logit = jnp.sum(jnp.where(sel, both[k][:, ff:], 0.0), axis=1, keepdims=True)
        chosen = jax.nn.sigmoid(logit)
        square = pre * pre
        t = jnp.tanh(GELU_C * (pre + GELU_K * (square * pre)))
        half = 0.5 * (1.0 + t)
        act = (half * pre).astype(BF)
        slope = half + 0.5 * pre * (1.0 - t * t) * (GELU_C * (1.0 + 3.0 * GELU_K * square))
        act32 = act.astype(F32)
        dchosen = jnp.sum(u * act32, axis=1, keepdims=True)
        drl = dchosen * chosen * (1.0 - chosen)
        scaled.append((chosen * act32).astype(BF))
        d2[k, :, :ff] = (chosen * u * slope).astype(BF)
        d2[k, :, ff:] = jnp.where(sel, drl, 0.0).astype(BF)
    for k in range(many):
        dgot = lax.dot_general(
            d2[k], w[k], (((1,), (1,)), ((), ())), preferred_element_type=F32
        ).astype(BF)
        got = lax.dot_general(
            scaled[k], down[k], (((1,), (1,)), ((), ())), preferred_element_type=F32
        ).astype(BF)
        at = pl.multiple_of((step * many + k) * cap, cap)
        for s in range(groups):
            moe[s][k] = got[s * cap : (s + 1) * cap]
            dr[s, pl.ds(at, cap), :] = dgot[s * cap : (s + 1) * cap]
    x_size, _, _, _, lanes = near.shape
    for k in range(many):
        gu = lax.dot_general(d2[k], xs[k], (((0,), (0,)), ((), ())), preferred_element_type=F32)
        gacc[k, 0] = gu[:ff]
        grt[...] += gu[ff : ff + grt.shape[0]]
        gacc[k, 1] = lax.dot_general(
            scaled[k], gs[k], (((0,), (0,)), ((), ())), preferred_element_type=F32
        )
        for xr in range(x_size):
            base = lax.rem(at_ref[1] + xr, x_size) * 2
            for cr, out in enumerate((near, far)):
                cut = pl.multiple_of((base + lax.rem(at_ref[0] + cr, 2)) * lanes, lanes)
                for i in range(2):
                    out[xr, k, i] = gacc[k, i, :, pl.ds(cut, lanes)].astype(BF)

    @pl.when(step == pl.num_programs(0) - 1)
    def _():
        experts = slots[0].shape[1]
        spread = slot_spread(experts, cap)
        source = 0
        for group in slots:
            for i in range(group.shape[0]):
                put = slot_picks(group[i], spread, cap)
                dhid[source][...] = dot(put, dr[source]).astype(BF)
                source += 1


def slot_spread(experts, cap):
    rowi = lax.broadcasted_iota(jnp.int32, (experts, experts * cap), 0)
    coli = lax.broadcasted_iota(jnp.int32, (experts, experts * cap), 1)
    return (coli // cap == rowi).astype(F32).astype(BF)


def slot_picks(slot, spread, cap):
    wide = dot_tn(slot.astype(BF), spread)
    lane = lax.broadcasted_iota(jnp.int32, wide.shape, 1) % cap
    return (wide == lane.astype(F32)).astype(F32).astype(BF)


def expert_call(coords, x_size, groups, xs, gs, up, down, router, slots, cap, many=4):
    experts, width, ff = up.shape
    rows = groups * cap
    pad = -(-experts // 8) * 8
    seq_rows = slots[0].shape[2]
    lanes = width // (2 * x_size)
    row_specs = [
        pl.BlockSpec((many, v.shape[1], width), lambda e, _: (e, 0, 0)) for v in (*xs, *gs)
    ]
    w_spec = pl.BlockSpec((many, width, ff), lambda e, _: (e, 0, 0))
    whole = lambda *shape: pl.BlockSpec(shape, lambda e, _: (0,) * len(shape))
    g_spec = pl.BlockSpec((x_size, many, 2, ff, lanes), lambda e, _: (0, e, 0, 0, 0))
    s_spec = pl.BlockSpec((many, cap, width), lambda e, _: (e, 0, 0))
    one = jax.ShapeDtypeStruct((experts, cap, width), BF)
    outs = pl.pallas_call(
        functools.partial(expert_kernel, (len(xs), len(gs)), groups, cap, many),
        grid_spec=pltpu.PrefetchScalarGridSpec(
            num_scalar_prefetch=1,
            grid=(experts // many,),
            in_specs=[*row_specs, w_spec, w_spec, whole(width, ff)] + [whole(*v.shape) for v in slots],
            out_specs=[s_spec] * groups
            + [whole(seq_rows, width)] * groups
            + [g_spec, g_spec, whole(pad, width)],
            scratch_shapes=[
                pltpu.VMEM((many, rows, width), BF),
                pltpu.VMEM((many, rows, width), BF),
                pltpu.VMEM((many, width, 2 * ff), BF),
                pltpu.VMEM((many, rows, 2 * ff), BF),
                pltpu.VMEM((many, 2, ff, width), F32),
                pltpu.VMEM((groups, experts * cap, width), BF),
            ],
        ),
        out_shape=[one] * groups
        + [jax.ShapeDtypeStruct((seq_rows, width), BF)] * groups
        + [jax.ShapeDtypeStruct((x_size, experts, 2, ff, lanes), BF)] * 2
        + [jax.ShapeDtypeStruct((pad, width), F32)],
        compiler_params=pltpu.CompilerParams(vmem_limit_bytes=VMEM_LIMIT),
        cost_estimate=pl.CostEstimate(
            flops=experts * rows * width * ff * 2 * 8,
            bytes_accessed=experts * rows * width * 8,
            transcendentals=0,
        ),
        name="experts",
    )(coords, *xs, *gs, up, down, router, *slots)
    return outs[:groups], outs[groups : 2 * groups], outs[-3], outs[-2], outs[-1]


def finish_kernel(starts, near, got, *refs):
    accs, (up, down) = refs[: len(starts) - 1], refs[-2:]
    step = pl.program_id(0)
    for acc, first, after in zip(accs, starts, starts[1:]):

        @pl.when((step >= first) & (step < after))
        def _(acc=acc):
            for k in range(acc.shape[0]):
                for i, out in enumerate((up, down)):
                    out[k] = jnp.transpose(
                        near[0, k, i].astype(F32) + got[0, k, i].astype(F32) + acc[k, i].astype(F32)
                    )


def finish_call(near, got, accs, skip=0, known=()):
    _, experts, _, ff, lanes = near.shape
    each = accs[0].shape[0]
    starts = [sum(v.shape[0] for v in accs[:i]) // each for i in range(skip, len(accs) + 1)]
    before = starts[0]
    mine = pl.BlockSpec((1, each, 2, ff, lanes), lambda c: (0, c + before, 0, 0, 0))
    out = pl.BlockSpec((each, lanes, ff), lambda c: (c + before, 0, 0))
    starts = [v - before for v in starts]
    accs = accs[skip:]

    def acc_spec(first, after):
        return pl.BlockSpec(
            (each, 2, ff, lanes), lambda c: (jnp.clip(c - first, 0, after - first - 1), 0, 0, 0)
        )

    return pl.pallas_call(
        functools.partial(finish_kernel, starts),
        grid=(starts[-1],),
        in_specs=[mine, mine]
        + [acc_spec(*pair) for pair in zip(starts, starts[1:])]
        + [pl.BlockSpec(memory_space=pl.ANY)] * len(known),
        out_specs=[out, out],
        out_shape=[jax.ShapeDtypeStruct((experts, lanes, ff), F32)] * 2,
        input_output_aliases={2 + len(accs) + i: i for i in range(len(known))},
        compiler_params=pltpu.CompilerParams(vmem_limit_bytes=VMEM_LIMIT),
        cost_estimate=pl.CostEstimate(
            flops=0, bytes_accessed=20 * experts * lanes * ff, transcendentals=0
        ),
        name="expert_grads",
    )(near, got, *accs, *known)


def scatter_kernel(places, *refs):
    count = len(places)
    rows, slots, outs = refs[:count], refs[count : 2 * count], refs[2 * count :]
    experts, cap, width = rows[0].shape
    spread = slot_spread(experts, cap)
    for s in range(count):
        put = slot_picks(slots[s][places[s]], spread, cap)
        outs[s][...] = dot(put, rows[s][...].reshape(experts * cap, width)).astype(BF)


def scatter_call(rows, slots):
    count = len(rows)
    experts, cap, width = rows[0].shape
    seq_rows = slots[0][0].shape[2]
    return pl.pallas_call(
        functools.partial(scatter_kernel, tuple(j for _, j in slots)),
        out_shape=[jax.ShapeDtypeStruct((seq_rows, width), BF)] * count,
        compiler_params=pltpu.CompilerParams(vmem_limit_bytes=VMEM_LIMIT),
        cost_estimate=pl.CostEstimate(
            flops=2 * count * seq_rows * experts * cap * width,
            bytes_accessed=2 * count * experts * cap * width,
            transcendentals=0,
        ),
        name="scatter_rows",
    )(*rows, *[v for v, _ in slots])


def put_rows(res, outs, sizes, rows, at_ref):
    lo, hi = sizes
    for lr in range(lo):
        l = lax.rem(at_ref[2] + lr, lo)
        for hr in range(hi):
            h = lax.rem(at_ref[3] + hr, hi)
            start = pl.multiple_of((h * lo + l) * rows, rows)
            outs[lr][hr] = res[pl.ds(start, rows), :].astype(BF)


def gate_widener(at):
    shape = (128, AEXP * HEAD)
    row = lax.broadcasted_iota(jnp.int32, shape, 0)
    want = at + lax.broadcasted_iota(jnp.int32, shape, 1) // HEAD
    return ((row == want) | (row == want + 2 * HEADS * AEXP)).astype(F32).astype(BF)


def gated_kernel(count, sizes, rows, gate_at, at_ref, left, *refs):
    bases, gates, outs, (right, res) = refs[:count], refs[count : 2 * count], refs[2 * count : -2], refs[-2:]
    seq_rows = bases[0].shape[0]
    widen = gate_widener(gate_at + pl.program_id(0) * AEXP)
    for p in range(count):
        base, wide = bases[p][...].astype(F32), dot(gates[p][...], widen)
        for e in range(AEXP):
            cut = slice(e * HEAD, (e + 1) * HEAD)
            right[p * seq_rows : (p + 1) * seq_rows, cut] = (wide[:, cut] * base).astype(BF)
    res[...] = dot(left[...], right[...])
    put_rows(res, outs, sizes, rows, at_ref)


def gated_call(coords, grid, left, bases, base_at, packs, gate_at):
    width, tokens = left.shape
    seq_rows = bases[0].shape[0]
    sizes = (grid.lo, grid.hi)
    rows = width // (grid.lo * grid.hi)
    tile = AEXP * HEAD
    count = len(bases)
    out = (grid.hi, rows, HEADS * tile)
    return pl.pallas_call(
        functools.partial(gated_kernel, count, sizes, rows, gate_at),
        grid_spec=pltpu.PrefetchScalarGridSpec(
            num_scalar_prefetch=1,
            grid=(HEADS,),
            in_specs=[whole_spec(width, tokens)]
            + [pl.BlockSpec((seq_rows, HEAD), lambda h, _: (0, base_at // HEAD + h))] * count
            + [pl.BlockSpec((seq_rows, 128), lambda h, _: (0, HEADS))] * count,
            out_specs=[pl.BlockSpec((grid.hi, rows, tile), lambda h, _: (0, 0, h))] * grid.lo,
            scratch_shapes=[pltpu.VMEM((tokens, tile), BF), pltpu.VMEM((width, tile), F32)],
        ),
        out_shape=[jax.ShapeDtypeStruct(out, BF)] * grid.lo,
        compiler_params=pltpu.CompilerParams(vmem_limit_bytes=VMEM_LIMIT),
        cost_estimate=pl.CostEstimate(
            flops=2 * width * tokens * HEADS * tile,
            bytes_accessed=2 * width * HEADS * tile,
            transcendentals=0,
        ),
        name="gated_grad",
    )(coords, left, *bases, *packs)


def plain_kernel(count, sizes, rows, at_ref, left, last_left, extra, *refs):
    factors, outs, (right, res) = refs[:count], refs[count:-2], refs[-2:]
    step, last = pl.program_id(0), pl.num_programs(0) - 1
    seq_rows = factors[0].shape[0]
    for p in range(count):
        right[p * seq_rows : (p + 1) * seq_rows, :] = factors[p][...]

    @pl.when(step < last)
    def _():
        res[...] = dot(left[...], right[...])

    @pl.when(step == last)
    def _():
        width = res.shape[0]
        mine = pl.ds(pl.multiple_of((at_ref[1] * 2 + at_ref[0]) * width, width), width)
        res[...] = dot(last_left[...], right[...]) + jnp.transpose(extra[:, mine])

    put_rows(res, outs, sizes, rows, at_ref)


def plain_call(coords, grid, left, last_left, extra, factors, cols):
    width, tokens = left.shape
    seq_rows = factors[0].shape[0]
    tile = extra.shape[0]
    sizes = (grid.lo, grid.hi)
    rows = width // (grid.lo * grid.hi)
    count = len(factors)
    return pl.pallas_call(
        functools.partial(plain_kernel, count, sizes, rows),
        grid_spec=pltpu.PrefetchScalarGridSpec(
            num_scalar_prefetch=1,
            grid=(cols // tile,),
            in_specs=[
                whole_spec(width, tokens),
                whole_spec(width, tokens),
                whole_spec(*extra.shape),
            ]
            + [head_spec(seq_rows, tile)] * count,
            out_specs=[pl.BlockSpec((grid.hi, rows, tile), lambda j, _: (0, 0, j))] * grid.lo,
            scratch_shapes=[pltpu.VMEM((tokens, tile), BF), pltpu.VMEM((width, tile), F32)],
        ),
        out_shape=[jax.ShapeDtypeStruct((grid.hi, rows, cols), BF)] * grid.lo,
        compiler_params=pltpu.CompilerParams(vmem_limit_bytes=VMEM_LIMIT),
        cost_estimate=pl.CostEstimate(
            flops=2 * width * tokens * cols, bytes_accessed=2 * width * cols, transcendentals=0
        ),
        name="plain_grad",
    )(coords, left, last_left, extra, *factors)


def turn_kernel(count, at_ref, *refs):
    for n in range(len(refs) * count // (count + 1)):
        seq_rows, out = refs[n].shape[0], refs[len(refs) * count // (count + 1) + n // count]
        each = out.shape[0]
        mine = pl.ds(pl.multiple_of((at_ref[1] * 2 + at_ref[0]) * each, each), each)
        at = n % count * seq_rows
        out[:, at : at + seq_rows] = jnp.transpose(refs[n][:, mine])


def turn_call(coords, grid, groups):
    seq_rows, width = groups[0][0].shape
    count = len(groups[0])
    vmem = pl.BlockSpec(memory_space=pltpu.VMEM)
    return pl.pallas_call(
        functools.partial(turn_kernel, count),
        in_specs=[pl.BlockSpec(memory_space=pltpu.SMEM)] + [vmem] * (count * len(groups)),
        out_specs=[vmem] * len(groups),
        out_shape=[jax.ShapeDtypeStruct((width // grid.dp, count * seq_rows), BF)] * len(groups),
        compiler_params=pltpu.CompilerParams(vmem_limit_bytes=VMEM_LIMIT),
        name="turn",
    )(coords, *[v for group in groups for v in group])


NT = (((1,), (1,)), ((), ()))
TN = (((0,), (0,)), ((), ()))


def dot_nt(a, b):
    return lax.dot_general(a, b, NT, preferred_element_type=F32)


def dot_tn(a, b):
    return lax.dot_general(a, b, TN, preferred_element_type=F32)


def dot(a, b):
    return jnp.dot(a, b, preferred_element_type=F32)


def pick_mask(choice):
    picks = choice.shape[0]
    row = lax.broadcasted_iota(jnp.int32, (picks, HEADS * AEXP), 0)
    head = lax.broadcasted_iota(jnp.int32, (picks, HEADS * AEXP), 1) // AEXP
    low = choice.astype(F32).astype(BF)
    first = dot_tn(low, (row == head).astype(F32).astype(BF))
    second = dot_tn(low, (row == HEADS + head).astype(F32).astype(BF))
    expert = (lax.broadcasted_iota(jnp.int32, first.shape, 1) % AEXP).astype(F32)
    return ((first == expert) | (second == expert)).astype(F32)


def normalize(x):
    mean = jnp.mean(x, axis=1, keepdims=True)
    centered = x - mean
    inverse = lax.rsqrt(jnp.mean(centered * centered, axis=1, keepdims=True) + 1e-05)
    return centered * inverse, inverse


def probabilities(q, k, length):
    scores = dot_nt(q, k) * (1.0 / math.sqrt(HEAD))
    row = lax.broadcasted_iota(jnp.int32, scores.shape, 0)
    col = lax.broadcasted_iota(jnp.int32, scores.shape, 1)
    scores = jnp.where((col <= row) & (col < length), scores, -1e30)
    expo = jnp.exp(scores - jnp.max(scores, axis=1, keepdims=True))
    return expo / jnp.sum(expo, axis=1, keepdims=True)


def forward_head(
    h, length, tokens, normed, cos, sin, wq, wk, wv, wo, gates,
    q_out, k_out, mixed_out, vals_out, att_out, expanded,
):
    q = dot(normed[...], wq[...])
    k = dot(normed[...], wk[...])
    q = (q * cos[...] + pltpu.roll(q, HEAD // 2, 1) * sin[...]).astype(BF)
    k = (k * cos[...] + pltpu.roll(k, HEAD // 2, 1) * sin[...]).astype(BF)
    q_out[...] = q
    k_out[...] = k
    vals = dot(tokens[...], wv[...])
    vals_out[...] = vals
    mixed = jnp.zeros_like(q, F32)
    wide = dot(gates[...], gate_widener(h * AEXP))
    for e in range(AEXP):
        cut = slice(e * HEAD, (e + 1) * HEAD)
        mixed += wide[:, cut] * vals[:, cut]
    mixed = mixed.astype(BF)
    mixed_out[...] = mixed
    probs = probabilities(q, k, length).astype(BF)
    att = dot(probs, mixed)
    att_out[...] = att
    wide = dot(gates[...], gate_widener((HEADS + h) * AEXP))
    for e in range(AEXP):
        cut = slice(e * HEAD, (e + 1) * HEAD)
        expanded[:, cut] = (wide[:, cut] * att).astype(BF)
    return dot_nt(expanded[...], wo[...])


def first_heads_kernel(
    length_ref, tokens, cos, sin, wq, wk, wv, wo, gain, vr, orr, vc, oc,
    acc, q_out, k_out, mixed_out, vals_out, att_out, normed, gates, slopes, expanded,
):
    @pl.when(pl.program_id(0) == 0)
    def _():
        scaled, _ = normalize(tokens[...].astype(F32))
        normed[...] = (scaled * gain[...]).astype(BF)
        gates[...] = jnp.zeros_like(gates)
        slopes[...] = jnp.zeros_like(slopes)
        for n, (router, choice) in enumerate(((vr, vc), (orr, oc))):
            sig, mask = jax.nn.sigmoid(dot_nt(tokens[...], router[...])), pick_mask(choice[...])
            high = (sig * mask).astype(BF)
            many = HEADS * AEXP
            gates[:, n * many : (n + 1) * many] = high
            gates[:, (n + 2) * many : (n + 3) * many] = (sig * mask - high.astype(F32)).astype(BF)
            slopes[:, n * many : (n + 1) * many] = mask * sig * (1.0 - sig)
        acc[...] = tokens[...].astype(F32)

    acc[...] += forward_head(
        pl.program_id(0), length_ref[0], tokens, normed, cos, sin, wq, wk, wv, wo,
        gates,
        q_out, k_out, mixed_out, vals_out, att_out, expanded,
    )


def last_heads_kernel(start, *refs):
    length_ref, tokens, cos, sin, wq, wk, wv, wo, normed, gates, codes, acc, known_att = refs[:13]
    hidden, q_out, k_out, mixed_out, vals_out, att_out, hidden_low, pack, expanded = refs[-9:]

    @pl.when(pl.program_id(0) == 0)
    def _():
        hidden[...] = acc[...]

    hidden[...] += forward_head(
        start + pl.program_id(0), length_ref[0], tokens, normed, cos, sin, wq, wk, wv, wo,
        gates,
        q_out, k_out, mixed_out, vals_out, att_out, expanded,
    )

    at = (start + pl.program_id(0)) * HEAD
    pack[:, pl.ds(pl.multiple_of(at, HEAD), HEAD)] = att_out[...].astype(BF)

    @pl.when(pl.program_id(0) == 0)
    def _():
        pack[:, : start * HEAD] = known_att[...].astype(BF)
        pack[:, HEADS * HEAD :] = gates[...]

    @pl.when(pl.program_id(0) == pl.num_programs(0) - 1)
    def _():
        rows = hidden.shape[0]
        hidden_low[:rows, :] = hidden[...].astype(BF)
        code = codes[...]
        high = lax.shift_right_logical(code, 4)
        hidden_low[rows:, :rows] = high.astype(F32).astype(BF)
        hidden_low[rows:, rows : 2 * rows] = (code - high * 16).astype(F32).astype(BF)
        hidden_low[rows:, 2 * rows :] = jnp.zeros((code.shape[0], hidden_low.shape[1] - 2 * rows), BF)


def whole_spec(*shape):
    return pl.BlockSpec(shape, lambda h, _: (0,) * len(shape))


def head_spec(rows, cols):
    return pl.BlockSpec((rows, cols), lambda h, _: (0, h))


def heads_common(rows, width, start):
    many = AEXP * HEAD
    head = lambda rows, cols: pl.BlockSpec((rows, cols), lambda h, _: (0, h + start))
    shape = lambda cols, kind: jax.ShapeDtypeStruct((rows, cols), kind)
    in_specs = [
        whole_spec(rows, width),
        whole_spec(rows, HEAD),
        whole_spec(rows, HEAD),
        head(width, HEAD),
        head(width, HEAD),
        head(width, many),
        head(width, many),
    ]
    out_specs = [whole_spec(rows, width)] + [head(rows, HEAD)] * 3
    out_specs += [head(rows, many), head(rows, HEAD)]
    out_shape = [shape(width, F32)] + [shape(HEADS * HEAD, BF)] * 3
    out_shape += [shape(HEADS * many, F32), shape(HEADS * HEAD, F32)]
    cost = pl.CostEstimate(
        flops=rows * width * HEADS * (2 * HEAD + 2 * many),
        bytes_accessed=width * HEADS * (2 * HEAD + 2 * many),
        transcendentals=0,
    )
    return in_specs, out_specs, out_shape, cost


def first_heads(lengths, tokens, cos, sin, wq, wk, wv, wo, gain, vr, orr, vc, oc):
    rows, width = tokens.shape
    in_specs, out_specs, out_shape, cost = heads_common(rows, width, 0)
    return pl.pallas_call(
        first_heads_kernel,
        grid_spec=pltpu.PrefetchScalarGridSpec(
            num_scalar_prefetch=1,
            grid=(HEADS // 2,),
            in_specs=in_specs + [whole_spec(*v.shape) for v in (gain, vr, orr, vc, oc)],
            out_specs=out_specs + [whole_spec(rows, width)] + [whole_spec(rows, 128)] * 2,
            scratch_shapes=[pltpu.VMEM((rows, AEXP * HEAD), BF)],
        ),
        out_shape=out_shape
        + [jax.ShapeDtypeStruct((rows, width), BF)]
        + [jax.ShapeDtypeStruct((rows, 128), kind) for kind in (BF, F32)],
        compiler_params=pltpu.CompilerParams(vmem_limit_bytes=VMEM_LIMIT),
        cost_estimate=cost,
        name="attention_forward",
    )(lengths, tokens, cos, sin, wq, wk, wv, wo, gain, vr, orr, vc, oc)


def last_heads(lengths, tokens, cos, sin, wq, wk, wv, wo, normed, gates, codes, acc, known):
    rows, width = tokens.shape
    start = HEADS // 2
    in_specs, out_specs, out_shape, cost = heads_common(rows, width, start)
    operands = [lengths, tokens, cos, sin, wq, wk, wv, wo, normed, gates, codes, acc]
    in_specs += [whole_spec(*v.shape) for v in operands[8:]]
    operands.append(known[-1])
    in_specs.append(whole_spec(rows, start * HEAD))
    low = (rows + codes.shape[0], width)
    packed = (rows, HEADS * HEAD + 128)
    return pl.pallas_call(
        functools.partial(last_heads_kernel, start),
        grid_spec=pltpu.PrefetchScalarGridSpec(
            num_scalar_prefetch=1,
            grid=(HEADS - start,),
            in_specs=in_specs + [pl.BlockSpec(memory_space=pl.ANY)] * len(known),
            out_specs=out_specs + [whole_spec(*low), whole_spec(*packed)],
            scratch_shapes=[pltpu.VMEM((rows, AEXP * HEAD), BF)],
        ),
        out_shape=out_shape + [jax.ShapeDtypeStruct(low, BF), jax.ShapeDtypeStruct(packed, BF)],
        input_output_aliases={len(operands) + i: 1 + i for i in range(len(known))},
        compiler_params=pltpu.CompilerParams(vmem_limit_bytes=VMEM_LIMIT),
        cost_estimate=cost,
        name="attention_forward_rest",
    )(*operands, *known)


def backward_kernel(
    length_ref, cos, sin, wo, q_in, k_in, mixed_in, vals, att, gates, slopes, dbranch,
    factors, mixes, dvals, dl,
):
    h = pl.program_id(0)
    logit_at = 2 * HEADS * HEAD

    @pl.when(h == 0)
    def _():
        dl[...] = jnp.zeros_like(dl)
        factors[:, logit_at:] = jnp.zeros((dl.shape[0], factors.shape[1] - logit_at), BF)

    lane = lax.broadcasted_iota(jnp.int32, dl.shape, 1)
    scale = 1.0 / math.sqrt(HEAD)
    dexp = dot(dbranch[...], wo[...])
    datt = jnp.zeros_like(att)
    wide = dot(gates[...], gate_widener((HEADS + h) * AEXP))
    sums = jnp.zeros_like(dl)
    for e in range(AEXP):
        part = dexp[:, e * HEAD : (e + 1) * HEAD]
        datt += wide[:, e * HEAD : (e + 1) * HEAD] * part
        logit = jnp.sum(part * att[...], axis=1, keepdims=True)
        sums = jnp.where(lane == (HEADS + h) * AEXP + e, logit, sums)
    datt = datt.astype(BF)
    q, k, mixed = q_in[...], k_in[...], mixed_in[...]
    probs = probabilities(q, k, length_ref[0])
    dp = dot_nt(datt, mixed)
    inner = jnp.sum(probs * dp, axis=1, keepdims=True)
    dscore = (probs * (dp - inner)).astype(BF)
    dq = dot(dscore, k) * scale
    dk = dot_tn(dscore, q) * scale
    dmixed = dot_tn(probs.astype(BF), datt)
    dq = (dq * cos[...] - pltpu.roll(dq, HEAD // 2, 1) * sin[...]).astype(BF)
    dk = (dk * cos[...] - pltpu.roll(dk, HEAD // 2, 1) * sin[...]).astype(BF)
    put = lambda at, value: factors.__setitem__(
        (slice(None), pl.ds(pl.multiple_of(at, HEAD), HEAD)), value
    )
    put(h * 2 * HEAD, dq)
    put(h * 2 * HEAD + HEAD, dk)
    mixes[...] = dmixed.astype(BF)
    wide = dot(gates[...], gate_widener(h * AEXP))
    for e in range(AEXP):
        part = vals[:, e * HEAD : (e + 1) * HEAD]
        dvals[:, e * HEAD : (e + 1) * HEAD] = (wide[:, e * HEAD : (e + 1) * HEAD] * dmixed).astype(BF)
        logit = jnp.sum(part * dmixed, axis=1, keepdims=True)
        sums = jnp.where(lane == h * AEXP + e, logit, sums)
    dl[...] += sums * slopes[...]

    @pl.when(h == pl.num_programs(0) - 1)
    def _():
        factors[:, logit_at : logit_at + dl.shape[1]] = dl[...].astype(BF)


def backward_call(small, lengths, dbranch, cos, sin, wo, q, k, mixed, vals, att, gates, slopes):
    rows, width = dbranch.shape
    many = AEXP * HEAD
    cols = HEADS * 2 * HEAD + small
    return pl.pallas_call(
        backward_kernel,
        grid_spec=pltpu.PrefetchScalarGridSpec(
            num_scalar_prefetch=1,
            grid=(HEADS,),
            in_specs=[
                whole_spec(rows, HEAD),
                whole_spec(rows, HEAD),
                head_spec(width, many),
                head_spec(rows, HEAD),
                head_spec(rows, HEAD),
                head_spec(rows, HEAD),
                head_spec(rows, many),
                head_spec(rows, HEAD),
            ]
            + [whole_spec(rows, 128)] * 2
            + [whole_spec(rows, width)],
            out_specs=[whole_spec(rows, cols), head_spec(rows, HEAD), head_spec(rows, many)],
            scratch_shapes=[pltpu.VMEM((rows, 128), F32)],
        ),
        out_shape=[
            jax.ShapeDtypeStruct((rows, cols), BF),
            jax.ShapeDtypeStruct((rows, HEADS * HEAD), BF),
            jax.ShapeDtypeStruct((rows, HEADS * many), BF),
        ],
        compiler_params=pltpu.CompilerParams(vmem_limit_bytes=VMEM_LIMIT),
        cost_estimate=pl.CostEstimate(
            flops=2 * rows * width * HEADS * many * 2,
            bytes_accessed=2 * width * HEADS * many,
            transcendentals=0,
        ),
        name="attention_backward",
    )(lengths, cos, sin, wo, q, k, mixed, vals, att, gates, slopes, dbranch)


def input_kernel(tokens, gain, dhidden, factors, dvals, wq, wk, wv, vr, orr, out, dn, rest):
    h = pl.program_id(0)
    logit_at = 2 * HEADS * HEAD

    @pl.when(h == 0)
    def _():
        gates = HEADS * AEXP
        dlogits = factors[:, logit_at : logit_at + 2 * gates]
        dn[...] = jnp.zeros_like(dn)
        rest[...] = (
            dhidden[...]
            + dot(dlogits[:, :gates], vr[...])
            + dot(dlogits[:, gates:], orr[...])
        )

    take = lambda at, size: factors[:, pl.ds(pl.multiple_of(at, HEAD), size)]
    dn[...] += dot_nt(take(h * 2 * HEAD, HEAD), wq[...])
    dn[...] += dot_nt(take(h * 2 * HEAD + HEAD, HEAD), wk[...])
    rest[...] += dot_nt(dvals[...], wv[...])

    @pl.when(h == pl.num_programs(0) - 1)
    def _():
        scaled, inverse = normalize(tokens[...].astype(F32))
        dscaled = dn[...] * gain[...]
        inside = (
            dscaled
            - jnp.mean(dscaled, axis=1, keepdims=True)
            - scaled * jnp.mean(dscaled * scaled, axis=1, keepdims=True)
        )
        out[...] = (rest[...] + inverse * inside).astype(BF)


def input_call(tokens, gain, dhidden, factors, dvals, wq, wk, wv, vr, orr):
    rows, width = tokens.shape
    many = AEXP * HEAD
    whole = lambda *shape: pl.BlockSpec(shape, lambda h: (0,) * len(shape))
    head = lambda *shape: pl.BlockSpec(shape, lambda h: (0, h))
    return pl.pallas_call(
        input_kernel,
        grid=(HEADS,),
        in_specs=[
            whole(rows, width),
            whole(1, width),
            whole(rows, width),
            whole(*factors.shape),
            head(rows, many),
            head(width, HEAD),
            head(width, HEAD),
            head(width, many),
            whole(HEADS * AEXP, width),
            whole(HEADS * AEXP, width),
        ],
        out_specs=whole(rows, width),
        out_shape=jax.ShapeDtypeStruct((rows, width), BF),
        scratch_shapes=[pltpu.VMEM((rows, width), F32)] * 2,
        compiler_params=pltpu.CompilerParams(vmem_limit_bytes=VMEM_LIMIT),
        cost_estimate=pl.CostEstimate(
            flops=2 * rows * width * HEADS * (many + 2 * HEAD),
            bytes_accessed=2 * width * HEADS * (many + 2 * HEAD),
            transcendentals=0,
        ),
        name="input_grad",
    )(tokens, gain, dhidden, factors, dvals, wq, wk, wv, vr, orr)


def last_kernel(count, experts_all, *refs):
    terms, (wq, wk, gain) = refs[:count], refs[count : count + 3]
    query, key, value, vr, orr, er, dgain, counts = refs[count + 3 :]
    summed = total(*[t[...] for t in terms])
    gates, pair = HEADS * AEXP, 2 * HEAD
    at = HEADS * pair
    small = summed.shape[1] - at - value.shape[1]
    value[...] = summed[:, at + small :]
    of_gain = jnp.zeros((query.shape[0], HEAD), F32)
    for h in range(HEADS):
        cut = slice(h * HEAD, (h + 1) * HEAD)
        q = summed[:, h * pair : h * pair + HEAD]
        k = summed[:, h * pair + HEAD : (h + 1) * pair]
        query[:, cut], key[:, cut] = q, k
        of_gain += q * wq[:, cut].astype(F32) + k * wk[:, cut].astype(F32)
    dgain[...] = jnp.sum(jnp.transpose(of_gain), axis=0, keepdims=True) / gain[...]
    tile = summed[:, at : at + small]
    turned = jnp.transpose(tile)
    vr[...] = turned[:gates]
    orr[...] = turned[gates : 2 * gates]
    er[...] = tile[:, 2 * gates : 2 * gates + experts_all]
    bit = lax.broadcasted_iota(jnp.int32, turned.shape, 0) - 2 * gates - experts_all
    worth = jnp.where((bit >= 0) & (bit < 6), jnp.left_shift(1, jnp.clip(bit, 0, 5)), 0)
    counts[...] = jnp.sum(turned * worth.astype(F32), axis=0, keepdims=True)


def last_call(terms, wq, wk, gain, experts_all):
    rows, qk = wq.shape
    gates = HEADS * AEXP
    shapes = [(rows, qk), (rows, qk), (rows, HEADS * AEXP * HEAD), (gates, rows), (gates, rows)]
    shapes += [(rows, experts_all), (1, rows), (1, rows)]
    return pl.pallas_call(
        functools.partial(last_kernel, len(terms), experts_all),
        out_shape=[jax.ShapeDtypeStruct(v, F32) for v in shapes],
        compiler_params=pltpu.CompilerParams(vmem_limit_bytes=VMEM_LIMIT),
        name="last_sums",
    )(*terms, wq, wk, gain)


def shards(
    tokens,
    norm_gain,
    query_weight,
    key_weight,
    value_weight,
    output_weight,
    value_router,
    output_router,
    expert_router,
    expert_up,
    expert_down,
    lengths,
    value_choice,
    output_choice,
    expert_choice,
    running_counts,
    cotangent,
):
    seq_rows, model_width = tokens.shape
    groups = lax.axis_size("expert")
    grid = Grid(lax.axis_size("dp"), groups)
    coords = grid.coords()
    me = lax.axis_index("expert")
    local_experts, _, ff = expert_up.shape
    experts_all = local_experts * groups
    picks_per = expert_choice.shape[1]
    cap = 3 * seq_rows * picks_per // (2 * experts_all)
    position = jnp.arange(seq_rows, dtype=jnp.int32)
    seq_length = lengths[0]

    code = jnp.where((position < seq_length)[:, None], expert_choice + 1, 0)
    all_grads, all_hidden = {}, {}
    grad_ring = Task(grid.gather_rows(cotangent, all_grads, True))

    cosine, sine = rope_tables(seq_rows, HEAD)
    gain = norm_gain.reshape(1, model_width)
    vc, oc = (
        jnp.transpose(v, (2, 1, 0)).reshape(-1, seq_rows) for v in (value_choice, output_choice)
    )
    turned_routers = (jnp.transpose(value_router), jnp.transpose(output_router))
    weights = (query_weight, key_weight, value_weight, output_weight)
    tokens_task = Task(grid.pieces(tokens))
    got = first_heads(
        lengths, tokens, cosine, sine, *weights, gain, *turned_routers, vc, oc
    )
    acc, *known, normed_low, gates, slopes = end_round([grad_ring, tokens_task], got)
    normed_task = Task(grid.pieces(normed_low))
    got = last_heads(
        lengths, tokens, cosine, sine, *weights, normed_low, gates, jnp.transpose(code), acc, known
    )
    got = end_round([grad_ring, tokens_task, normed_task], got)
    hidden, query_rot, key_rot, mixed, values_all, attended, hidden_low, pack = got
    pack_task = Task(grid.pieces(pack))
    hidden_low = end_round([grad_ring, tokens_task, normed_task, pack_task], hidden_low)

    ring = Task(grid.gather_rows(hidden_low, all_hidden))
    end_round([ring, tokens_task, normed_task, pack_task])
    finish([tokens_task, normed_task, pack_task])
    turned = turn_call(coords, grid, [normed_task.result, tokens_task.result])
    packs = pack_task.result
    base = (me * local_experts).reshape(1)
    xs, gs, slots, slot_groups = [], [], {}, []

    def gather(js):
        return gather_call(
            base, [all_hidden[j] for j in js], [all_grads[j] for j in js], local_experts, cap
        )

    def keep(js, got):
        xs.append(got[0])
        gs.append(got[1])
        slot_groups.append(got[2])
        for i, j in enumerate(js):
            slots[j] = (got[2], i)

    if grid.lo == 2:
        got, turned = end_round([ring], (gather(range(3)), turned))
        keep(range(3), got)
        keep((3, 4), end_round([ring, grad_ring], gather((3, 4))))
        keep((5, 6), end_round([ring, grad_ring], gather((5, 6))))
        finish([ring, grad_ring])
        keep((7,), gather((7,)))
    else:
        finish([ring, grad_ring])
        for j in range(0, groups, 4):
            keep(range(j, j + 4), gather(range(j, j + 4)))

    router_mine = lax.dynamic_slice_in_dim(expert_router, me * local_experts, local_experts, 1)
    router_pad = jnp.pad(router_mine, ((0, 0), (0, ff - local_experts)))
    moe_rows, dhid, near, far, grad_router_t = expert_call(
        coords, grid.xs, groups, xs, gs, expert_up, expert_down, router_pad, slot_groups, cap
    )
    moe = {}

    moe = {}

    def scatter(places):
        js = [grid.at(*place) for place in places]
        moe.update(zip(js, scatter_call([moe_rows[j] for j in js], [slots[j] for j in js])))

    def moe_part(j):
        if j not in moe:
            mate = j ^ 1
            got = scatter_call([moe_rows[j], moe_rows[mate]], [slots[j], slots[mate]])
            moe[j], moe[mate] = got
        return moe[j]

    devices = grid.dp * groups
    rows_each = model_width // devices
    labels_all = jnp.arange(experts_all, dtype=jnp.int32)
    local_counts = jnp.sum(
        (code[:, :, None] == labels_all + 1).astype(jnp.int32), axis=(0, 1), dtype=jnp.int32
    )
    bits = (local_counts[None, :] >> jnp.arange(6, dtype=jnp.int32)[:, None]) & 1
    bits = bits.reshape(6, devices, experts_all // devices)
    bits = jnp.pad(bits, ((0, 0), (0, 0), (0, rows_each - experts_all // devices)))
    bits = bits.reshape(6, model_width).astype(BF)
    routers = 2 * HEADS * AEXP
    small = -(-(routers + experts_all + 6) // 256) * 256
    held = -(-(local_experts + 6) // 16) * 16
    compact = jnp.concatenate(
        [
            grad_router_t[:local_experts].astype(BF),
            jnp.pad(bits, ((0, held - local_experts - 6), (0, 0))),
        ],
        axis=0,
    )

    two = grid.lo == 2
    back = Task(grid.sum_rows_hi(lambda j: dhid[j]))
    sixth = local_experts // 6
    summed = []
    cuts = (sixth,) * 3 + (local_experts - 3 * sixth,)
    shares = Task(grid.expert_tree(near, far, cuts, summed))
    if two:
        scatter([(3, 1), (3, 0)])
        moe.update(end_round([back, shares], moe))
        scatter([(2, 1), (2, 0)])
        ready, compact = end_round([back, shares], (moe, compact))
        moe.update(ready)
        scatter([(1, 1), (1, 0)])
    small_task = Task(grid.pieces(compact))
    if two:
        moe.update(end_round([back, shares, small_task], moe))
        scatter([(0, 1), (0, 0)])
    out_ring = Task(grid.sum_rows(moe_part))
    early = 2 if two else 0
    done = finish_call(*summed[early - 1]) if early else ()
    ready, done = end_round([back, shares, small_task, out_ring], (moe, done))
    moe.update(ready)
    finish([back, small_task])
    extra = total(*small_task.result)
    extra = lax.dynamic_update_slice_in_dim(
        jnp.pad(
            extra[local_experts : local_experts + 6],
            ((routers + experts_all, small - routers - experts_all - 6), (0, 0)),
        ),
        extra[:local_experts],
        routers + me * local_experts,
        0,
    )

    dhidden = total(cotangent, *back.result)
    dbranch = dhidden.astype(BF)
    branch_task = Task(grid.pieces(dbranch))
    factors, mixes, dvalues = backward_call(
        small, lengths, dbranch, cosine, sine, output_weight, query_rot, key_rot, mixed, values_all,
        attended, gates, slopes,
    )
    factors, mixes, dvalues, extra = end_round(
        [out_ring, branch_task], (factors, mixes, dvalues, extra)
    )
    mix_task = Task(grid.pieces(mixes))
    finish([branch_task])
    factors = end_round([mix_task], factors)
    factor_task = Task(grid.pieces(factors))
    [branch_turned] = turn_call(coords, grid, [branch_task.result])
    output_parts = gated_call(coords, grid, branch_turned, packs, 0, packs, HEADS * AEXP)

    output_sum = Task(grid.over_lo_hi(output_parts))
    finish([mix_task])
    value_parts = gated_call(coords, grid, turned[1], mix_task.result, 0, packs, 0)
    value_parts = end_round([out_ring], value_parts)
    value_sum = Task(grid.over_lo(value_parts))
    end_round([factor_task, shares])
    finish([factor_task])
    qk_part = plain_call(coords, grid, *turned, extra, factor_task.result, factors.shape[1])
    qk_part, factors = end_round([out_ring, output_sum], (qk_part, factors))
    finish([out_ring])
    qk_sum = Task(grid.over_lo(qk_part))
    grad_tokens = input_call(
        tokens, gain, dhidden, factors, dvalues, query_weight, key_weight, value_weight,
        *turned_routers,
    )
    grad_tokens = end_round([output_sum], grad_tokens)
    output = (hidden + total(*out_ring.result)).astype(BF)
    output = end_round([value_sum, qk_sum, output_sum], output)
    finish([value_sum, qk_sum])
    last = Task(grid.over_hi([qk_sum.result, value_sum.result]))
    finish([shares])
    expert_grads = finish_call(*shares.result, early, done)
    finish([output_sum])
    expert_grads, sum_output = end_round([last], (expert_grads, output_sum.result))
    finish([last])
    first = (lax.axis_index("dp") * groups + me) * rows_each
    rows_of = lambda w: lax.dynamic_slice_in_dim(w, first, rows_each, 0)
    grad_query, grad_key, grad_value, grad_vr, grad_or, grad_er, grad_gain, got_counts = last_call(
        last.result, rows_of(query_weight), rows_of(key_weight), rows_of(norm_gain)[None],
        experts_all,
    )
    counts = running_counts + got_counts[0, : experts_all // devices].astype(jnp.int32)
    return (
        output,
        grad_tokens,
        grad_gain[0],
        grad_query,
        grad_key,
        grad_value,
        sum_output,
        jnp.transpose(grad_vr),
        jnp.transpose(grad_or),
        grad_er,
        *expert_grads,
        counts,
    )


def solution(mesh):
    both = ("dp", "expert")
    in_specs = (
        P(both, None),
        P(),
        P(),
        P(),
        P(),
        P(),
        P(),
        P(),
        P(),
        P("expert", None, None),
        P("expert", None, None),
        P(both),
        P(both, None, None),
        P(both, None, None),
        P(both, None),
        P(both),
        P(both, None),
    )
    out_specs = (
        P(both, None),
        P(both, None),
        P(both),
        P(both, None),
        P(both, None),
        P(both, None),
        P(both, None),
        P(both, None),
        P(both, None),
        P(both, None),
        P("expert", "dp", None),
        P("expert", "dp", None),
        P(both),
    )
    return jax.shard_map(shards, mesh=mesh, in_specs=in_specs, out_specs=out_specs, check_vma=False)
```
